32 devices in a mesh: dp: 4 (over x, core), ctx: 8 (over z, y).
Axes of the slice: x: 2, y: 2, z: 4, core: 2. Of those that a mesh axis runs over, the one named last changes fastest.
Arguments:
- features: bfloat16 [4, 1024, 6144], P('dp', 'ctx'), may hold values from -6 to 6
- upstream: bfloat16 [4, 1024, 2048], P('dp', 'ctx'), may hold values from -6 to 6
- lengths: int32 [4, 8], P('dp'), may hold values from 1 to 512, 1024 in all within a row
- conv_taps: float32 [3, 6144], replicated, may hold values from -3 to 3
- residues: float32 [16, 2048], P(None, 'ctx'), may hold values from -0.12 to 0.12
- log_rate: float32 [16, 2048], P(None, 'ctx'), may hold values from -13.2 to -3.5
- skip_gain: float32 [2048], P('ctx'), may hold values from -4 to 4
Outputs:
- grad_features: bfloat16 [4, 1024, 6144], P('dp', 'ctx')
- grad_taps: float32 [3, 6144], replicated
- grad_residues: float32 [16, 2048], P(None, 'ctx')
- grad_skip: float32 [2048], P('ctx')
The draws below stay inside these ranges and needn't reach their ends.
All inputs are finite; a program needn't handle non-finite values.
Results may differ from the reference program's by a relative error of at most 0.0095.
Values may be sent and summed in bfloat16 or wider, within the bound.
No kernel may reach another device: no remote copies, remote signals or barrier semaphores. Data moves between devices by JAX's collectives and lax.ppermute only.
A program may use at most 192 MiB of HBM per device.

```python
import math
import jax
import jax.numpy as jnp
import numpy as np
from jax import lax

CHANNELS = 2048
POLES = 16
BLOCK_ROWS = 128
SEGMENTS = 8
WINDOW_LEN = 1024
WINDOWS = 4


def draw_log_rate(key, part):
    lowest = math.log(2e-06)
    highest = math.log(0.03)
    return jax.random.uniform(key, (POLES, CHANNELS), jnp.float32, lowest, highest)


def levels(rng, extent, pieces, low, largest):
    def one(axis_at, parts):
        heights = jax.random.uniform(jax.random.fold_in(jax.random.fold_in(rng, 6), axis_at), (parts,), jnp.float32, low / len(pieces), largest / len(pieces))
        return jnp.repeat(jnp.exp(heights), extent[axis_at] // parts).reshape((-1,) + (1,) * (len(extent) - axis_at - 1))

    level = one(*pieces[0])
    for cut in pieces[1:]:
        level = level * one(*cut)
    return level


def length_profile(amount, total, reach, lean):
    loads = [(1 << 20) // math.isqrt(standing ** lean) + 1 for standing in range(2, amount + 1)]
    spare, given = total - reach - (amount - 1), [1] * (amount - 1)
    while spare > 0:
        movable = [i for i in range(amount - 1) if given[i] < reach]
        pool, left = sum([loads[i] for i in movable]), spare
        for i in movable:
            addition = min(reach - given[i], max(1, left * loads[i] // pool), spare)
            given[i] = given[i] + addition
            spare = spare - addition
    return np.array([reach] + given)


def uneven(rng, count, total, bound, slope):
    if count == 2:
        one = jax.random.randint(rng, (), max(1, total - bound), min(bound, total - 1) + 1)
        return jnp.stack([one, total - one])
    sizes = jnp.asarray(length_profile(count, total, bound, slope), jnp.int32)
    couples = (count - 1) // 2
    donor, sink = sizes[1:1 + 2 * couples:2], sizes[2:2 + 2 * couples:2]
    room = jnp.minimum(donor - 1, bound - sink)
    passed = jax.random.randint(jax.random.fold_in(rng, 1), (couples,), 0, 1 << 20) % (room + 1)
    sizes = sizes.at[1:1 + 2 * couples:2].set(donor - passed).at[2:2 + 2 * couples:2].set(sink + passed)
    return sizes[jax.random.permutation(jax.random.fold_in(rng, 2), count)]


def normal_values(own_key, shape, spread, most, pieces=(), held_as=jnp.bfloat16):
    entries = spread * jax.random.normal(own_key, shape, jnp.float32)
    if pieces:
        entries = entries * levels(own_key, shape, pieces, -0.22, 0.18)
    return jnp.clip(entries, -most, most).astype(held_as)


def setup_inputs(seed: int = 0) -> dict:
    key_of = jax.random.split(jax.random.key(seed), 8)
    return {
        "features": normal_values(key_of[0], (WINDOWS, WINDOW_LEN, 3 * CHANNELS), 1.0, 6.0, ((0, 4), (1, 8))),
        "upstream": normal_values(key_of[1], (WINDOWS, WINDOW_LEN, CHANNELS), 1.0, 6.0, ((0, 4), (1, 8))),
        "lengths": jax.vmap(lambda own: uneven(own, SEGMENTS, WINDOW_LEN, WINDOW_LEN // 2, 2))(jax.random.split(key_of[2], WINDOWS)).reshape((WINDOWS, SEGMENTS)).astype(jnp.int32),
        "conv_taps": normal_values(key_of[3], (3, 3 * CHANNELS), 0.6, 3.0, (), jnp.float32),
        "residues": normal_values(key_of[4], (POLES, CHANNELS), 0.02, 0.12, ((1, 8),), jnp.float32),
        "log_rate": draw_log_rate(jax.random.fold_in(key_of[7], 71), 0),
        "skip_gain": normal_values(key_of[6], (CHANNELS,), 1.0, 4.0, ((0, 8),), jnp.float32),
    }


def segment_of(positions, bounds):
    return lax.optimization_barrier(jnp.sum((positions[:, None] >= bounds[None, :]).astype(jnp.int32), axis=1))

def segment_masks(positions, bounds, window_len):
    seg_ids = segment_of(positions, bounds)
    keep_one = ((positions >= 1) & (segment_of(positions - 1, bounds) == seg_ids)).astype(jnp.float32)
    keep_two = ((positions >= 2) & (segment_of(positions - 2, bounds) == seg_ids)).astype(jnp.float32)
    next_one = ((positions + 1 < window_len) & (segment_of(positions + 1, bounds) == seg_ids)).astype(jnp.float32)
    next_two = ((positions + 2 < window_len) & (segment_of(positions + 2, bounds) == seg_ids)).astype(jnp.float32)
    return (seg_ids, keep_one, keep_two, next_one, next_two)

def causal_taps(current, before, tap_rows, keep_one, keep_two):
    extended = jnp.concatenate([before, current], axis=0)
    return tap_rows[0] * current + tap_rows[1] * (keep_one[:, None] * extended[1:-1]) + tap_rows[2] * (keep_two[:, None] * extended[:-2])

def transposed_taps(current, after, tap_rows, next_one, next_two):
    extended = jnp.concatenate([current, after], axis=0)
    return tap_rows[0] * current + tap_rows[1] * (next_one[:, None] * extended[1:-1]) + tap_rows[2] * (next_two[:, None] * extended[2:])

def tap_terms(gradient, current, before, keep_one, keep_two):
    extended = jnp.concatenate([before, current], axis=0)
    first = lax.optimization_barrier(jnp.sum(gradient * current, axis=0))
    second = lax.optimization_barrier(jnp.sum(gradient * (keep_one[:, None] * extended[1:-1]), axis=0))
    third = lax.optimization_barrier(jnp.sum(gradient * (keep_two[:, None] * extended[:-2]), axis=0))
    return jnp.stack([first, second, third])

def modal_sweep(source, segment_ids, decay_rate, coeff, other):
    length, chan_count = source.shape
    pole_count = decay_rate.shape[0]
    blocks = length // BLOCK_ROWS
    per_step = 4
    groups = blocks // per_step
    offsets = jnp.arange(BLOCK_ROWS, dtype=jnp.float32)
    rising = jnp.exp(decay_rate[None] * offsets[:, None, None])
    falling = jnp.exp(-decay_rate[None] * offsets[:, None, None])
    causal = offsets[:, None] >= offsets[None, :]

    def group_fn(inputs):
        src_blk, seg_blk, other_blk = inputs
        joined_mask = ((seg_blk[:, :, None] == seg_blk[:, None, :]) & causal[None]).astype(source.dtype)
        lifted = (src_blk[:, :, None, :] * rising[None]).reshape(per_step, BLOCK_ROWS, pole_count * chan_count)
        inner_state = jnp.einsum('pij,pjk->pik', joined_mask, lifted, precision=lax.Precision.HIGHEST)
        inner_state = inner_state.reshape(per_step, BLOCK_ROWS, pole_count, chan_count) * falling[None]
        block_out = jnp.einsum('pimc,mc->pic', inner_state, coeff, precision=lax.Precision.HIGHEST)
        last_row = inner_state[:, -1]
        start_same = (seg_blk == seg_blk[:, :1]).astype(source.dtype)
        partial_sum = jnp.einsum('pic,pimc->mc', other_blk, inner_state, precision=lax.Precision.HIGHEST)
        weights = jnp.einsum('pic,imc->pmc', other_blk * start_same[:, :, None], falling, precision=lax.Precision.HIGHEST)
        return (block_out, last_row, partial_sum, weights)
    src_groups = source.reshape(groups, per_step, BLOCK_ROWS, chan_count)
    seg_groups = segment_ids.reshape(groups, per_step, BLOCK_ROWS)
    other_groups = other.reshape(groups, per_step, BLOCK_ROWS, chan_count)
    block_out, last_row, partial_sum, weights = lax.map(group_fn, (src_groups, seg_groups, other_groups))
    block_out = block_out.reshape(blocks, BLOCK_ROWS, chan_count)
    last_row = last_row.reshape(blocks, pole_count, chan_count)
    weights = weights.reshape(blocks, pole_count, chan_count)
    seg_rows = segment_ids.reshape(blocks, BLOCK_ROWS)
    starts = seg_rows[:, 0]
    finals = seg_rows[:, -1]
    joined = (starts[1:] == finals[:-1]).astype(source.dtype)
    through = (starts[:-1] == finals[:-1]).astype(source.dtype)
    one_step = jnp.exp(-decay_rate)
    block_decay = jnp.exp(-decay_rate * BLOCK_ROWS)
    factors = (joined * through)[:, None, None] * block_decay[None]
    inputs_in = joined[:, None, None] * one_step[None] * last_row[:-1]

    def combine(earlier, later):
        return (earlier[0] * later[0], later[0] * earlier[1] + later[1])
    unused, states = lax.associative_scan(combine, (factors, inputs_in))
    carried = jnp.concatenate([jnp.zeros((1, pole_count, chan_count), source.dtype), states], axis=0)
    start_rows = (seg_rows == starts[:, None]).astype(source.dtype)
    carry_out = jnp.einsum('kmc,imc->kic', carried * coeff[None], falling, precision=lax.Precision.HIGHEST) * start_rows[:, :, None]
    result = (block_out + carry_out).reshape(length, chan_count)
    grad_part = lax.optimization_barrier(jnp.sum(partial_sum, axis=0)) + jnp.einsum('kmc,kmc->mc', weights, carried, precision=lax.Precision.HIGHEST)
    return (result, grad_part)

def reference(features, upstream, lengths, conv_taps, residues, log_rate, skip_gain):
    decay_rate = jnp.exp(log_rate)
    positions = jnp.arange(WINDOW_LEN, dtype=jnp.int32)
    zeros_rows = jnp.zeros((2, 3 * CHANNELS), jnp.float32)
    grad_list = []
    tap_total = jnp.zeros((3, 3 * CHANNELS), jnp.float32)
    resid_total = jnp.zeros((POLES, CHANNELS), jnp.float32)
    skip_total = jnp.zeros((CHANNELS,), jnp.float32)
    for window in range(WINDOWS):
        bounds = jnp.cumsum(lengths[window])[:-1]
        seg_ids, keep_one, keep_two, next_one, next_two = segment_masks(positions, bounds, WINDOW_LEN)
        source = features[window].astype(jnp.float32)
        featured = causal_taps(source, zeros_rows, conv_taps, keep_one, keep_two)
        query = featured[:, :CHANNELS]
        keys = featured[:, CHANNELS:2 * CHANNELS]
        values = featured[:, 2 * CHANNELS:]
        mixed = (keys * values).astype(jnp.bfloat16)
        mixedf = mixed.astype(jnp.float32)
        conv_out, unused = modal_sweep(mixedf, seg_ids, decay_rate, residues, jnp.zeros_like(mixedf))
        output = (conv_out + skip_gain * mixedf).astype(jnp.bfloat16)
        upf = upstream[window].astype(jnp.float32)
        grad_out = (upf * query).astype(jnp.bfloat16)
        gradf = grad_out.astype(jnp.float32)
        adjoint, grad_resid = modal_sweep(gradf[::-1], seg_ids[::-1], decay_rate, residues, mixedf[::-1])
        grad_mixed = (adjoint[::-1] + skip_gain * gradf).astype(jnp.bfloat16)
        dmixf = grad_mixed.astype(jnp.float32)
        resid_total = resid_total + grad_resid
        skip_total = skip_total + lax.optimization_barrier(jnp.sum(mixedf * gradf, axis=0))
        grad_post = jnp.concatenate([upf * output.astype(jnp.float32), dmixf * values, dmixf * keys], axis=1)
        grad_list.append(transposed_taps(grad_post, zeros_rows, conv_taps, next_one, next_two).astype(jnp.bfloat16))
        tap_total = tap_total + tap_terms(grad_post, source, zeros_rows, keep_one, keep_two)
    grad_scale = 1.0 / math.sqrt(WINDOWS * WINDOW_LEN)
    return (jnp.stack(grad_list), tap_total * grad_scale, resid_total * grad_scale, skip_total * grad_scale)
```

```python
import functools
import math

import jax
import jax.numpy as jnp
from jax import lax
from jax.experimental import pallas as pl
from jax.experimental.pallas import tpu as pltpu
from jax.sharding import PartitionSpec as P

F32 = jnp.float32
BF16 = jnp.bfloat16
LANES = 128
SUB = 8
GROUP = SUB * LANES
HALO = 2


def shifted(block, axis, distance):
    count = lax.axis_size(axis)
    route = [(i - distance, i) for i in range(count) if 0 <= i - distance < count]
    return lax.ppermute(block, axis, route)


def vec(ref, index):
    return ref[pl.ds(pl.multiple_of(index * SUB, SUB), SUB), :]


def put(ref, index, value):
    ref[pl.ds(pl.multiple_of(index * SUB, SUB), SUB), :] = value


def spread(dst, first, src, rows):
    for j in range(SUB):
        value = src[:, j * LANES : (j + 1) * LANES].astype(F32)
        dst[pl.ds(first * SUB + j, rows, stride=SUB), :] = value


def spread_rows(dst, first, src, rows):
    def step(i, carry):
        for j in range(SUB):
            value = src[0, pl.ds(pl.multiple_of(i * 16, 16), 16), j * LANES : (j + 1) * LANES]
            dst[pl.ds((i * 16 + first) * SUB + j, 16, stride=SUB), :] = value.astype(F32)
        return carry

    lax.fori_loop(0, rows // 16, step, 0)


def spread_params(dst, par, rows):
    pieces, _, width = par.shape
    for j in range(SUB):
        if width >= LANES:
            per = width // LANES
            at = (j % per) * LANES
            parts = [(j // per, at, LANES)]
        else:
            per = LANES // width
            parts = [(j * per + i, 0, width) for i in range(per)]
        for first in range(0, rows, SUB):
            many = min(SUB, rows - first)
            got = [par[k, first : first + many, at : at + w] for k, at, w in parts]
            value = got[0] if len(got) == 1 else jnp.concatenate(got, axis=1)
            dst[pl.ds(first * SUB + j, many, stride=SUB), :] = value


def segment_starts(lengths):
    starts = [jnp.int32(0)]
    for j in range(lengths.shape[1]):
        starts.append(starts[-1] + lengths[0, j])
    return starts


def fill_keep(keep, starts, base, rows):
    count = rows + HALO + 2

    def step(i, carry):
        keep[i] = jnp.float32(1.0)
        return carry

    lax.fori_loop(0, count, step, 0, unroll=4)
    for start in starts:
        at = start - base + 1

        @pl.when((at >= 0) & (at < count))
        def _():
            keep[at] = jnp.float32(0.0)


def load_inputs(cur, left, right, taps, feat_scr, tap_scr, up_scr, rows):
    for third in range(3):
        spread_rows(feat_scr[third], HALO, cur[third], rows)
        spread(feat_scr[third], 0, left[third], HALO)
        spread(feat_scr[third], rows + HALO, right[third], HALO)
        spread(tap_scr[third], 0, taps[third], 3)
    spread_rows(up_scr, 0, cur[3], rows)
    spread(up_scr, rows, right[3], HALO)


def featured(feat, taps, p, keep_one, keep_two):
    return (
        taps[0] * vec(feat, p + 2)
        + taps[1] * (keep_one * vec(feat, p + 1))
        + taps[2] * (keep_two * vec(feat, p))
    )


def rounded(value):
    return value.astype(BF16).astype(F32)


def ends_kernel(rows, count, lengths, *refs):
    cur, left, right, taps = refs[0:4], refs[4:7], refs[7:11], refs[11:14]
    par, out = refs[14], refs[15]
    feat_scr, up_scr, tap_scr = refs[16:19], refs[19], refs[20:23]
    par_scr, mixed_scr, gout_scr, stack, keep = refs[23:28]
    me = lax.axis_index("ctx")
    base = me * rows
    poles = (par.shape[1] - 1) // 2
    starts = segment_starts(lengths)
    fill_keep(keep, starts, base, rows)
    load_inputs(cur, left, right, taps, feat_scr, tap_scr, up_scr, rows)
    spread_params(par_scr, par, poles)
    tap = [[vec(tap_scr[third], j) for j in range(3)] for third in range(3)]

    def product(p, carry):
        keep_one = keep[p + 1]
        keep_two = keep_one * keep[p]
        query, key, val = (featured(feat_scr[i], tap[i], p, keep_one, keep_two) for i in range(3))
        put(mixed_scr, p, rounded(key * val))
        put(gout_scr, p, rounded(vec(up_scr, p) * query))
        return carry

    lax.fori_loop(0, rows + HALO, product, 0, unroll=2)
    low, high = jnp.int32(0), jnp.int32(rows + HALO)
    for start in starts:
        at = start - base
        low = jnp.where(at < rows, jnp.maximum(low, at), low)
        high = jnp.where(at > HALO, jnp.minimum(high, at), high)
    decay = [jnp.exp(-jnp.exp(vec(par_scr, m))) for m in range(poles)]

    def sweep(i, carry):
        state, adjoint = carry
        back = rows + HALO - 1 - i
        x = vec(mixed_scr, i) * jnp.where(i >= low, 1.0, 0.0).astype(F32)
        g = vec(gout_scr, back) * jnp.where(back < high, 1.0, 0.0).astype(F32)
        state = [decay[m] * state[m] + x for m in range(poles)]
        adjoint = [decay[m] * adjoint[m] + g for m in range(poles)]
        return state, adjoint

    zeros = [jnp.zeros((SUB, LANES), F32)] * poles
    state, adjoint = lax.fori_loop(0, rows, sweep, (zeros, zeros), unroll=2)
    for m in range(0, poles, 2):
        at = slice(m * SUB, (m + 2) * SUB)
        stack[0, at, :] = jnp.concatenate(state[m : m + 2], axis=0).astype(BF16)
        stack[1, at, :] = jnp.concatenate(adjoint[m : m + 2], axis=0).astype(BF16)
    for e in range(count):
        out[e, 0] = stack[jnp.where(e > me, 0, 1)]


def main_kernel(rows, count, lengths, *refs):
    cur, left, right, taps = refs[0:4], refs[4:7], refs[7:11], refs[11:14]
    par, arrived, grads, sums = refs[14], refs[15], refs[16], refs[17]
    feat_scr, up_scr, tap_scr = refs[18:21], refs[21], refs[22:25]
    par_scr, mixed_scr, gout_scr, conv_scr, adj_scr = refs[25:30]
    post_scr, zero_scr, keep = refs[30:33], refs[33], refs[34]
    me = lax.axis_index("ctx")
    half = pl.program_id(0)
    groups = pl.num_programs(0)
    base = me * rows
    poles = (par.shape[1] - 1) // 2
    extended = rows + HALO
    starts = segment_starts(lengths)
    fill_keep(keep, starts, base, rows)
    load_inputs(cur, left, right, taps, feat_scr, tap_scr, up_scr, rows)
    spread_params(par_scr, par, 2 * poles + 1)
    tap = [[vec(tap_scr[third], j) for j in range(3)] for third in range(3)]

    def product(p, carry):
        keep_one = keep[p + 1]
        keep_two = keep_one * keep[p]
        query, key, val = (featured(feat_scr[i], tap[i], p, keep_one, keep_two) for i in range(3))
        put(mixed_scr, p, rounded(key * val))
        put(gout_scr, p, rounded(vec(up_scr, p) * query))
        put(post_scr[1], p, val)
        put(post_scr[2], p, key)
        return carry

    lax.fori_loop(0, extended, product, 0, unroll=2)

    first, last = jnp.int32(0), jnp.int32(2**30)
    after = base + extended
    for start in starts:
        first = jnp.where(start <= base, jnp.maximum(first, start), first)
        last = jnp.where(start > after, jnp.minimum(last, start), last)
    per_pass = poles // 2
    zero_scr[...] = jnp.zeros((SUB, LANES), F32)
    zero = zero_scr[...]
    for part in range(2):
        chosen = list(range(part * per_pass, (part + 1) * per_pass))
        rate = [jnp.exp(vec(par_scr, m)) for m in chosen]
        block = [jnp.exp(-rows * r) for r in rate]
        zeros = [zero] * per_pass

        def arrived_states(d):
            got = []
            for m in range(chosen[0], chosen[-1] + 1, 2):
                pair = arrived[d, 0, m * SUB : (m + 2) * SUB, :].astype(F32)
                got += [pair[:SUB], pair[SUB:]]
            return got

        def from_before(d, carry):
            joined = jnp.where((d + 1) * rows - 1 >= first, 1.0, 0.0).astype(F32)
            got = arrived_states(d)
            return [block[i] * carry[i] + joined * got[i] for i in range(per_pass)]

        def from_after(i, carry):
            d = count - 1 - i
            joined = jnp.where(d * rows + HALO < last, 1.0, 0.0).astype(F32)
            got = arrived_states(d)
            return [block[i] * carry[i] + joined * got[i] for i in range(per_pass)]

        state = lax.fori_loop(0, me, from_before, zeros)
        adjoint = lax.fori_loop(0, count - 1 - me, from_after, zeros)
        decay = [jnp.exp(-r) for r in rate]
        coeff = [vec(par_scr, poles + m) for m in chosen]

        def sweep(i, carry):
            state, adjoint, resid = carry
            back = extended - 1 - i
            x = vec(mixed_scr, i)
            g = vec(gout_scr, back)
            own = vec(mixed_scr, back) * jnp.where(back < rows, 1.0, 0.0).astype(F32)
            keep_fwd = keep[i + 1]
            keep_bwd = keep[back + 2]
            state = [decay[m] * (state[m] * keep_fwd) + x for m in range(per_pass)]
            adjoint = [decay[m] * (adjoint[m] * keep_bwd) + g for m in range(per_pass)]
            resid = [resid[m] + own * adjoint[m] for m in range(per_pass)]
            conv = sum(coeff[m] * state[m] for m in range(per_pass))
            adj = sum(coeff[m] * adjoint[m] for m in range(per_pass))
            if part == 0:
                put(conv_scr, i, conv)
                put(adj_scr, back, adj)
            else:
                put(conv_scr, i, conv + vec(conv_scr, i))
                put(adj_scr, back, adj + vec(adj_scr, back))
            return state, adjoint, resid

        _, _, resid = lax.fori_loop(0, extended, sweep, (state, adjoint, zeros), unroll=2)
        for i, m in enumerate(chosen):
            at = (9 + m) * groups * SUB + half * SUB
            sums[pl.ds(pl.multiple_of(at, SUB), SUB), :] = resid[i]

    gain = vec(par_scr, 2 * poles)

    def finish(i, carry):
        one, two, tap_sums, skip_sum = carry
        p = extended - 1 - i
        own = jnp.where(p < rows, 1.0, 0.0).astype(F32)
        x = vec(mixed_scr, p)
        g = vec(gout_scr, p)
        conv = rounded(vec(conv_scr, p) + gain * x)
        grad_mixed = rounded(vec(adj_scr, p) + gain * g)
        val, key = vec(post_scr[1], p), vec(post_scr[2], p)
        post = [vec(up_scr, p) * conv, grad_mixed * val, grad_mixed * key]
        keep_one = keep[p + 1]
        keep_two = keep_one * keep[p]
        next_one = keep[p + 2]
        next_two = next_one * keep[jnp.minimum(p + 3, extended + 1)]
        new_sums = []
        for third in range(3):
            back = (
                tap[third][0] * post[third]
                + tap[third][1] * (next_one * one[third])
                + tap[third][2] * (next_two * two[third])
            )
            put(post_scr[third], p, back)
            mine = post[third] * own
            new_sums += [
                tap_sums[3 * third] + mine * vec(feat_scr[third], p + 2),
                tap_sums[3 * third + 1] + mine * (keep_one * vec(feat_scr[third], p + 1)),
                tap_sums[3 * third + 2] + mine * (keep_two * vec(feat_scr[third], p)),
            ]
        return post, one, new_sums, skip_sum + own * (x * g)

    _, _, tap_sums, skip_sum = lax.fori_loop(
        0, extended, finish, ([zero] * 3, [zero] * 3, [zero] * 9, zero), unroll=2
    )
    for third in range(3):
        for j in range(3):
            at = (3 * j + third) * groups * SUB + half * SUB
            sums[pl.ds(pl.multiple_of(at, SUB), SUB), :] = tap_sums[3 * third + j]
    at = (9 + poles) * groups * SUB + half * SUB
    sums[pl.ds(pl.multiple_of(at, SUB), SUB), :] = skip_sum

    def write(i, carry):
        for third in range(3):
            for j in range(SUB):
                value = post_scr[third][pl.ds(i * 16 * SUB + j, 16, stride=SUB), :]
                column = (third * groups + half) * GROUP + j * LANES
                grads[
                    0,
                    pl.ds(pl.multiple_of(i * 16, 16), 16),
                    pl.ds(pl.multiple_of(column, LANES), LANES),
                ] = value.astype(BF16)
        return carry

    lax.fori_loop(0, rows // 16, write, 0)


def per_device(features, upstream, lengths, conv_taps, residues, log_rate, skip_gain):
    rows = features.shape[1]
    channels = upstream.shape[2]
    poles = residues.shape[0]
    ctx_count = lax.axis_size("ctx")
    total = ctx_count * lax.axis_size("dp")
    shard_index = lax.axis_index("ctx")
    per_shard = channels // ctx_count
    groups = channels // GROUP
    grad_scale = 1.0 / math.sqrt(rows * ctx_count * lax.axis_size("dp"))
    extended = rows + HALO

    edge = features[0, rows - HALO :, :]
    head = jnp.concatenate([features[0, :HALO, :], upstream[0, :HALO, :]], axis=1)
    left = shifted(edge, "ctx", 1)
    right = shifted(head, "ctx", -1)
    params = jnp.concatenate([log_rate, residues, skip_gain[None]], axis=0)
    params = lax.all_to_all(
        jnp.broadcast_to(params[None], (ctx_count,) + params.shape),
        "ctx",
        split_axis=0,
        concat_axis=0,
        tiled=True,
    )

    def row_spec(third):
        return pl.BlockSpec((1, rows, GROUP), lambda h: (0, 0, third * groups + h))

    def edge_spec(height, third):
        return pl.BlockSpec((height, GROUP), lambda h: (0, third * groups + h))

    in_specs = (
        [pl.BlockSpec(memory_space=pltpu.SMEM)]
        + [row_spec(0), row_spec(1), row_spec(2), row_spec(0)]
        + [edge_spec(HALO, i) for i in range(3)]
        + [edge_spec(HALO, i) for i in range(4)]
        + [edge_spec(3, i) for i in range(3)]
        + [
            pl.BlockSpec(
                (ctx_count // groups, 2 * poles + 1, per_shard), lambda h: (h, 0, 0)
            )
        ]
    )
    operands = (
        [lengths]
        + [features, features, features, upstream]
        + [left] * 3
        + [right] * 4
        + [conv_taps] * 3
        + [params]
    )

    def tall(height):
        return pltpu.VMEM((height * SUB, LANES), F32)

    common = (
        [tall(rows + 2 * HALO)] * 3
        + [tall(extended)]
        + [tall(3)] * 3
        + [tall(2 * poles + 1)]
        + [tall(extended)] * 2
    )
    keep = pltpu.SMEM((rows + 8,), F32)
    limits = pltpu.CompilerParams(
        dimension_semantics=("arbitrary",), vmem_limit_bytes=40 * 1024 * 1024
    )
    state_rows = poles * SUB
    ends = pl.pallas_call(
        functools.partial(ends_kernel, rows, ctx_count),
        out_shape=jax.ShapeDtypeStruct((ctx_count, groups, state_rows, LANES), BF16),
        grid=(groups,),
        in_specs=in_specs,
        out_specs=pl.BlockSpec((ctx_count, 1, state_rows, LANES), lambda h: (0, h, 0, 0)),
        scratch_shapes=common + [pltpu.VMEM((2, state_rows, LANES), BF16), keep],
        compiler_params=limits,
        name="ends",
    )(*operands)
    arrived = lax.all_to_all(ends, "ctx", split_axis=0, concat_axis=0, tiled=True)

    used = (10 + poles) * groups * SUB
    share = -(-used // (total * SUB)) * SUB
    grads, sums = pl.pallas_call(
        functools.partial(main_kernel, rows, ctx_count),
        out_shape=(
            jax.ShapeDtypeStruct(features.shape, BF16),
            jax.ShapeDtypeStruct((total * share, LANES), F32),
        ),
        grid=(groups,),
        in_specs=in_specs
        + [pl.BlockSpec((ctx_count, 1, state_rows, LANES), lambda h: (0, h, 0, 0))],
        out_specs=(
            pl.BlockSpec(features.shape, lambda h: (0, 0, 0)),
            pl.BlockSpec((total * share, LANES), lambda h: (0, 0)),
        ),
        scratch_shapes=common + [tall(extended)] * 5 + [tall(1), keep],
        compiler_params=limits,
        name="main",
    )(*operands, arrived)

    both = ("dp", "ctx")
    parts = lax.all_to_all(
        sums.reshape(total, share, LANES), both, split_axis=0, concat_axis=0, tiled=True
    )
    mine = jnp.sum(parts, axis=0) * grad_scale
    whole = lax.all_to_all(
        jnp.broadcast_to(mine[None], parts.shape), both, split_axis=0, concat_axis=0, tiled=True
    ).reshape(total * share, LANES)
    width = groups * SUB
    grad_taps = whole[: 9 * width].reshape(3, 3 * channels)
    rest = whole[9 * width : used].reshape(poles + 1, channels)
    rest = lax.dynamic_slice(rest, (0, shard_index * per_shard), (poles + 1, per_shard))
    return grads, grad_taps, rest[:poles], rest[poles]


def solution(mesh):
    return jax.shard_map(
        per_device,
        mesh=mesh,
        in_specs=(
            P("dp", "ctx", None),
            P("dp", "ctx", None),
            P("dp", None),
            P(),
            P(None, "ctx"),
            P(None, "ctx"),
            P("ctx"),
        ),
        out_specs=(P("dp", "ctx", None), P(), P(None, "ctx"), P("ctx")),
        check_vma=False,
    )
```

```python
import functools
import math

import jax
import jax.numpy as jnp
from jax import lax
from jax.experimental import pallas as pl
from jax.experimental.pallas import tpu as pltpu
from jax.sharding import PartitionSpec as P

F32 = jnp.float32
BF16 = jnp.bfloat16
LANES = 128
SUB = 8
GROUP = SUB * LANES
HALO = 2


def shifted(block, axis, distance):
    count = lax.axis_size(axis)
    route = [(i - distance, i) for i in range(count) if 0 <= i - distance < count]
    return lax.ppermute(block, axis, route)


def vec(ref, index):
    return ref[pl.ds(pl.multiple_of(index * SUB, SUB), SUB), :]


def put(ref, index, value):
    ref[pl.ds(pl.multiple_of(index * SUB, SUB), SUB), :] = value


def spread(dst, first, src, row_count, column):
    for j in range(SUB):
        value = src[:, pl.ds(pl.multiple_of(column + j * LANES, LANES), LANES)].astype(F32)
        dst[pl.ds(first * SUB + j, row_count, stride=SUB), :] = value


def spread_rows(dst, first, src, row_count, column):
    def step(i, carry):
        for j in range(SUB):
            lanes = pl.ds(pl.multiple_of(column + j * LANES, LANES), LANES)
            value = src[0, pl.ds(pl.multiple_of(i * 16, 16), 16), lanes]
            dst[pl.ds((i * 16 + first) * SUB + j, 16, stride=SUB), :] = value.astype(F32)
        return carry

    lax.fori_loop(0, row_count // 16, step, 0)


def spread_params(dst, par, half, groups, first_row, rows):
    pieces, _, width = par.shape
    base = half * (pieces // groups)
    for j in range(SUB):
        if width >= LANES:
            per = width // LANES
            at = (j % per) * LANES
            parts = [(j // per, at, LANES)]
        else:
            per = LANES // width
            parts = [(j * per + i, 0, width) for i in range(per)]
        for first in range(0, rows, SUB):
            many = min(SUB, rows - first)
            at_row = first_row + first
            got = [par[base + k, at_row : at_row + many, at : at + w] for k, at, w in parts]
            value = got[0] if len(got) == 1 else jnp.concatenate(got, axis=1)
            dst[pl.ds(first * SUB + j, many, stride=SUB), :] = value


def segment_starts(lengths):
    starts = [jnp.int32(0)]
    for j in range(lengths.shape[1]):
        starts.append(starts[-1] + lengths[0, j])
    return starts


def fill_keep(keep, starts, base, rows):
    count = rows + HALO + 2

    def step(i, carry):
        keep[i] = jnp.float32(1.0)
        return carry

    lax.fori_loop(0, count, step, 0, unroll=4)
    for start in starts:
        at = start - base + 1

        @pl.when((at >= 0) & (at < count))
        def _():
            keep[at] = jnp.float32(0.0)


def rounded(value):
    return value.astype(BF16).astype(F32)


def flag(condition):
    return jnp.where(condition, 1.0, 0.0).astype(F32)


def each_group(groups, body):
    def step(half, carry):
        body(half)
        return carry

    lax.fori_loop(0, groups, step, 0)


def features_kernel(
    rows, groups, lengths, features, upstream, left, right, taps,
    feat, tapv, up, mixed, gout, key_out, val_out, keep,
):
    base = lax.axis_index("ctx") * rows
    extended = rows + HALO
    fill_keep(keep, segment_starts(lengths), base, rows)

    def group(half):
        def feat_at(third):
            return (half * 3 + third) * (rows + 2 * HALO)

        def tap_at(third):
            return (half * 3 + third) * 3

        for third in range(3):
            column = (third * groups + half) * GROUP
            spread_rows(feat, feat_at(third) + HALO, features, rows, column)
            spread(feat, feat_at(third), left, HALO, column)
            spread(feat, feat_at(third) + rows + HALO, right, HALO, column)
            spread(tapv, tap_at(third), taps, 3, column)
        spread_rows(up, half * extended, upstream, rows, half * GROUP)
        spread(up, half * extended + rows, right, HALO, (3 * groups + half) * GROUP)
        tap = [[vec(tapv, tap_at(third) + j) for j in range(3)] for third in range(3)]

        def product(p, carry):
            keep_one = keep[p + 1]
            keep_two = keep_one * keep[p]
            query, key, val = (
                tap[third][0] * vec(feat, feat_at(third) + p + 2)
                + tap[third][1] * (keep_one * vec(feat, feat_at(third) + p + 1))
                + tap[third][2] * (keep_two * vec(feat, feat_at(third) + p))
                for third in range(3)
            )
            at = half * extended + p
            put(mixed, at, rounded(key * val))
            put(gout, at, rounded(vec(up, at) * query))
            put(key_out, at, key)
            put(val_out, at, val)
            return carry

        lax.fori_loop(0, extended, product, 0, unroll=2)

    each_group(groups, group)


def ends_kernel(rows, groups, lengths, params, mixed, gout, payload, own, par, stack, zero_scr):
    me = lax.axis_index("ctx")
    base = me * rows
    count = payload.shape[0]
    poles = (params.shape[1] - 1) // 2
    extended = rows + HALO
    starts = segment_starts(lengths)
    low, high = jnp.int32(0), jnp.int32(extended)
    for start in starts:
        at = start - base
        low = jnp.where(at < rows, jnp.maximum(low, at), low)
        high = jnp.where(at > HALO, jnp.minimum(high, at), high)
    zero_scr[...] = jnp.zeros((SUB, LANES), F32)
    zeros = [zero_scr[...]] * poles

    def group(half):
        spread_params(par, params, half, groups, 0, poles)
        decay = [jnp.exp(-jnp.exp(vec(par, m))) for m in range(poles)]

        def sweep(i, carry):
            state, adjoint = carry
            back = extended - 1 - i
            x = vec(mixed, half * extended + i) * flag(i >= low)
            g = vec(gout, half * extended + back) * flag(back < high)
            state = [decay[m] * state[m] + x for m in range(poles)]
            adjoint = [decay[m] * adjoint[m] + g for m in range(poles)]
            return state, adjoint

        state, adjoint = lax.fori_loop(0, rows, sweep, (zeros, zeros), unroll=2)
        for m in range(poles):
            put(own, half * poles + m, state[m])
        for m in range(0, poles, 2):
            at = slice(m * SUB, (m + 2) * SUB)
            stack[0, at, :] = jnp.concatenate(state[m : m + 2], axis=0).astype(BF16)
            stack[1, at, :] = jnp.concatenate(adjoint[m : m + 2], axis=0).astype(BF16)
        for e in range(count):
            payload[e, half] = stack[jnp.where(e > me, 0, 1)]

    each_group(groups, group)


def local_kernel(
    rows, groups, lengths, params, mixed, gout, conv, adj, partial, par, zero_scr, keep
):
    base = lax.axis_index("ctx") * rows
    poles = (params.shape[1] - 1) // 2
    extended = rows + HALO
    fill_keep(keep, segment_starts(lengths), base, rows)
    zero_scr[...] = jnp.zeros((SUB, LANES), F32)
    zero = zero_scr[...]
    per_pass = poles // 2
    zeros = [zero] * per_pass

    def group(half):
        spread_params(par, params, half, groups, 0, 2 * poles)
        for part in range(2):
            chosen = list(range(part * per_pass, (part + 1) * per_pass))
            decay = [jnp.exp(-jnp.exp(vec(par, m))) for m in chosen]
            coeff = [vec(par, poles + m) for m in chosen]

            def sweep(i, carry):
                state, adjoint, resid, skip = carry
                back = extended - 1 - i
                at, back_at = half * extended + i, half * extended + back
                x = vec(mixed, at)
                g = vec(gout, back_at)
                own = vec(mixed, back_at) * flag(back < rows)
                keep_fwd = keep[i + 1]
                keep_bwd = keep[back + 2]
                state = [decay[m] * (state[m] * keep_fwd) + x for m in range(per_pass)]
                adjoint = [decay[m] * (adjoint[m] * keep_bwd) + g for m in range(per_pass)]
                resid = [resid[m] + own * adjoint[m] for m in range(per_pass)]
                forward = sum(coeff[m] * state[m] for m in range(per_pass))
                backward = sum(coeff[m] * adjoint[m] for m in range(per_pass))
                if part == 0:
                    put(conv, at, forward)
                    put(adj, back_at, backward)
                    skip = skip + own * g
                else:
                    put(conv, at, forward + vec(conv, at))
                    put(adj, back_at, backward + vec(adj, back_at))
                return state, adjoint, resid, skip

            _, _, resid, skip = lax.fori_loop(
                0, extended, sweep, (zeros, zeros, zeros, zero), unroll=2
            )
            for i, m in enumerate(chosen):
                put(partial, m * groups + half, resid[i])
            if part == 0:
                put(partial, poles * groups + half, skip)

    each_group(groups, group)


def carry_kernel(
    rows, groups, lengths, params, arrived, own, partial, before, after, sums, par, zero_scr
):
    me = lax.axis_index("ctx")
    base = me * rows
    count = arrived.shape[0]
    poles = (params.shape[1] - 1) // 2
    extended = rows + HALO
    first, last, newest = jnp.int32(0), jnp.int32(2**30), jnp.int32(0)
    for start in segment_starts(lengths):
        first = jnp.where(start <= base, jnp.maximum(first, start), first)
        last = jnp.where(start > base + extended, jnp.minimum(last, start), last)
        newest = jnp.where(start <= base + extended, jnp.maximum(newest, start), newest)
    through = flag(newest < base + rows)
    zero_scr[...] = jnp.zeros((SUB, LANES), F32)
    per_pass = poles // 2
    zeros = [zero_scr[...]] * per_pass

    def group(half):
        spread_params(par, params, half, groups, 0, poles)
        for part in range(2):
            chosen = list(range(part * per_pass, (part + 1) * per_pass))
            rate = [jnp.exp(vec(par, m)) for m in chosen]
            block = [jnp.exp(-rows * r) for r in rate]

            def arrived_states(d):
                got = []
                for m in range(chosen[0], chosen[-1] + 1, 2):
                    pair = arrived[d, half, m * SUB : (m + 2) * SUB, :].astype(F32)
                    got += [pair[:SUB], pair[SUB:]]
                return got

            def from_before(d, carry):
                joined = flag((d + 1) * rows - 1 >= first)
                got = arrived_states(d)
                return [block[i] * carry[i] + joined * got[i] for i in range(per_pass)]

            def from_after(i, carry):
                d = count - 1 - i
                joined = flag(d * rows + HALO < last)
                got = arrived_states(d)
                return [block[i] * carry[i] + joined * got[i] for i in range(per_pass)]

            state = lax.fori_loop(0, me, from_before, zeros)
            adjoint = lax.fori_loop(0, count - 1 - me, from_after, zeros)
            for i, m in enumerate(chosen):
                put(before, half * poles + m, state[i])
                put(after, half * poles + m, adjoint[i])
                cross = jnp.exp(-(HALO + 1) * rate[i]) * (adjoint[i] * through)
                at = m * groups + half
                put(sums, at, vec(partial, at) + cross * vec(own, half * poles + m))
        at = poles * groups + half
        put(sums, at, vec(partial, at))

    each_group(groups, group)


def finish_kernel(
    rows, groups, lengths, params, feat, tapv, up, mixed, gout, key_in, val_in, conv, adj,
    before, after, grads, sums, par, post, zero_scr, keep,
):
    base = lax.axis_index("ctx") * rows
    poles = (params.shape[1] - 1) // 2
    extended = rows + HALO
    starts = segment_starts(lengths)
    fill_keep(keep, starts, base, rows)
    until, since = jnp.int32(extended), jnp.int32(0)
    for start in starts:
        at = start - base
        until = jnp.where(at >= 0, jnp.minimum(until, at), until)
        since = jnp.where(at <= extended, jnp.maximum(since, at), since)
    steps = jnp.maximum(until, extended - since)
    zero_scr[...] = jnp.zeros((SUB, LANES), F32)
    zero = zero_scr[...]

    def group(half):
        start_at = half * extended
        spread_params(par, params, half, groups, 0, 2 * poles + 1)
        decay = [jnp.exp(-jnp.exp(vec(par, m))) for m in range(poles)]
        enter = [
            vec(par, poles + m) * (decay[m] * vec(before, half * poles + m)) for m in range(poles)
        ]
        leave = [
            vec(par, poles + m) * (decay[m] * vec(after, half * poles + m)) for m in range(poles)
        ]

        def carried(i, carry):
            enter, leave = carry
            for step in range(2):
                p = 2 * i + step
                back = extended - 1 - p
                at, back_at = start_at + p, start_at + back
                put(conv, at, vec(conv, at) + flag(p < until) * sum(enter))
                put(adj, back_at, vec(adj, back_at) + flag(back >= since) * sum(leave))
                enter = [decay[m] * enter[m] for m in range(poles)]
                leave = [decay[m] * leave[m] for m in range(poles)]
            return enter, leave

        lax.fori_loop(0, (steps + 1) // 2, carried, (enter, leave))
        gain = vec(par, 2 * poles)
        tap = [[vec(tapv, (half * 3 + third) * 3 + j) for j in range(3)] for third in range(3)]

        def finish(i, carry):
            one, two, tap_sums = carry
            p = extended - 1 - i
            at = start_at + p
            mine = flag(p < rows)
            conv_out = rounded(vec(conv, at) + gain * vec(mixed, at))
            grad_mixed = rounded(vec(adj, at) + gain * vec(gout, at))
            now = [vec(up, at) * conv_out, grad_mixed * vec(val_in, at), grad_mixed * vec(key_in, at)]
            keep_one = keep[p + 1]
            keep_two = keep_one * keep[p]
            next_one = keep[p + 2]
            next_two = next_one * keep[jnp.minimum(p + 3, extended + 1)]
            new_sums = []
            for third in range(3):
                back = (
                    tap[third][0] * now[third]
                    + tap[third][1] * (next_one * one[third])
                    + tap[third][2] * (next_two * two[third])
                )
                put(post, third * extended + p, back)
                own = now[third] * mine
                f_at = (half * 3 + third) * (rows + 2 * HALO) + p
                new_sums += [
                    tap_sums[3 * third] + own * vec(feat, f_at + 2),
                    tap_sums[3 * third + 1] + own * (keep_one * vec(feat, f_at + 1)),
                    tap_sums[3 * third + 2] + own * (keep_two * vec(feat, f_at)),
                ]
            return now, one, new_sums

        _, _, tap_sums = lax.fori_loop(
            0, extended, finish, ([zero] * 3, [zero] * 3, [zero] * 9), unroll=2
        )
        for third in range(3):
            for j in range(3):
                put(sums, (3 * j + third) * groups + half, tap_sums[3 * third + j])

        def write(i, carry):
            for third in range(3):
                for j in range(SUB):
                    first = (third * extended + i * 16) * SUB + j
                    value = post[pl.ds(first, 16, stride=SUB), :]
                    column = (third * groups + half) * GROUP + j * LANES
                    lanes = pl.ds(pl.multiple_of(column, LANES), LANES)
                    grads[0, pl.ds(pl.multiple_of(i * 16, 16), 16), lanes] = value.astype(BF16)
            return carry

        lax.fori_loop(0, rows // 16, write, 0)

    each_group(groups, group)


def swap(block, axes):
    return lax.all_to_all(block, axes, split_axis=0, concat_axis=0, tiled=True)


def sum_over_all(rows, used):
    total = lax.axis_size("dp") * lax.axis_size("ctx")
    parts = swap(rows.reshape(total, -1, LANES), ("dp", "ctx"))
    mine = jnp.sum(parts, axis=0)
    whole = swap(jnp.broadcast_to(mine[None], parts.shape), ("dp", "ctx"))
    return whole.reshape(-1, LANES)[:used]


def per_device(features, upstream, lengths, conv_taps, residues, log_rate, skip_gain):
    rows = features.shape[1]
    channels = upstream.shape[2]
    poles = residues.shape[0]
    ctx_count = lax.axis_size("ctx")
    total = ctx_count * lax.axis_size("dp")
    shard_index = lax.axis_index("ctx")
    per_shard = channels // ctx_count
    groups = channels // GROUP
    grad_scale = 1.0 / math.sqrt(rows * ctx_count * lax.axis_size("dp"))
    extended = rows + HALO
    vmem = pl.BlockSpec(memory_space=pltpu.VMEM)
    smem = pl.BlockSpec(memory_space=pltpu.SMEM)
    limits = pltpu.CompilerParams(vmem_limit_bytes=32 * 1024 * 1024)

    def tall(height):
        return jax.ShapeDtypeStruct((height * SUB, LANES), F32)

    def scratch(height):
        return pltpu.VMEM((height * SUB, LANES), F32)

    def call(kernel, name, out_shape, scratch_shapes, *operands):
        outs = [vmem] * len(out_shape)
        return pl.pallas_call(
            functools.partial(kernel, rows, groups),
            out_shape=out_shape,
            in_specs=[smem] + [vmem] * len(operands),
            out_specs=outs,
            scratch_shapes=scratch_shapes,
            compiler_params=limits,
            name=name,
        )(lengths, *operands)

    keep = pltpu.SMEM((rows + 8,), F32)
    edge = features[0, rows - HALO :, :]
    head = jnp.concatenate([features[0, :HALO, :], upstream[0, :HALO, :]], axis=1)
    left = shifted(edge, "ctx", 1)
    right = shifted(head, "ctx", -1)
    params = jnp.concatenate([log_rate, residues, skip_gain[None]], axis=0)
    params = swap(jnp.broadcast_to(params[None], (ctx_count,) + params.shape), "ctx")

    whole = tall(groups * extended)
    feat, tapv, up, mixed, gout, key, val = call(
        features_kernel,
        "features",
        [tall(groups * 3 * (rows + 2 * HALO)), tall(groups * 9)] + [whole] * 5,
        [keep],
        features, upstream, left, right, conv_taps,
    )
    states = tall(groups * poles)
    payload, own = call(
        ends_kernel,
        "ends",
        [jax.ShapeDtypeStruct((ctx_count, groups, poles * SUB, LANES), BF16), states],
        [scratch(poles), pltpu.VMEM((2, poles * SUB, LANES), BF16), scratch(1)],
        params, mixed, gout,
    )
    arrived = swap(payload, "ctx")
    conv, adj, partial = call(
        local_kernel,
        "local",
        [whole, whole, tall(groups * (poles + 1))],
        [scratch(2 * poles), scratch(1), keep],
        params, mixed, gout,
    )

    def shares(used):
        return total * -(-used // (total * SUB))

    before, after, resid_rows = call(
        carry_kernel,
        "carry",
        [states, states, tall(shares(groups * (poles + 1) * SUB))],
        [scratch(poles), scratch(1)],
        params, arrived, own, partial,
    )
    resid = sum_over_all(resid_rows, groups * (poles + 1) * SUB)
    grads, tap_rows = call(
        finish_kernel,
        "finish",
        [jax.ShapeDtypeStruct(features.shape, BF16), tall(shares(groups * 9 * SUB))],
        [scratch(2 * poles + 1), scratch(3 * extended), scratch(1), keep],
        params, feat, tapv, up, mixed, gout, key, val, conv, adj, before, after,
    )
    grad_taps = sum_over_all(tap_rows, groups * 9 * SUB).reshape(3, 3 * channels) * grad_scale
    rest = resid.reshape(poles + 1, channels)
    rest = lax.dynamic_slice(rest, (0, shard_index * per_shard), (poles + 1, per_shard))
    rest = rest * grad_scale
    return grads, grad_taps, rest[:poles], rest[poles]


def solution(mesh):
    return jax.shard_map(
        per_device,
        mesh=mesh,
        in_specs=(
            P("dp", "ctx", None),
            P("dp", "ctx", None),
            P("dp", None),
            P(),
            P(None, "ctx"),
            P(None, "ctx"),
            P("ctx"),
        ),
        out_specs=(P("dp", "ctx", None), P(), P(None, "ctx"), P("ctx")),
        check_vma=False,
    )
```

```python
import functools
import math

import jax
import jax.numpy as jnp
from jax import lax
from jax.experimental import pallas as pl
from jax.experimental.pallas import tpu as pltpu
from jax.sharding import PartitionSpec as P

F32 = jnp.float32
BF16 = jnp.bfloat16
LANES = 128
SUB = 8
GROUP = SUB * LANES
HALO = 2


def shifted(block, axis, distance):
    count = lax.axis_size(axis)
    route = [(i - distance, i) for i in range(count) if 0 <= i - distance < count]
    return lax.ppermute(block, axis, route)


def vec(ref, index):
    return ref[pl.ds(pl.multiple_of(index * SUB, SUB), SUB), :]


def put(ref, index, value):
    ref[pl.ds(pl.multiple_of(index * SUB, SUB), SUB), :] = value


def spread(dst, first, src, row_count):
    for j in range(SUB):
        value = src[:, j * LANES : (j + 1) * LANES].astype(F32)
        dst[pl.ds(first * SUB + j, row_count, stride=SUB), :] = value


def spread_rows(dst, first, src, row_count):
    def step(i, carry):
        for j in range(SUB):
            value = src[0, pl.ds(pl.multiple_of(i * 16, 16), 16), j * LANES : (j + 1) * LANES]
            dst[pl.ds((i * 16 + first) * SUB + j, 16, stride=SUB), :] = value.astype(F32)
        return carry

    lax.fori_loop(0, row_count // 16, step, 0)


def spread_params(dst, par, rows):
    pieces, _, width = par.shape
    for j in range(SUB):
        if width >= LANES:
            per = width // LANES
            at = (j % per) * LANES
            parts = [(j // per, at, LANES)]
        else:
            per = LANES // width
            parts = [(j * per + i, 0, width) for i in range(per)]
        for first in range(0, rows, SUB):
            many = min(SUB, rows - first)
            got = [par[k, first : first + many, at : at + w] for k, at, w in parts]
            value = got[0] if len(got) == 1 else jnp.concatenate(got, axis=1)
            dst[pl.ds(first * SUB + j, many, stride=SUB), :] = value


def segment_starts(lengths):
    starts = [jnp.int32(0)]
    for j in range(lengths.shape[1]):
        starts.append(starts[-1] + lengths[0, j])
    return starts


def fill_keep(keep, starts, base, rows):
    count = rows + HALO + 2

    def step(i, carry):
        keep[i] = jnp.float32(1.0)
        return carry

    lax.fori_loop(0, count, step, 0, unroll=4)
    for start in starts:
        at = start - base + 1

        @pl.when((at >= 0) & (at < count))
        def _():
            keep[at] = jnp.float32(0.0)


def rounded(value):
    return value.astype(BF16).astype(F32)


def flag(condition):
    return jnp.where(condition, 1.0, 0.0).astype(F32)


def featured(feat, tap, p, keep_one, keep_two):
    return (
        tap[0] * vec(feat, p + 2)
        + tap[1] * (keep_one * vec(feat, p + 1))
        + tap[2] * (keep_two * vec(feat, p))
    )


def spread_inputs(rows, inputs, feats, up, taps):
    cur, left, right, tap_rows = inputs[0:4], inputs[4:7], inputs[7:11], inputs[11:14]
    for third in range(3):
        feat, first = feats[third]
        spread_rows(feat, first + HALO, cur[third], rows)
        spread(feat, first, left[third], HALO)
        spread(feat, first + rows + HALO, right[third], HALO)
        spread(taps, third * 3, tap_rows[third], 3)
    spread_rows(up, 0, cur[3], rows)
    spread(up, rows, right[3], HALO)


def features_kernel(rows, lengths, *refs):
    inputs, (mixed, gout), (query_in, key_in, val_in, up, taps, keep) = (
        refs[:14], refs[14:16], refs[16:],
    )
    base = lax.axis_index("ctx") * rows
    fill_keep(keep, segment_starts(lengths), base, rows)
    feats = (query_in, key_in, val_in)
    spread_inputs(rows, inputs, [(feat, 0) for feat in feats], up, taps)
    tap = [[vec(taps, third * 3 + j) for j in range(3)] for third in range(3)]

    def product(p, carry):
        keep_one = keep[p + 1]
        keep_two = keep_one * keep[p]
        query, key, val = (featured(feats[i], tap[i], p, keep_one, keep_two) for i in range(3))
        put(mixed, p, rounded(key * val))
        put(gout, p, rounded(vec(up, p) * query))
        return carry

    lax.fori_loop(0, rows + HALO, product, 0, unroll=2)


def ends_kernel(rows, lengths, params, mixed, gout, payload, own, par, stack, zero_scr):
    me = lax.axis_index("ctx")
    base = me * rows
    count = payload.shape[0]
    poles = (params.shape[1] - 1) // 2
    extended = rows + HALO
    low, high = jnp.int32(0), jnp.int32(extended)
    for start in segment_starts(lengths):
        at = start - base
        low = jnp.where(at < rows, jnp.maximum(low, at), low)
        high = jnp.where(at > HALO, jnp.minimum(high, at), high)
    zero_scr[...] = jnp.zeros((SUB, LANES), F32)
    zeros = [zero_scr[...]] * poles
    spread_params(par, params, poles)
    decay = [jnp.exp(-jnp.exp(vec(par, m))) for m in range(poles)]

    def sweep(i, carry):
        state, adjoint = carry
        back = extended - 1 - i
        x = vec(mixed, i) * flag(i >= low)
        g = vec(gout, back) * flag(back < high)
        state = [decay[m] * state[m] + x for m in range(poles)]
        adjoint = [decay[m] * adjoint[m] + g for m in range(poles)]
        return state, adjoint

    state, adjoint = lax.fori_loop(0, rows, sweep, (zeros, zeros), unroll=2)
    for m in range(poles):
        put(own, m, state[m])
    for m in range(0, poles, 2):
        at = slice(m * SUB, (m + 2) * SUB)
        stack[0, at, :] = jnp.concatenate(state[m : m + 2], axis=0).astype(BF16)
        stack[1, at, :] = jnp.concatenate(adjoint[m : m + 2], axis=0).astype(BF16)
    for e in range(count):
        payload[e] = stack[jnp.where(e > me, 0, 1)]


def local_kernel(rows, lengths, *refs):
    inputs, (params, mixed, gout) = refs[:14], refs[14:17]
    feat, taps, up, key_out, val_out, conv, adj, partial = refs[17:25]
    par, zero_scr, keep = refs[25:]
    base = lax.axis_index("ctx") * rows
    poles = (params.shape[1] - 1) // 2
    extended = rows + HALO
    padded = rows + 2 * HALO
    fill_keep(keep, segment_starts(lengths), base, rows)
    spread_inputs(rows, inputs, [(feat, third * padded) for third in range(3)], up, taps)
    tap = [[vec(taps, third * 3 + j) for j in range(3)] for third in range(3)]

    def product(p, carry):
        keep_one = keep[p + 1]
        keep_two = keep_one * keep[p]
        put(key_out, p, featured(feat, tap[1], padded + p, keep_one, keep_two))
        put(val_out, p, featured(feat, tap[2], 2 * padded + p, keep_one, keep_two))
        return carry

    lax.fori_loop(0, extended, product, 0, unroll=2)
    zero_scr[...] = jnp.zeros((SUB, LANES), F32)
    zero = zero_scr[...]
    per_pass = poles // 2
    zeros = [zero] * per_pass
    spread_params(par, params, 2 * poles)
    for part in range(2):
        chosen = list(range(part * per_pass, (part + 1) * per_pass))
        decay = [jnp.exp(-jnp.exp(vec(par, m))) for m in chosen]
        coeff = [vec(par, poles + m) for m in chosen]

        def sweep(i, carry):
            state, adjoint, resid, skip = carry
            back = extended - 1 - i
            x = vec(mixed, i)
            g = vec(gout, back)
            own = vec(mixed, back) * flag(back < rows)
            keep_fwd = keep[i + 1]
            keep_bwd = keep[back + 2]
            state = [decay[m] * (state[m] * keep_fwd) + x for m in range(per_pass)]
            adjoint = [decay[m] * (adjoint[m] * keep_bwd) + g for m in range(per_pass)]
            resid = [resid[m] + own * adjoint[m] for m in range(per_pass)]
            forward = sum(coeff[m] * state[m] for m in range(per_pass))
            backward = sum(coeff[m] * adjoint[m] for m in range(per_pass))
            if part == 0:
                put(conv, i, forward)
                put(adj, back, backward)
                skip = skip + own * g
            else:
                put(conv, i, forward + vec(conv, i))
                put(adj, back, backward + vec(adj, back))
            return state, adjoint, resid, skip

        _, _, resid, skip = lax.fori_loop(
            0, extended, sweep, (zeros, zeros, zeros, zero), unroll=2
        )
        for i, m in enumerate(chosen):
            put(partial, m, resid[i])
        if part == 0:
            put(partial, poles, skip)


def carry_states(rows, lengths, params, arrived, own, partial, sums, before, after, par, zeros):
    me = lax.axis_index("ctx")
    half = pl.program_id(0)
    groups = pl.num_programs(0)
    base = me * rows
    count = arrived.shape[0]
    poles = (params.shape[1] - 1) // 2
    extended = rows + HALO
    first, last, newest = jnp.int32(0), jnp.int32(2**30), jnp.int32(0)
    for start in segment_starts(lengths):
        first = jnp.where(start <= base, jnp.maximum(first, start), first)
        last = jnp.where(start > base + extended, jnp.minimum(last, start), last)
        newest = jnp.where(start <= base + extended, jnp.maximum(newest, start), newest)
    through = flag(newest < base + rows)
    per_pass = poles // 2
    zeros = zeros[:per_pass]
    for part in range(2):
        chosen = list(range(part * per_pass, (part + 1) * per_pass))
        rate = [jnp.exp(vec(par, m)) for m in chosen]
        block = [jnp.exp(-rows * r) for r in rate]

        def arrived_states(d):
            got = []
            for m in range(chosen[0], chosen[-1] + 1, 2):
                pair = arrived[d, m * SUB : (m + 2) * SUB, :].astype(F32)
                got += [pair[:SUB], pair[SUB:]]
            return got

        def from_before(d, carry):
            joined = flag((d + 1) * rows - 1 >= first)
            got = arrived_states(d)
            return [block[i] * carry[i] + joined * got[i] for i in range(per_pass)]

        def from_after(i, carry):
            d = count - 1 - i
            joined = flag(d * rows + HALO < last)
            got = arrived_states(d)
            return [block[i] * carry[i] + joined * got[i] for i in range(per_pass)]

        state = lax.fori_loop(0, me, from_before, zeros)
        adjoint = lax.fori_loop(0, count - 1 - me, from_after, zeros)
        for i, m in enumerate(chosen):
            put(before, m, state[i])
            put(after, m, adjoint[i])
            cross = jnp.exp(-(HALO + 1) * rate[i]) * (adjoint[i] * through)
            put(sums, (9 + m) * groups + half, vec(partial, m) + cross * vec(own, m))
    put(sums, (9 + poles) * groups + half, vec(partial, poles))


def finish_kernel(rows, lengths, *refs):
    params, arrived, own, partial, taps = refs[0:5]
    far, grads, sums_out = refs[5:13], refs[13], refs[14]
    near, (sums, before, after, par, post, zero_scr, keep, sems) = refs[15:23], refs[23:]
    half = pl.program_id(0)
    groups = pl.num_programs(0)
    base = lax.axis_index("ctx") * rows
    poles = (params.shape[1] - 1) // 2
    extended = rows + HALO
    padded = rows + 2 * HALO

    def copies(group):
        return [
            pltpu.make_async_copy(far[i].at[group], near[i].at[group], sems.at[i, group])
            for i in range(len(far))
        ]

    @pl.when(half == 0)
    def _():
        for group in range(far[0].shape[0]):
            for copy in copies(group):
                copy.start()

    starts = segment_starts(lengths)
    fill_keep(keep, starts, base, rows)
    until, since = jnp.int32(extended), jnp.int32(0)
    for start in starts:
        at = start - base
        until = jnp.where(at >= 0, jnp.minimum(until, at), until)
        since = jnp.where(at <= extended, jnp.maximum(since, at), since)
    steps = jnp.maximum(until, extended - since)
    zero_scr[...] = jnp.zeros((SUB, LANES), F32)
    zero = zero_scr[...]
    spread_params(par, params, 2 * poles + 1)
    carry_states(
        rows, lengths, params, arrived, own, partial, sums, before, after, par, [zero] * poles
    )
    decay = [jnp.exp(-jnp.exp(vec(par, m))) for m in range(poles)]
    enter = [vec(par, poles + m) * (decay[m] * vec(before, m)) for m in range(poles)]
    leave = [vec(par, poles + m) * (decay[m] * vec(after, m)) for m in range(poles)]
    for copy in copies(half):
        copy.wait()
    conv, adj, up, mixed, gout, key_in, val_in, feat = [ref.at[half] for ref in near]

    def carried(i, carry):
        enter, leave = carry
        for step in range(2):
            p = 2 * i + step
            back = extended - 1 - p
            put(conv, p, vec(conv, p) + flag(p < until) * sum(enter))
            put(adj, back, vec(adj, back) + flag(back >= since) * sum(leave))
            enter = [decay[m] * enter[m] for m in range(poles)]
            leave = [decay[m] * leave[m] for m in range(poles)]
        return enter, leave

    lax.fori_loop(0, (steps + 1) // 2, carried, (enter, leave))
    gain = vec(par, 2 * poles)
    tap = [[vec(taps, third * 3 + j) for j in range(3)] for third in range(3)]

    def finish(i, carry):
        one, two, tap_sums = carry
        p = extended - 1 - i
        mine = flag(p < rows)
        conv_out = rounded(vec(conv, p) + gain * vec(mixed, p))
        grad_mixed = rounded(vec(adj, p) + gain * vec(gout, p))
        now = [vec(up, p) * conv_out, grad_mixed * vec(val_in, p), grad_mixed * vec(key_in, p)]
        keep_one = keep[p + 1]
        keep_two = keep_one * keep[p]
        next_one = keep[p + 2]
        next_two = next_one * keep[jnp.minimum(p + 3, extended + 1)]
        new_sums = []
        for third in range(3):
            back = (
                tap[third][0] * now[third]
                + tap[third][1] * (next_one * one[third])
                + tap[third][2] * (next_two * two[third])
            )
            put(post, third * extended + p, back)
            mine_now = now[third] * mine
            at = third * padded + p
            new_sums += [
                tap_sums[3 * third] + mine_now * vec(feat, at + 2),
                tap_sums[3 * third + 1] + mine_now * (keep_one * vec(feat, at + 1)),
                tap_sums[3 * third + 2] + mine_now * (keep_two * vec(feat, at)),
            ]
        return now, one, new_sums

    _, _, tap_sums = lax.fori_loop(
        0, extended, finish, ([zero] * 3, [zero] * 3, [zero] * 9), unroll=2
    )
    for third in range(3):
        for j in range(3):
            put(sums, (3 * j + third) * groups + half, tap_sums[3 * third + j])

    def write(i, carry):
        for third in range(3):
            for j in range(SUB):
                first = (third * extended + i * 16) * SUB + j
                value = post[pl.ds(first, 16, stride=SUB), :]
                column = (third * groups + half) * GROUP + j * LANES
                lanes = pl.ds(pl.multiple_of(column, LANES), LANES)
                grads[0, pl.ds(pl.multiple_of(i * 16, 16), 16), lanes] = value.astype(BF16)
        return carry

    lax.fori_loop(0, rows // 16, write, 0)

    @pl.when(half == groups - 1)
    def _():
        sums_out[...] = sums[...].astype(BF16)


def swap(block, axes):
    return lax.all_to_all(block, axes, split_axis=0, concat_axis=0, tiled=True)


def per_device(features, upstream, lengths, conv_taps, residues, log_rate, skip_gain):
    rows = features.shape[1]
    channels = upstream.shape[2]
    poles = residues.shape[0]
    ctx_count = lax.axis_size("ctx")
    total = ctx_count * lax.axis_size("dp")
    shard_index = lax.axis_index("ctx")
    per_shard = channels // ctx_count
    groups = channels // GROUP
    grad_scale = 1.0 / math.sqrt(rows * total)
    extended = rows + HALO
    padded = rows + 2 * HALO
    limits = pltpu.CompilerParams(
        dimension_semantics=("arbitrary",), vmem_limit_bytes=58 * 1024 * 1024
    )

    def tall(height):
        return jax.ShapeDtypeStruct((groups, height * SUB, LANES), F32)

    def tall_spec(height):
        return pl.BlockSpec((None, height * SUB, LANES), lambda h: (h, 0, 0))

    def scratch(height):
        return pltpu.VMEM((height * SUB, LANES), F32)

    def row_spec(third):
        return pl.BlockSpec((1, rows, GROUP), lambda h: (0, 0, third * groups + h))

    def edge_spec(height, third):
        return pl.BlockSpec((height, GROUP), lambda h: (0, third * groups + h))

    smem = pl.BlockSpec(memory_space=pltpu.SMEM)
    anywhere = pl.BlockSpec(memory_space=pl.ANY)
    keep = pltpu.SMEM((rows + 8,), F32)

    def call(kernel, name, operands, in_specs, outs, out_specs, scratch_shapes):
        return pl.pallas_call(
            functools.partial(kernel, rows),
            out_shape=outs,
            grid=(groups,),
            in_specs=[smem] + in_specs,
            out_specs=out_specs,
            scratch_shapes=scratch_shapes,
            compiler_params=limits,
            name=name,
        )(lengths, *operands)

    edge = features[0, rows - HALO :, :]
    head = jnp.concatenate([features[0, :HALO, :], upstream[0, :HALO, :]], axis=1)
    left = shifted(edge, "ctx", 1)
    right = shifted(head, "ctx", -1)
    params = jnp.concatenate([log_rate, residues, skip_gain[None]], axis=0)
    params = swap(jnp.broadcast_to(params[None], (ctx_count,) + params.shape), "ctx")
    params_spec = pl.BlockSpec(
        (ctx_count // groups, 2 * poles + 1, per_shard), lambda h: (h, 0, 0)
    )

    inputs = [features] * 3 + [upstream] + [left] * 3 + [right] * 4 + [conv_taps] * 3
    input_specs = (
        [row_spec(0), row_spec(1), row_spec(2), row_spec(0)]
        + [edge_spec(HALO, i) for i in range(3)]
        + [edge_spec(HALO, i) for i in range(4)]
        + [edge_spec(3, i) for i in range(3)]
    )
    mixed, gout = call(
        features_kernel,
        "features",
        inputs,
        input_specs,
        [tall(extended)] * 2,
        [tall_spec(extended)] * 2,
        [scratch(padded)] * 3 + [scratch(extended), scratch(9), keep],
    )
    state_rows = poles * SUB
    payload_spec = pl.BlockSpec((ctx_count, None, state_rows, LANES), lambda h: (0, h, 0, 0))
    payload, own = call(
        ends_kernel,
        "ends",
        [params, mixed, gout],
        [params_spec] + [tall_spec(extended)] * 2,
        [jax.ShapeDtypeStruct((ctx_count, groups, state_rows, LANES), BF16), tall(poles)],
        [payload_spec, tall_spec(poles)],
        [scratch(poles), pltpu.VMEM((2, state_rows, LANES), BF16), scratch(1)],
    )
    arrived = swap(payload, "ctx")
    heights = [3 * padded, 9] + [extended] * 5 + [poles + 1]
    feat, tap_rows, up, key, val, conv, adj, partial = call(
        local_kernel,
        "local",
        inputs + [params, mixed, gout],
        input_specs + [params_spec] + [tall_spec(extended)] * 2,
        [tall(height) for height in heights],
        [tall_spec(height) for height in heights],
        [scratch(2 * poles), scratch(1), keep],
    )
    far = [conv, adj, up, mixed, gout, key, val, feat]
    used = (10 + poles) * groups * SUB
    share = -(-used // (total * 16)) * 16
    grads, sums = call(
        finish_kernel,
        "finish",
        [params, arrived, own, partial, tap_rows] + far,
        [params_spec, payload_spec, tall_spec(poles), tall_spec(poles + 1), tall_spec(9)]
        + [anywhere] * len(far),
        [
            jax.ShapeDtypeStruct(features.shape, BF16),
            jax.ShapeDtypeStruct((total * share, LANES), BF16),
        ],
        [
            pl.BlockSpec(features.shape, lambda h: (0, 0, 0)),
            pl.BlockSpec((total * share, LANES), lambda h: (0, 0)),
        ],
        [pltpu.VMEM(array.shape, F32) for array in far]
        + [pltpu.VMEM((total * share, LANES), F32)]
        + [scratch(poles)] * 2
        + [scratch(2 * poles + 1), scratch(3 * extended), scratch(1), keep]
        + [pltpu.SemaphoreType.DMA((len(far), groups))],
    )

    both = ("dp", "ctx")
    parts = swap(sums.reshape(total, share, LANES), both).astype(F32)
    mine = (jnp.sum(parts, axis=0) * grad_scale).astype(BF16)
    whole = swap(jnp.broadcast_to(mine[None], parts.shape), both).reshape(total * share, LANES)
    width = groups * SUB
    grad_taps = whole[: 9 * width].reshape(3, 3 * channels).astype(F32)
    rest = whole[9 * width : used].reshape(poles + 1, channels)
    rest = lax.dynamic_slice(rest, (0, shard_index * per_shard), (poles + 1, per_shard))
    rest = rest.astype(F32)
    return grads, grad_taps, rest[:poles], rest[poles]


def solution(mesh):
    return jax.shard_map(
        per_device,
        mesh=mesh,
        in_specs=(
            P("dp", "ctx", None),
            P("dp", "ctx", None),
            P("dp", None),
            P(),
            P(None, "ctx"),
            P(None, "ctx"),
            P("ctx"),
        ),
        out_specs=(P("dp", "ctx", None), P(), P(None, "ctx"), P("ctx")),
        check_vma=False,
    )
```

```python
import functools
import math

import jax
import jax.numpy as jnp
from jax import lax
from jax.experimental import pallas as pl
from jax.experimental.pallas import tpu as pltpu
from jax.sharding import PartitionSpec as P

F32 = jnp.float32
BF16 = jnp.bfloat16
LANES = 128
SUB = 8
GROUP = SUB * LANES
HALO = 2


def shifted(block, axis, distance):
    count = lax.axis_size(axis)
    route = [(i - distance, i) for i in range(count) if 0 <= i - distance < count]
    return lax.ppermute(block, axis, route)


def vec(ref, index):
    return ref[pl.ds(pl.multiple_of(index * SUB, SUB), SUB), :]


def put(ref, index, value):
    ref[pl.ds(pl.multiple_of(index * SUB, SUB), SUB), :] = value


def spread(dst, first, src, column, row_count):
    for j in range(SUB):
        lanes = pl.ds(pl.multiple_of(column + j * LANES, LANES), LANES)
        dst[pl.ds(first * SUB + j, row_count, stride=SUB), :] = src[:, lanes].astype(F32)


def spread_rows(dst, first, src, row_count):
    def step(i, carry):
        for j in range(SUB):
            value = src[pl.ds(pl.multiple_of(i * 16, 16), 16), j * LANES : (j + 1) * LANES]
            dst[pl.ds((i * 16 + first) * SUB + j, 16, stride=SUB), :] = value.astype(F32)
        return carry

    lax.fori_loop(0, row_count // 16, step, 0)


def spread_params(dst, par, half, groups):
    pieces, rows, width = par.shape
    base = half * (pieces // groups)
    for j in range(SUB):
        if width >= LANES:
            per = width // LANES
            at = (j % per) * LANES
            parts = [(j // per, at, LANES)]
        else:
            per = LANES // width
            parts = [(j * per + i, 0, width) for i in range(per)]
        for first in range(0, rows, SUB):
            many = min(SUB, rows - first)
            got = [par[base + k, first : first + many, at : at + w] for k, at, w in parts]
            value = got[0] if len(got) == 1 else jnp.concatenate(got, axis=1)
            dst[pl.ds(first * SUB + j, many, stride=SUB), :] = value


def segment_starts(lengths):
    starts = [jnp.int32(0)]
    for j in range(lengths.shape[1]):
        starts.append(starts[-1] + lengths[0, j])
    return starts


def fill_keep(keep, starts, base, rows):
    count = rows + HALO + 2

    def step(i, carry):
        keep[i] = jnp.float32(1.0)
        return carry

    lax.fori_loop(0, count, step, 0, unroll=4)
    for start in starts:
        at = start - base + 1

        @pl.when((at >= 0) & (at < count))
        def _():
            keep[at] = jnp.float32(0.0)


def rounded(value):
    return value.astype(BF16).astype(F32)


def flag(condition):
    return jnp.where(condition, 1.0, 0.0).astype(F32)


def unroll_of(trips):
    return max(d for d in range(1, 14) if trips % d == 0)


def featured(feat, tap, p, keep_one, keep_two):
    return (
        tap[0] * vec(feat, p + 2)
        + tap[1] * (keep_one * vec(feat, p + 1))
        + tap[2] * (keep_two * vec(feat, p))
    )


def each_group(groups, body):
    def step(half, carry):
        body(half)
        return carry

    lax.fori_loop(0, groups, step, 0)


def group_copies(sources, targets, sems, half):
    return [
        pltpu.make_async_copy(source.at[half], target.at[half], sems.at[half, i])
        for i, (source, target) in enumerate(zip(sources, targets))
    ]


def start_all(copies):
    for copy in copies:
        copy.start()


def wait_all(copies):
    for copy in copies:
        copy.wait()


def ends_kernel(
    rows, groups, far_lengths, features, upstream, left, right, taps, params,
    payload, feat_out, up_out, mixed_out, gout_out, par_out, tap_out,
    lengths, raw, raw_up, feat, up, mixed, gout, par, tap, stack, zero_scr, keep,
    length_sem, in_sems, out_sems,
):
    me = lax.axis_index("ctx")
    base = me * rows
    count = payload.shape[0]
    poles = (params.shape[1] - 1) // 2
    extended = rows + HALO
    padded = rows + 2 * HALO
    get_lengths = pltpu.make_async_copy(far_lengths, lengths, length_sem)
    get_lengths.start()

    def arriving(half):
        lanes = [
            pl.ds(pl.multiple_of((third * groups + half) * GROUP, GROUP), GROUP)
            for third in range(3)
        ]
        return [
            pltpu.make_async_copy(
                features.at[0, :, lanes[third]], raw.at[half, third], in_sems.at[half, third]
            )
            for third in range(3)
        ] + [pltpu.make_async_copy(upstream.at[0, :, lanes[0]], raw_up.at[half], in_sems.at[half, 3])]

    near = [feat, up, tap, par, mixed, gout]
    far = [feat_out, up_out, tap_out, par_out, mixed_out, gout_out]

    each_group(groups, lambda half: start_all(arriving(half)))
    zero_scr[...] = jnp.zeros((SUB, LANES), F32)
    zeros = [zero_scr[...]] * poles

    def prepare(half):
        spread_params(par.at[half], params, half, groups)
        for third in range(3):
            column = (third * groups + half) * GROUP
            spread(feat.at[half], third * padded, left, column, HALO)
            spread(feat.at[half], third * padded + rows + HALO, right, column, HALO)
            spread(tap.at[half], third * 3, taps, column, 3)
        spread(up.at[half], rows, right, (3 * groups + half) * GROUP, HALO)

    each_group(groups, prepare)
    get_lengths.wait()
    starts = segment_starts(lengths)
    fill_keep(keep, starts, base, rows)
    low, high = jnp.int32(0), jnp.int32(extended)
    for start in starts:
        at = start - base
        low = jnp.where(at < rows, jnp.maximum(low, at), low)
        high = jnp.where(at > HALO, jnp.minimum(high, at), high)

    def group(half):
        incoming = arriving(half)
        outgoing = group_copies(near, far, out_sems, half)
        feat_h, up_h, mixed_h, gout_h = feat.at[half], up.at[half], mixed.at[half], gout.at[half]
        for third in range(3):
            incoming[third].wait()
            spread_rows(feat_h, third * padded + HALO, raw.at[half, third], rows)
        incoming[3].wait()
        spread_rows(up_h, 0, raw_up.at[half], rows)
        start_all(outgoing[:4])
        taps_h = [[vec(tap.at[half], third * 3 + j) for j in range(3)] for third in range(3)]

        def product(p, carry):
            keep_one = keep[p + 1]
            keep_two = keep_one * keep[p]
            query, key, val = (
                featured(feat_h, taps_h[third], third * padded + p, keep_one, keep_two)
                for third in range(3)
            )
            put(mixed_h, p, rounded(key * val))
            put(gout_h, p, rounded(vec(up_h, p) * query))
            return carry

        lax.fori_loop(0, extended, product, 0, unroll=unroll_of(extended))
        start_all(outgoing[4:])
        decay = [jnp.exp(-jnp.exp(vec(par.at[half], m))) for m in range(poles)]

        def sweep(i, carry):
            state, adjoint = carry
            back = extended - 1 - i
            x = vec(mixed_h, i) * flag(i >= low)
            g = vec(gout_h, back) * flag(back < high)
            state = [decay[m] * state[m] + x for m in range(poles)]
            adjoint = [decay[m] * adjoint[m] + g for m in range(poles)]
            return state, adjoint

        state, adjoint = lax.fori_loop(0, rows, sweep, (zeros, zeros), unroll=8)
        for m in range(0, poles, 2):
            at = slice(m * SUB, (m + 2) * SUB)
            stack[0, at, :] = jnp.concatenate(state[m : m + 2], axis=0).astype(BF16)
            stack[1, at, :] = jnp.concatenate(adjoint[m : m + 2], axis=0).astype(BF16)
        for e in range(count):
            payload[e, half] = stack[jnp.where(e >= me, 0, 1)]

    each_group(groups, group)
    each_group(groups, lambda half: wait_all(group_copies(near, far, out_sems, half)))


def local_kernel(
    rows, groups, far_lengths, feat_in, mixed_in, gout_in, par_in, tap_in,
    key_out, val_out, conv_out, adj_out, partial_out,
    lengths, mixed, gout, par, tap, feat, key, val, conv, adj, partial, zero_scr, keep,
    length_sem, in_sems, out_sems,
):
    poles = (par.shape[1] // SUB - 1) // 2
    extended = rows + HALO
    padded = rows + 2 * HALO
    get_lengths = pltpu.make_async_copy(far_lengths, lengths, length_sem)
    get_lengths.start()
    far_in, near_in = [par_in, tap_in, feat_in, mixed_in, gout_in], [par, tap, feat, mixed, gout]
    near_out = [key, val, conv, adj, partial]
    far_out = [key_out, val_out, conv_out, adj_out, partial_out]
    each_group(groups, lambda half: start_all(group_copies(far_in, near_in, in_sems, half)))
    zero_scr[...] = jnp.zeros((SUB, LANES), F32)
    zero = zero_scr[...]
    per_pass = poles // 4
    zeros = [zero] * per_pass
    get_lengths.wait()
    fill_keep(keep, segment_starts(lengths), lax.axis_index("ctx") * rows, rows)

    def group(half):
        incoming = group_copies(far_in, near_in, in_sems, half)
        outgoing = group_copies(near_out, far_out, out_sems, half)
        feat_h, mixed_h, gout_h, par_h = feat.at[half], mixed.at[half], gout.at[half], par.at[half]
        conv_h, adj_h, key_h, val_h = conv.at[half], adj.at[half], key.at[half], val.at[half]
        wait_all(incoming)
        taps_h = [[vec(tap.at[half], third * 3 + j) for j in range(3)] for third in range(3)]

        def product(p, carry):
            keep_one = keep[p + 1]
            keep_two = keep_one * keep[p]
            put(key_h, p, featured(feat_h, taps_h[1], padded + p, keep_one, keep_two))
            put(val_h, p, featured(feat_h, taps_h[2], 2 * padded + p, keep_one, keep_two))
            return carry

        lax.fori_loop(0, extended, product, 0, unroll=unroll_of(extended))
        start_all(outgoing[:2])
        gain = vec(par_h, 2 * poles)
        for part in range(poles // per_pass):
            chosen = list(range(part * per_pass, (part + 1) * per_pass))
            decay = [jnp.exp(-jnp.exp(vec(par_h, m))) for m in chosen]
            coeff = [vec(par_h, poles + m) for m in chosen]

            def sweep(i, carry):
                state, adjoint, resid, skip = carry
                back = extended - 1 - i
                x = vec(mixed_h, i)
                g = vec(gout_h, back)
                own = vec(mixed_h, back) * flag(back < rows)
                keep_fwd = keep[i + 1]
                keep_bwd = keep[back + 2]
                state = [decay[m] * (state[m] * keep_fwd) + x for m in range(per_pass)]
                adjoint = [decay[m] * (adjoint[m] * keep_bwd) + g for m in range(per_pass)]
                resid = [resid[m] + own * adjoint[m] for m in range(per_pass)]
                forward = sum(coeff[m] * state[m] for m in range(per_pass))
                backward = sum(coeff[m] * adjoint[m] for m in range(per_pass))
                if part == 0:
                    put(conv_h, i, forward + gain * x)
                    put(adj_h, back, backward + gain * g)
                    skip = skip + own * g
                else:
                    put(conv_h, i, forward + vec(conv_h, i))
                    put(adj_h, back, backward + vec(adj_h, back))
                return state, adjoint, resid, skip

            _, _, resid, skip = lax.fori_loop(
                0, extended, sweep, (zeros, zeros, zeros, zero), unroll=unroll_of(extended)
            )
            for i, m in enumerate(chosen):
                put(partial.at[half], m, resid[i])
            if part == 0:
                put(partial.at[half], poles, skip)
        start_all(outgoing[2:])

    each_group(groups, group)
    each_group(groups, lambda half: wait_all(group_copies(near_out, far_out, out_sems, half)))


def finish_kernel(
    rows, groups, far_lengths, arrived, par_in, partial_in, tap_in, conv_in, adj_in, up_in,
    key_in, val_in, feat_in, grads, sums,
    lengths, par, partial, tap, conv, adj, up, key, val, feat, before, after, post, ready,
    zero_scr, keep, length_sem, in_sems, out_sems,
):
    me = lax.axis_index("ctx")
    base = me * rows
    count = arrived.shape[0]
    poles = (par.shape[1] // SUB - 1) // 2
    extended = rows + HALO
    padded = rows + 2 * HALO
    get_lengths = pltpu.make_async_copy(far_lengths, lengths, length_sem)
    get_lengths.start()
    far = [par_in, partial_in, conv_in, adj_in, tap_in, up_in, key_in, val_in, feat_in]
    near = [par, partial, conv, adj, tap, up, key, val, feat]
    each_group(groups, lambda half: start_all(group_copies(far, near, in_sems, half)))

    def leaving(half):
        return [
            pltpu.make_async_copy(
                ready.at[half, third],
                grads.at[
                    0, :, pl.ds(pl.multiple_of((third * groups + half) * GROUP, GROUP), GROUP)
                ],
                out_sems.at[half, third],
            )
            for third in range(3)
        ]

    zero_scr[...] = jnp.zeros((SUB, LANES), F32)
    zero = zero_scr[...]
    get_lengths.wait()
    starts = segment_starts(lengths)
    fill_keep(keep, starts, base, rows)
    until, since = jnp.int32(extended), jnp.int32(0)
    first, last, newest = jnp.int32(0), jnp.int32(2**30), jnp.int32(0)
    for start in starts:
        at = start - base
        until = jnp.where(at >= 0, jnp.minimum(until, at), until)
        since = jnp.where(at <= extended, jnp.maximum(since, at), since)
        first = jnp.where(at <= 0, jnp.maximum(first, start), first)
        last = jnp.where(at > extended, jnp.minimum(last, start), last)
        newest = jnp.where(at <= extended, jnp.maximum(newest, start), newest)
    steps = jnp.maximum(until, extended - since)
    through = flag(newest < base + rows)
    chunk = unroll_of(extended)

    def group(half):
        incoming = group_copies(far, near, in_sems, half)
        par_h, partial_h, conv_h, adj_h = par.at[half], partial.at[half], conv.at[half], adj.at[half]
        up_h, key_h, val_h, feat_h = up.at[half], key.at[half], val.at[half], feat.at[half]
        wait_all(incoming[:2])
        per_pass = poles // 2
        zeros = [zero] * per_pass
        for part in range(2):
            chosen = list(range(part * per_pass, (part + 1) * per_pass))
            rate = [jnp.exp(vec(par_h, m)) for m in chosen]
            block = [jnp.exp(-rows * r) for r in rate]

            def arrived_states(d):
                got = []
                for m in range(chosen[0], chosen[-1] + 1, 2):
                    pair = arrived[d, half, m * SUB : (m + 2) * SUB, :].astype(F32)
                    got += [pair[:SUB], pair[SUB:]]
                return got

            def from_before(d, carry):
                joined = flag((d + 1) * rows - 1 >= first)
                got = arrived_states(d)
                return [block[i] * carry[i] + joined * got[i] for i in range(per_pass)]

            def from_after(i, carry):
                d = count - 1 - i
                joined = flag(d * rows + HALO < last)
                got = arrived_states(d)
                return [block[i] * carry[i] + joined * got[i] for i in range(per_pass)]

            state = lax.fori_loop(0, me, from_before, zeros)
            adjoint = lax.fori_loop(0, count - 1 - me, from_after, zeros)
            own = arrived_states(me)
            for i, m in enumerate(chosen):
                scale = vec(par_h, poles + m) * jnp.exp(-rate[i])
                put(before, m, scale * state[i])
                put(after, m, scale * adjoint[i])
                cross = jnp.exp(-(HALO + 1) * rate[i]) * (adjoint[i] * through)
                put(sums, (9 + m) * groups + half, vec(partial_h, m) + cross * own[i])
        put(sums, (9 + poles) * groups + half, vec(partial_h, poles))
        decay = [jnp.exp(-jnp.exp(vec(par_h, m))) for m in range(poles)]
        enter = [vec(before, m) for m in range(poles)]
        leave = [vec(after, m) for m in range(poles)]
        wait_all(incoming[2:4])

        def carried(i, carry):
            enter, leave = carry
            for step in range(chunk):
                p = chunk * i + step
                back = extended - 1 - p
                put(conv_h, p, vec(conv_h, p) + flag(p < until) * sum(enter))
                put(adj_h, back, vec(adj_h, back) + flag(back >= since) * sum(leave))
                enter = [decay[m] * enter[m] for m in range(poles)]
                leave = [decay[m] * leave[m] for m in range(poles)]
            return enter, leave

        lax.fori_loop(0, (steps + chunk - 1) // chunk, carried, (enter, leave))
        wait_all(incoming[4:])
        taps_h = [[vec(tap.at[half], third * 3 + j) for j in range(3)] for third in range(3)]

        def posted(p):
            keep_one = keep[p + 1]
            keep_two = keep_one * keep[p]
            conv_out = rounded(vec(conv_h, p))
            grad_mixed = rounded(vec(adj_h, p))
            now = [vec(up_h, p) * conv_out, grad_mixed * vec(val_h, p), grad_mixed * vec(key_h, p)]
            return now, [keep_one * g for g in now], [keep_two * g for g in now]

        _, _, far_two = posted(extended - 1)
        _, near_one, near_two = posted(extended - 2)

        def finish(i, carry):
            one, two, three, tap_sums = carry
            p = rows - 1 - i
            now, masked_one, masked_two = posted(p)
            new_sums = []
            for third in range(3):
                back = (
                    taps_h[third][0] * now[third]
                    + taps_h[third][1] * one[third]
                    + taps_h[third][2] * three[third]
                )
                put(post, third * rows + p, back)
                at = third * padded + p
                new_sums += [
                    tap_sums[3 * third] + now[third] * vec(feat_h, at + 2),
                    tap_sums[3 * third + 1] + masked_one[third] * vec(feat_h, at + 1),
                    tap_sums[3 * third + 2] + masked_two[third] * vec(feat_h, at),
                ]
            return masked_one, masked_two, two, new_sums

        _, _, _, tap_sums = lax.fori_loop(
            0, rows, finish, (near_one, near_two, far_two, [zero] * 9), unroll=4
        )
        for third in range(3):
            for j in range(3):
                put(sums, (3 * j + third) * groups + half, tap_sums[3 * third + j])

        def write(i, carry):
            for third in range(3):
                for j in range(SUB):
                    value = post[pl.ds((third * rows + i * 16) * SUB + j, 16, stride=SUB), :]
                    ready[
                        half, third, pl.ds(pl.multiple_of(i * 16, 16), 16), j * LANES : (j + 1) * LANES
                    ] = value.astype(BF16)
            return carry

        lax.fori_loop(0, rows // 16, write, 0)
        start_all(leaving(half))

    each_group(groups, group)
    each_group(groups, lambda half: wait_all(leaving(half)))


def share_kernel(scale, parts, out):
    count = lax.axis_size("dp") * lax.axis_size("ctx")
    share = parts.shape[0] // count
    mine = parts[0:share, :]
    for k in range(1, count):
        mine = mine + parts[k * share : (k + 1) * share, :]
    mine = mine * scale
    for k in range(count):
        out[k * share : (k + 1) * share, :] = mine


def emit_kernel(groups, whole, grad_taps, resid, skip):
    me = lax.axis_index("ctx")
    width = groups * SUB
    poles, per_shard = resid.shape
    for k in range(3 * width):
        lanes = slice(k * LANES, (k + 1) * LANES)
        grad_taps[:, lanes] = whole[pl.ds(k, 3, stride=3 * width), :]
    if per_shard >= LANES:
        per = per_shard // LANES
        for j in range(per):
            first = 9 * width + me * per + j
            lanes = slice(j * LANES, (j + 1) * LANES)
            resid[:, lanes] = whole[pl.ds(first, poles, stride=width), :]
            skip[:, lanes] = whole[pl.ds(first + poles * width, 1), :]
    else:
        per = LANES // per_shard
        first = 9 * width + me // per
        rows = whole[pl.ds(first, poles, stride=width), :]
        last = whole[pl.ds(first + poles * width, 1), :]
        place = lax.rem(me, per)
        chosen, chosen_last = rows[:, :per_shard], last[:, :per_shard]
        for i in range(1, per):
            lanes = slice(i * per_shard, (i + 1) * per_shard)
            chosen = jnp.where(place == i, rows[:, lanes], chosen)
            chosen_last = jnp.where(place == i, last[:, lanes], chosen_last)
        resid[...] = chosen
        skip[...] = chosen_last


def swap(block, axes):
    return lax.all_to_all(block, axes, split_axis=0, concat_axis=0, tiled=True)


def per_device(features, upstream, lengths, conv_taps, residues, log_rate, skip_gain):
    rows = features.shape[1]
    channels = upstream.shape[2]
    poles = residues.shape[0]
    ctx_count = lax.axis_size("ctx")
    total = ctx_count * lax.axis_size("dp")
    per_shard = channels // ctx_count
    groups = channels // GROUP
    grad_scale = 1.0 / math.sqrt(rows * total)
    extended = rows + HALO
    padded = rows + 2 * HALO
    state_rows = poles * SUB
    limits = pltpu.CompilerParams(vmem_limit_bytes=40 * 1024 * 1024)
    hbm = pl.BlockSpec(memory_space=pltpu.HBM)
    vmem = pl.BlockSpec(memory_space=pltpu.VMEM)

    def tall(height):
        return jax.ShapeDtypeStruct((groups, height * SUB, LANES), F32)

    def near(*heights):
        return [pltpu.VMEM((groups, height * SUB, LANES), F32) for height in heights]

    def scratch(height):
        return pltpu.VMEM((height * SUB, LANES), F32)

    def sems(*shape):
        return pltpu.SemaphoreType.DMA(shape)

    keep = pltpu.SMEM((rows + 8,), F32)
    small = pltpu.SMEM(lengths.shape, jnp.int32)

    def call(kernel, name, ins, in_specs, outs, out_specs, scratch_shapes=()):
        ins = [
            pltpu.with_memory_space_constraint(x, pltpu.HBM) if spec is hbm else x
            for x, spec in zip(ins, in_specs)
        ]
        if isinstance(outs, list):
            outs = [
                pltpu.HBM(out.shape, out.dtype) if spec is hbm else out
                for out, spec in zip(outs, out_specs)
            ]
        return pl.pallas_call(
            kernel,
            out_shape=outs,
            in_specs=in_specs,
            out_specs=out_specs,
            scratch_shapes=list(scratch_shapes),
            compiler_params=limits,
            name=name,
        )(*ins)

    edge = features[0, rows - HALO :, :]
    head = jnp.concatenate([features[0, :HALO, :], upstream[0, :HALO, :]], axis=1)
    left = shifted(edge, "ctx", 1)
    right = shifted(head, "ctx", -1)
    params = jnp.concatenate([log_rate, residues, skip_gain[None]], axis=0)
    params = swap(jnp.broadcast_to(params[None], (ctx_count,) + params.shape), "ctx")

    payload, feat, up, mixed, gout, par, tap = call(
        functools.partial(ends_kernel, rows, groups),
        "ends",
        [lengths, features, upstream, left, right, conv_taps, params],
        [hbm] * 3 + [vmem] * 4,
        [jax.ShapeDtypeStruct((ctx_count, groups, state_rows, LANES), BF16)]
        + [tall(height) for height in [3 * padded] + [extended] * 3 + [2 * poles + 1, 9]],
        [vmem] + [hbm] * 6,
        [
            small,
            pltpu.VMEM((groups, 3, rows, GROUP), BF16),
            pltpu.VMEM((groups, rows, GROUP), BF16),
        ]
        + near(3 * padded, extended, extended, extended, 2 * poles + 1, 9)
        + [pltpu.VMEM((2, state_rows, LANES), BF16), scratch(1), keep]
        + [sems(), sems(groups, 4), sems(groups, 6)],
    )
    arrived = swap(payload, "ctx")
    key, val, conv, adj, partial = call(
        functools.partial(local_kernel, rows, groups),
        "local",
        [lengths, feat, mixed, gout, par, tap],
        [hbm] * 6,
        [tall(extended)] * 4 + [tall(poles + 1)],
        [hbm] * 5,
        [small]
        + near(extended, extended, 2 * poles + 1, 9, 3 * padded)
        + near(extended, extended, extended, extended, poles + 1)
        + [scratch(1), keep, sems(), sems(groups, 5), sems(groups, 5)],
    )
    used = (10 + poles) * groups * SUB
    share = -(-used // total)
    grads, sums = call(
        functools.partial(finish_kernel, rows, groups),
        "finish",
        [lengths, arrived, par, partial, tap, conv, adj, up, key, val, feat],
        [hbm, vmem] + [hbm] * 9,
        [
            jax.ShapeDtypeStruct(features.shape, BF16),
            jax.ShapeDtypeStruct((total * share, LANES), F32),
        ],
        [hbm, vmem],
        [small]
        + near(2 * poles + 1, poles + 1, 9, extended, extended, extended, extended, extended)
        + near(3 * padded)
        + [scratch(poles), scratch(poles), scratch(3 * rows)]
        + [pltpu.VMEM((groups, 3, rows, GROUP), BF16), scratch(1), keep]
        + [sems(), sems(groups, 9), sems(groups, 3)],
    )

    both = ("dp", "ctx")
    flat = (total, 1, share * LANES)
    parts = swap(sums.reshape(flat), both).reshape(sums.shape)
    shares = call(
        functools.partial(share_kernel, grad_scale),
        "share",
        [parts],
        [vmem],
        jax.ShapeDtypeStruct(sums.shape, F32),
        vmem,
    )
    whole = swap(shares.reshape(flat), both).reshape(sums.shape)
    grad_taps, resid, skip = call(
        functools.partial(emit_kernel, groups),
        "emit",
        [whole],
        [vmem],
        [
            jax.ShapeDtypeStruct((3, 3 * channels), F32),
            jax.ShapeDtypeStruct((poles, per_shard), F32),
            jax.ShapeDtypeStruct((1, per_shard), F32),
        ],
        [vmem] * 3,
    )
    return grads, grad_taps, resid, skip.reshape(per_shard)


def solution(mesh):
    return jax.shard_map(
        per_device,
        mesh=mesh,
        in_specs=(
            P("dp", "ctx", None),
            P("dp", "ctx", None),
            P("dp", None),
            P(),
            P(None, "ctx"),
            P(None, "ctx"),
            P("ctx"),
        ),
        out_specs=(P("dp", "ctx", None), P(), P(None, "ctx"), P("ctx")),
        check_vma=False,
    )
```

```python
import functools
import math

import jax
import jax.numpy as jnp
from jax import lax
from jax.experimental import pallas as pl
from jax.experimental.pallas import tpu as pltpu
from jax.sharding import PartitionSpec as P

F32 = jnp.float32
BF16 = jnp.bfloat16
LANES = 128
SUB = 8
GROUP = SUB * LANES
HALO = 2


def shifted(block, axis, distance):
    count = lax.axis_size(axis)
    route = [(i - distance, i) for i in range(count) if 0 <= i - distance < count]
    return lax.ppermute(block, axis, route)


def vec(ref, index):
    return ref[pl.ds(pl.multiple_of(index * SUB, SUB), SUB), :]


def put(ref, index, value):
    ref[pl.ds(pl.multiple_of(index * SUB, SUB), SUB), :] = value


def spread(dst, first, src, column, row_count):
    for j in range(SUB):
        lanes = pl.ds(pl.multiple_of(column + j * LANES, LANES), LANES)
        dst[pl.ds(first * SUB + j, row_count, stride=SUB), :] = src[:, lanes].astype(F32)


def spread_rows(dst, first, src, row_count):
    def step(i, carry):
        for j in range(SUB):
            value = src[pl.ds(pl.multiple_of(i * 16, 16), 16), j * LANES : (j + 1) * LANES]
            dst[pl.ds((i * 16 + first) * SUB + j, 16, stride=SUB), :] = value.astype(F32)
        return carry

    lax.fori_loop(0, row_count // 16, step, 0)


def spread_params(dst, par, half, groups):
    pieces, rows, width = par.shape
    base = half * (pieces // groups)
    for j in range(SUB):
        if width >= LANES:
            per = width // LANES
            at = (j % per) * LANES
            parts = [(j // per, at, LANES)]
        else:
            per = LANES // width
            parts = [(j * per + i, 0, width) for i in range(per)]
        for first in range(0, rows, SUB):
            many = min(SUB, rows - first)
            got = [par[base + k, first : first + many, at : at + w] for k, at, w in parts]
            value = got[0] if len(got) == 1 else jnp.concatenate(got, axis=1)
            dst[pl.ds(first * SUB + j, many, stride=SUB), :] = value


def segment_starts(lengths):
    starts = [jnp.int32(0)]
    for j in range(lengths.shape[1]):
        starts.append(starts[-1] + lengths[0, j])
    return starts


def fill_keep(keep, starts, base, rows):
    count = rows + HALO + 2

    def step(i, carry):
        keep[i] = jnp.float32(1.0)
        return carry

    lax.fori_loop(0, count, step, 0, unroll=4)
    for start in starts:
        at = start - base + 1

        @pl.when((at >= 0) & (at < count))
        def _():
            keep[at] = jnp.float32(0.0)


def rounded(value):
    return value.astype(BF16).astype(F32)


def flag(condition):
    return jnp.where(condition, 1.0, 0.0).astype(F32)


def unroll_of(trips):
    return max(d for d in range(1, 14) if trips % d == 0)


def featured(feat, tap, p, keep_one, keep_two):
    return (
        tap[0] * vec(feat, p + 2)
        + tap[1] * (keep_one * vec(feat, p + 1))
        + tap[2] * (keep_two * vec(feat, p))
    )


def each_group(groups, body):
    def step(half, carry):
        body(half)
        return carry

    lax.fori_loop(0, groups, step, 0)


def group_copies(sources, targets, sems, half):
    return [
        pltpu.make_async_copy(source.at[half], target.at[half], sems.at[half, i])
        for i, (source, target) in enumerate(zip(sources, targets))
    ]


def start_all(copies):
    for copy in copies:
        copy.start()


def wait_all(copies):
    for copy in copies:
        copy.wait()


def ends_kernel(
    rows, groups, far_lengths, features, upstream, left, right, taps, params,
    payload, feat_out, up_out, mixed_out, gout_out, par_out, tap_out,
    lengths, raw, raw_up, feat, up, mixed, gout, par, tap, stack, zero_scr, keep,
    length_sem, in_sems, out_sems,
):
    me = lax.axis_index("ctx")
    base = me * rows
    count = payload.shape[0]
    poles = (params.shape[1] - 1) // 2
    extended = rows + HALO
    padded = rows + 2 * HALO
    get_lengths = pltpu.make_async_copy(far_lengths, lengths, length_sem)
    get_lengths.start()

    def arriving(half):
        lanes = [
            pl.ds(pl.multiple_of((third * groups + half) * GROUP, GROUP), GROUP)
            for third in range(3)
        ]
        return [
            pltpu.make_async_copy(
                features.at[0, :, lanes[third]], raw.at[half, third], in_sems.at[half, third]
            )
            for third in range(3)
        ] + [pltpu.make_async_copy(upstream.at[0, :, lanes[0]], raw_up.at[half], in_sems.at[half, 3])]

    near = [feat, up, tap, par, mixed, gout]
    far = [feat_out, up_out, tap_out, par_out, mixed_out, gout_out]

    each_group(groups, lambda half: start_all(arriving(half)))
    zero_scr[...] = jnp.zeros((SUB, LANES), F32)
    zeros = [zero_scr[...]] * poles

    def prepare(half):
        spread_params(par.at[half], params, half, groups)
        for third in range(3):
            column = (third * groups + half) * GROUP
            spread(feat.at[half], third * padded, left, column, HALO)
            spread(feat.at[half], third * padded + rows + HALO, right, column, HALO)
            spread(tap.at[half], third * 3, taps, column, 3)
        spread(up.at[half], rows, right, (3 * groups + half) * GROUP, HALO)

    each_group(groups, prepare)
    get_lengths.wait()
    starts = segment_starts(lengths)
    fill_keep(keep, starts, base, rows)
    low, high = jnp.int32(0), jnp.int32(extended)
    for start in starts:
        at = start - base
        low = jnp.where(at < rows, jnp.maximum(low, at), low)
        high = jnp.where(at > HALO, jnp.minimum(high, at), high)

    def group(half):
        incoming = arriving(half)
        outgoing = group_copies(near, far, out_sems, half)
        feat_h, up_h, mixed_h, gout_h = feat.at[half], up.at[half], mixed.at[half], gout.at[half]
        for third in range(3):
            incoming[third].wait()
            spread_rows(feat_h, third * padded + HALO, raw.at[half, third], rows)
        incoming[3].wait()
        spread_rows(up_h, 0, raw_up.at[half], rows)
        start_all(outgoing[:4])
        taps_h = [[vec(tap.at[half], third * 3 + j) for j in range(3)] for third in range(3)]

        def product(p, carry):
            keep_one = keep[p + 1]
            keep_two = keep_one * keep[p]
            query, key, val = (
                featured(feat_h, taps_h[third], third * padded + p, keep_one, keep_two)
                for third in range(3)
            )
            put(mixed_h, p, rounded(key * val))
            put(gout_h, p, rounded(vec(up_h, p) * query))
            return carry

        lax.fori_loop(0, extended, product, 0, unroll=unroll_of(extended))
        start_all(outgoing[4:])
        decay = [jnp.exp(-jnp.exp(vec(par.at[half], m))) for m in range(poles)]

        def sweep(i, carry):
            state, adjoint = carry
            back = extended - 1 - i
            x = vec(mixed_h, i) * flag(i >= low)
            g = vec(gout_h, back) * flag(back < high)
            state = [decay[m] * state[m] + x for m in range(poles)]
            adjoint = [decay[m] * adjoint[m] + g for m in range(poles)]
            return state, adjoint

        state, adjoint = lax.fori_loop(0, rows, sweep, (zeros, zeros), unroll=8)
        for m in range(0, poles, 2):
            at = slice(m * SUB, (m + 2) * SUB)
            stack[0, at, :] = jnp.concatenate(state[m : m + 2], axis=0).astype(BF16)
            stack[1, at, :] = jnp.concatenate(adjoint[m : m + 2], axis=0).astype(BF16)
        for e in range(count):
            payload[e, half] = stack[jnp.where(e >= me, 0, 1)]

    each_group(groups, group)
    each_group(groups, lambda half: wait_all(group_copies(near, far, out_sems, half)))


def local_kernel(
    rows, groups, far_lengths, feat_in, mixed_in, gout_in, par_in, tap_in,
    key_out, val_out, conv_out, adj_out, partial_out,
    lengths, mixed, gout, par, tap, feat, key, val, conv, adj, partial, zero_scr, keep,
    length_sem, in_sems, out_sems,
):
    poles = (par.shape[1] // SUB - 1) // 2
    extended = rows + HALO
    padded = rows + 2 * HALO
    get_lengths = pltpu.make_async_copy(far_lengths, lengths, length_sem)
    get_lengths.start()
    far_in, near_in = [par_in, tap_in, feat_in, mixed_in, gout_in], [par, tap, feat, mixed, gout]
    near_out = [key, val, conv, adj, partial]
    far_out = [key_out, val_out, conv_out, adj_out, partial_out]
    each_group(groups, lambda half: start_all(group_copies(far_in, near_in, in_sems, half)))
    zero_scr[...] = jnp.zeros((SUB, LANES), F32)
    zero = zero_scr[...]
    per_pass = poles // 4
    zeros = [zero] * per_pass
    get_lengths.wait()
    fill_keep(keep, segment_starts(lengths), lax.axis_index("ctx") * rows, rows)

    def group(half):
        incoming = group_copies(far_in, near_in, in_sems, half)
        outgoing = group_copies(near_out, far_out, out_sems, half)
        feat_h, mixed_h, gout_h, par_h = feat.at[half], mixed.at[half], gout.at[half], par.at[half]
        conv_h, adj_h, key_h, val_h = conv.at[half], adj.at[half], key.at[half], val.at[half]
        wait_all(incoming)
        taps_h = [[vec(tap.at[half], third * 3 + j) for j in range(3)] for third in range(3)]

        def product(p, carry):
            keep_one = keep[p + 1]
            keep_two = keep_one * keep[p]
            put(key_h, p, featured(feat_h, taps_h[1], padded + p, keep_one, keep_two))
            put(val_h, p, featured(feat_h, taps_h[2], 2 * padded + p, keep_one, keep_two))
            return carry

        lax.fori_loop(0, extended, product, 0, unroll=unroll_of(extended))
        start_all(outgoing[:2])
        gain = vec(par_h, 2 * poles)
        for part in range(poles // per_pass):
            chosen = list(range(part * per_pass, (part + 1) * per_pass))
            decay = [jnp.exp(-jnp.exp(vec(par_h, m))) for m in chosen]
            coeff = [vec(par_h, poles + m) for m in chosen]

            def sweep(i, carry):
                state, adjoint, resid, skip = carry
                back = extended - 1 - i
                x = vec(mixed_h, i)
                g = vec(gout_h, back)
                own = vec(mixed_h, back) * flag(back < rows)
                keep_fwd = keep[i + 1]
                keep_bwd = keep[back + 2]
                state = [decay[m] * (state[m] * keep_fwd) + x for m in range(per_pass)]
                adjoint = [decay[m] * (adjoint[m] * keep_bwd) + g for m in range(per_pass)]
                resid = [resid[m] + own * adjoint[m] for m in range(per_pass)]
                forward = sum(coeff[m] * state[m] for m in range(per_pass))
                backward = sum(coeff[m] * adjoint[m] for m in range(per_pass))
                if part == 0:
                    put(conv_h, i, forward + gain * x)
                    put(adj_h, back, backward + gain * g)
                    skip = skip + own * g
                else:
                    put(conv_h, i, forward + vec(conv_h, i))
                    put(adj_h, back, backward + vec(adj_h, back))
                return state, adjoint, resid, skip

            _, _, resid, skip = lax.fori_loop(
                0, extended, sweep, (zeros, zeros, zeros, zero), unroll=unroll_of(extended)
            )
            for i, m in enumerate(chosen):
                put(partial.at[half], m, resid[i])
            if part == 0:
                put(partial.at[half], poles, skip)
        start_all(outgoing[2:])

    each_group(groups, group)
    each_group(groups, lambda half: wait_all(group_copies(near_out, far_out, out_sems, half)))


def finish_kernel(
    rows, groups, far_lengths, arrived, par_in, partial_in, tap_in, conv_in, adj_in, up_in,
    key_in, val_in, feat_in, grads, payload,
    lengths, par, partial, tap, conv, adj, up, key, val, feat, before, after, post, ready,
    sums, zero_scr, keep, length_sem, in_sems, out_sems,
):
    me = lax.axis_index("ctx")
    base = me * rows
    count = arrived.shape[0]
    poles = (par.shape[1] // SUB - 1) // 2
    extended = rows + HALO
    padded = rows + 2 * HALO
    get_lengths = pltpu.make_async_copy(far_lengths, lengths, length_sem)
    get_lengths.start()
    far = [par_in, partial_in, conv_in, adj_in, tap_in, up_in, key_in, val_in, feat_in]
    near = [par, partial, conv, adj, tap, up, key, val, feat]
    each_group(groups, lambda half: start_all(group_copies(far, near, in_sems, half)))

    def leaving(half):
        return [
            pltpu.make_async_copy(
                ready.at[half, third],
                grads.at[
                    0, :, pl.ds(pl.multiple_of((third * groups + half) * GROUP, GROUP), GROUP)
                ],
                out_sems.at[half, third],
            )
            for third in range(3)
        ]

    zero_scr[...] = jnp.zeros((SUB, LANES), F32)
    zero = zero_scr[...]
    get_lengths.wait()
    starts = segment_starts(lengths)
    fill_keep(keep, starts, base, rows)
    until, since = jnp.int32(extended), jnp.int32(0)
    first, last, newest = jnp.int32(0), jnp.int32(2**30), jnp.int32(0)
    for start in starts:
        at = start - base
        until = jnp.where(at >= 0, jnp.minimum(until, at), until)
        since = jnp.where(at <= extended, jnp.maximum(since, at), since)
        first = jnp.where(at <= 0, jnp.maximum(first, start), first)
        last = jnp.where(at > extended, jnp.minimum(last, start), last)
        newest = jnp.where(at <= extended, jnp.maximum(newest, start), newest)
    steps = jnp.maximum(until, extended - since)
    through = flag(newest < base + rows)
    chunk = unroll_of(extended)

    def group(half):
        incoming = group_copies(far, near, in_sems, half)
        par_h, partial_h, conv_h, adj_h = par.at[half], partial.at[half], conv.at[half], adj.at[half]
        up_h, key_h, val_h, feat_h = up.at[half], key.at[half], val.at[half], feat.at[half]
        wait_all(incoming[:2])
        per_pass = poles // 2
        zeros = [zero] * per_pass
        for part in range(2):
            chosen = list(range(part * per_pass, (part + 1) * per_pass))
            rate = [jnp.exp(vec(par_h, m)) for m in chosen]
            block = [jnp.exp(-rows * r) for r in rate]

            def arrived_states(d):
                got = []
                for m in range(chosen[0], chosen[-1] + 1, 2):
                    pair = arrived[d, half, m * SUB : (m + 2) * SUB, :].astype(F32)
                    got += [pair[:SUB], pair[SUB:]]
                return got

            def from_before(d, carry):
                joined = flag((d + 1) * rows - 1 >= first)
                got = arrived_states(d)
                return [block[i] * carry[i] + joined * got[i] for i in range(per_pass)]

            def from_after(i, carry):
                d = count - 1 - i
                joined = flag(d * rows + HALO < last)
                got = arrived_states(d)
                return [block[i] * carry[i] + joined * got[i] for i in range(per_pass)]

            state = lax.fori_loop(0, me, from_before, zeros)
            adjoint = lax.fori_loop(0, count - 1 - me, from_after, zeros)
            own = arrived_states(me)
            for i, m in enumerate(chosen):
                scale = vec(par_h, poles + m) * jnp.exp(-rate[i])
                put(before, m, scale * state[i])
                put(after, m, scale * adjoint[i])
                cross = jnp.exp(-(HALO + 1) * rate[i]) * (adjoint[i] * through)
                put(sums, (9 + m) * groups + half, vec(partial_h, m) + cross * own[i])
        put(sums, (9 + poles) * groups + half, vec(partial_h, poles))
        decay = [jnp.exp(-jnp.exp(vec(par_h, m))) for m in range(poles)]
        enter = [vec(before, m) for m in range(poles)]
        leave = [vec(after, m) for m in range(poles)]
        wait_all(incoming[2:4])

        def carried(i, carry):
            enter, leave = carry
            for step in range(chunk):
                p = chunk * i + step
                back = extended - 1 - p
                put(conv_h, p, vec(conv_h, p) + flag(p < until) * sum(enter))
                put(adj_h, back, vec(adj_h, back) + flag(back >= since) * sum(leave))
                enter = [decay[m] * enter[m] for m in range(poles)]
                leave = [decay[m] * leave[m] for m in range(poles)]
            return enter, leave

        lax.fori_loop(0, (steps + chunk - 1) // chunk, carried, (enter, leave))
        wait_all(incoming[4:])
        taps_h = [[vec(tap.at[half], third * 3 + j) for j in range(3)] for third in range(3)]

        def posted(p):
            keep_one = keep[p + 1]
            keep_two = keep_one * keep[p]
            conv_out = rounded(vec(conv_h, p))
            grad_mixed = rounded(vec(adj_h, p))
            now = [vec(up_h, p) * conv_out, grad_mixed * vec(val_h, p), grad_mixed * vec(key_h, p)]
            return now, [keep_one * g for g in now], [keep_two * g for g in now]

        _, _, far_two = posted(extended - 1)
        _, near_one, near_two = posted(extended - 2)

        def finish(i, carry):
            one, two, three, tap_sums = carry
            p = rows - 1 - i
            now, masked_one, masked_two = posted(p)
            new_sums = []
            for third in range(3):
                back = (
                    taps_h[third][0] * now[third]
                    + taps_h[third][1] * one[third]
                    + taps_h[third][2] * three[third]
                )
                put(post, third * rows + p, back)
                at = third * padded + p
                new_sums += [
                    tap_sums[3 * third] + now[third] * vec(feat_h, at + 2),
                    tap_sums[3 * third + 1] + masked_one[third] * vec(feat_h, at + 1),
                    tap_sums[3 * third + 2] + masked_two[third] * vec(feat_h, at),
                ]
            return masked_one, masked_two, two, new_sums

        _, _, _, tap_sums = lax.fori_loop(
            0, rows, finish, (near_one, near_two, far_two, [zero] * 9), unroll=4
        )
        for third in range(3):
            for j in range(3):
                put(sums, (3 * j + third) * groups + half, tap_sums[3 * third + j])

        def write(i, carry):
            for third in range(3):
                for j in range(SUB):
                    value = post[pl.ds((third * rows + i * 16) * SUB + j, 16, stride=SUB), :]
                    ready[
                        half, third, pl.ds(pl.multiple_of(i * 16, 16), 16), j * LANES : (j + 1) * LANES
                    ] = value.astype(BF16)
            return carry

        lax.fori_loop(0, rows // 16, write, 0)
        start_all(leaving(half))

    each_group(groups, group)
    width = groups * SUB
    same = 9 * width
    tap_sums = sums[0:same, :].astype(BF16)
    columns = (payload.shape[1] - same) // 16 - 1
    for e in range(count):
        payload[e, 0:same, :] = tap_sums
        first = same + (e * width) // count
        for j in range(columns):
            value = sums[pl.ds(first + j, 16, stride=width), :]
            payload[e, same + 16 * j : same + 16 * (j + 1), :] = value.astype(BF16)
        last = first + poles * width
        payload[e, same + 16 * columns :, :] = sums[last : last + 16, :].astype(BF16)
    each_group(groups, lambda half: wait_all(leaving(half)))


def share_kernel(parts, out):
    mine = parts[0].astype(F32)
    for k in range(1, parts.shape[0]):
        mine = mine + parts[k].astype(F32)
    out[...] = mine.astype(BF16)


def emit_kernel(groups, scale, shares, grad_taps, resid, skip, whole):
    me = lax.axis_index("ctx")
    width = groups * SUB
    poles, per_shard = resid.shape
    mine = shares[0].astype(F32)
    for k in range(1, shares.shape[0]):
        mine = mine + shares[k].astype(F32)
    whole[...] = mine * scale
    for k in range(3 * width):
        grad_taps[:, k * LANES : (k + 1) * LANES] = whole[pl.ds(k, 3, stride=3 * width), :]
    first = 9 * width
    columns = (whole.shape[0] - first) // 16 - 1
    last = first + 16 * columns
    if per_shard >= LANES:
        for j in range(columns):
            lanes = slice(j * LANES, (j + 1) * LANES)
            resid[:, lanes] = whole[first + 16 * j : first + 16 * (j + 1), :]
            skip[:, lanes] = whole[last + j : last + j + 1, :]
    else:
        per = LANES // per_shard
        rows = whole[first : first + 16, :]
        final = whole[last : last + 1, :]
        place = lax.rem(me, per)
        chosen, chosen_last = rows[:, :per_shard], final[:, :per_shard]
        for i in range(1, per):
            lanes = slice(i * per_shard, (i + 1) * per_shard)
            chosen = jnp.where(place == i, rows[:, lanes], chosen)
            chosen_last = jnp.where(place == i, final[:, lanes], chosen_last)
        resid[...] = chosen
        skip[...] = chosen_last


def swap(block, axes):
    return lax.all_to_all(block, axes, split_axis=0, concat_axis=0, tiled=True)


def per_device(features, upstream, lengths, conv_taps, residues, log_rate, skip_gain):
    rows = features.shape[1]
    channels = upstream.shape[2]
    poles = residues.shape[0]
    ctx_count = lax.axis_size("ctx")
    total = ctx_count * lax.axis_size("dp")
    per_shard = channels // ctx_count
    groups = channels // GROUP
    grad_scale = 1.0 / math.sqrt(rows * total)
    extended = rows + HALO
    padded = rows + 2 * HALO
    state_rows = poles * SUB
    limits = pltpu.CompilerParams(vmem_limit_bytes=40 * 1024 * 1024)
    hbm = pl.BlockSpec(memory_space=pltpu.HBM)
    vmem = pl.BlockSpec(memory_space=pltpu.VMEM)

    def tall(height):
        return jax.ShapeDtypeStruct((groups, height * SUB, LANES), F32)

    def near(*heights):
        return [pltpu.VMEM((groups, height * SUB, LANES), F32) for height in heights]

    def scratch(height):
        return pltpu.VMEM((height * SUB, LANES), F32)

    def sems(*shape):
        return pltpu.SemaphoreType.DMA(shape)

    keep = pltpu.SMEM((rows + 8,), F32)
    small = pltpu.SMEM(lengths.shape, jnp.int32)

    def call(kernel, name, ins, in_specs, outs, out_specs, scratch_shapes=()):
        ins = [
            pltpu.with_memory_space_constraint(x, pltpu.HBM) if spec is hbm else x
            for x, spec in zip(ins, in_specs)
        ]
        if isinstance(outs, list):
            outs = [
                pltpu.HBM(out.shape, out.dtype) if spec is hbm else out
                for out, spec in zip(outs, out_specs)
            ]
        return pl.pallas_call(
            kernel,
            out_shape=outs,
            in_specs=in_specs,
            out_specs=out_specs,
            scratch_shapes=list(scratch_shapes),
            compiler_params=limits,
            name=name,
        )(*ins)

    edge = features[0, rows - HALO :, :]
    head = jnp.concatenate([features[0, :HALO, :], upstream[0, :HALO, :]], axis=1)
    left = shifted(edge, "ctx", 1)
    right = shifted(head, "ctx", -1)
    params = jnp.concatenate([log_rate, residues, skip_gain[None]], axis=0)
    params = swap(jnp.broadcast_to(params[None], (ctx_count,) + params.shape), "ctx")

    payload, feat, up, mixed, gout, par, tap = call(
        functools.partial(ends_kernel, rows, groups),
        "ends",
        [lengths, features, upstream, left, right, conv_taps, params],
        [hbm] * 3 + [vmem] * 4,
        [jax.ShapeDtypeStruct((ctx_count, groups, state_rows, LANES), BF16)]
        + [tall(height) for height in [3 * padded] + [extended] * 3 + [2 * poles + 1, 9]],
        [vmem] + [hbm] * 6,
        [
            small,
            pltpu.VMEM((groups, 3, rows, GROUP), BF16),
            pltpu.VMEM((groups, rows, GROUP), BF16),
        ]
        + near(3 * padded, extended, extended, extended, 2 * poles + 1, 9)
        + [pltpu.VMEM((2, state_rows, LANES), BF16), scratch(1), keep]
        + [sems(), sems(groups, 4), sems(groups, 6)],
    )
    arrived = swap(payload, "ctx")
    key, val, conv, adj, partial = call(
        functools.partial(local_kernel, rows, groups),
        "local",
        [lengths, feat, mixed, gout, par, tap],
        [hbm] * 6,
        [tall(extended)] * 4 + [tall(poles + 1)],
        [hbm] * 5,
        [small]
        + near(extended, extended, 2 * poles + 1, 9, 3 * padded)
        + near(extended, extended, extended, extended, poles + 1)
        + [scratch(1), keep, sems(), sems(groups, 5), sems(groups, 5)],
    )
    used = (10 + poles) * groups * SUB
    sum_rows = 9 * groups * SUB + 16 * max(1, per_shard // LANES) + 16
    grads, sums = call(
        functools.partial(finish_kernel, rows, groups),
        "finish",
        [lengths, arrived, par, partial, tap, conv, adj, up, key, val, feat],
        [hbm, vmem] + [hbm] * 9,
        [
            jax.ShapeDtypeStruct(features.shape, BF16),
            jax.ShapeDtypeStruct((ctx_count, sum_rows, LANES), BF16),
        ],
        [hbm, vmem],
        [small]
        + near(2 * poles + 1, poles + 1, 9, extended, extended, extended, extended, extended)
        + near(3 * padded)
        + [scratch(poles), scratch(poles), scratch(3 * rows)]
        + [pltpu.VMEM((groups, 3, rows, GROUP), BF16)]
        + [pltpu.VMEM((used + 16, LANES), F32), scratch(1), keep]
        + [sems(), sems(groups, 9), sems(groups, 3)],
    )

    mine = call(
        share_kernel,
        "share",
        [swap(sums, "ctx")],
        [vmem],
        jax.ShapeDtypeStruct((sum_rows, LANES), BF16),
        vmem,
    )
    grad_taps, resid, skip = call(
        functools.partial(emit_kernel, groups, grad_scale),
        "emit",
        [lax.all_gather(mine, "dp")],
        [vmem],
        [
            jax.ShapeDtypeStruct((3, 3 * channels), F32),
            jax.ShapeDtypeStruct((poles, per_shard), F32),
            jax.ShapeDtypeStruct((1, per_shard), F32),
        ],
        [vmem] * 3,
        [pltpu.VMEM((sum_rows, LANES), F32)],
    )
    return grads, grad_taps, resid, skip.reshape(per_shard)


def solution(mesh):
    return jax.shard_map(
        per_device,
        mesh=mesh,
        in_specs=(
            P("dp", "ctx", None),
            P("dp", "ctx", None),
            P("dp", None),
            P(),
            P(None, "ctx"),
            P(None, "ctx"),
            P("ctx"),
        ),
        out_specs=(P("dp", "ctx", None), P(), P(None, "ctx"), P("ctx")),
        check_vma=False,
    )
```

```python
import functools
import math

import jax
import jax.numpy as jnp
from jax import lax
from jax.experimental import pallas as pl
from jax.experimental.pallas import tpu as pltpu
from jax.sharding import PartitionSpec as P

F32 = jnp.float32
BF16 = jnp.bfloat16
LANES = 128
SUB = 8
GROUP = SUB * LANES
HALO = 2


def shifted(block, axis, distance):
    count = lax.axis_size(axis)
    route = [(i - distance, i) for i in range(count) if 0 <= i - distance < count]
    return lax.ppermute(block, axis, route)


def vec(ref, index):
    return ref[pl.ds(pl.multiple_of(index * SUB, SUB), SUB), :]


def put(ref, index, value):
    ref[pl.ds(pl.multiple_of(index * SUB, SUB), SUB), :] = value


def spread(dst, first, src, column, row_count):
    for j in range(SUB):
        lanes = pl.ds(pl.multiple_of(column + j * LANES, LANES), LANES)
        dst[pl.ds(first * SUB + j, row_count, stride=SUB), :] = src[:, lanes].astype(F32)


def spread_rows(dst, first, src, row_count):
    def step(i, carry):
        for j in range(SUB):
            value = src[pl.ds(pl.multiple_of(i * 16, 16), 16), j * LANES : (j + 1) * LANES]
            dst[pl.ds((i * 16 + first) * SUB + j, 16, stride=SUB), :] = value.astype(F32)
        return carry

    lax.fori_loop(0, row_count // 16, step, 0)


def pack_kernel(log_rate, residues, skip_gain, out, slab):
    poles, width = log_rate.shape
    per = max(1, width // LANES)
    for j in range(per):
        lanes = slice(j * LANES, min(width, (j + 1) * LANES))
        slab[pl.ds(j, poles, stride=per), :] = log_rate[:, lanes]
        slab[pl.ds(poles * per + j, poles, stride=per), :] = residues[:, lanes]
        slab[pl.ds(2 * poles * per + j, 1), :] = skip_gain[:, lanes]
    for e in range(out.shape[0]):
        out[e] = slab[...]


def spread_params(dst, par, half, groups, rows):
    pieces, height, width = par.shape
    many = pieces // groups
    base = half * many
    if width == LANES:
        per = height // rows
        for k in range(many):
            for j in range(per):
                value = par[base + k, pl.ds(j, rows, stride=per), :]
                dst[pl.ds(k * per + j, rows, stride=SUB), :] = value
    else:
        per = LANES // width
        for j in range(SUB):
            parts = [par[base + j * per + i] for i in range(per)]
            dst[pl.ds(j, rows, stride=SUB), :] = jnp.concatenate(parts, axis=1)


def segment_starts(lengths):
    starts = [jnp.int32(0)]
    for j in range(lengths.shape[1]):
        starts.append(starts[-1] + lengths[0, j])
    return starts


def fill_keep(keep, starts, base, rows):
    count = rows + HALO + 2

    def step(i, carry):
        keep[i] = jnp.float32(1.0)
        return carry

    lax.fori_loop(0, count, step, 0, unroll=4)
    for start in starts:
        at = start - base + 1

        @pl.when((at >= 0) & (at < count))
        def _():
            keep[at] = jnp.float32(0.0)


def rounded(value):
    return value.astype(BF16).astype(F32)


def flag(condition):
    return jnp.where(condition, 1.0, 0.0).astype(F32)


def total_of(terms):
    terms = list(terms)
    while len(terms) > 1:
        odd = terms[-1:] if len(terms) % 2 else []
        terms = [x + y for x, y in zip(terms[::2], terms[1::2])] + odd
    return terms[0]


def unroll_of(trips):
    return max(d for d in range(1, 14) if trips % d == 0)


def featured(feat, tap, p, keep_one, keep_two):
    return (
        tap[0] * vec(feat, p + 2)
        + tap[1] * (keep_one * vec(feat, p + 1))
        + tap[2] * (keep_two * vec(feat, p))
    )


def each_group(groups, body):
    def step(half, carry):
        body(half)
        return carry

    lax.fori_loop(0, groups, step, 0)


def group_copies(sources, targets, sems, half):
    return [
        pltpu.make_async_copy(source.at[half], target.at[half], sems.at[half, i])
        for i, (source, target) in enumerate(zip(sources, targets))
    ]


def start_all(copies):
    for copy in copies:
        copy.start()


def wait_all(copies):
    for copy in copies:
        copy.wait()


def ends_kernel(
    rows, groups, far_lengths, features, upstream, left, right, taps, params,
    payload, feat_out, up_out, mixed_out, gout_out, par_out, tap_out,
    lengths, raw, raw_up, feat, up, mixed, gout, par, tap, stack, zero_scr, keep,
    length_sem, in_sems, out_sems,
):
    me = lax.axis_index("ctx")
    base = me * rows
    count = payload.shape[0]
    poles = (par.shape[1] // SUB - 1) // 2
    extended = rows + HALO
    padded = rows + 2 * HALO
    get_lengths = pltpu.make_async_copy(far_lengths, lengths, length_sem)
    get_lengths.start()

    def arriving(half):
        lanes = [
            pl.ds(pl.multiple_of((third * groups + half) * GROUP, GROUP), GROUP)
            for third in range(3)
        ]
        return [
            pltpu.make_async_copy(
                features.at[0, :, lanes[third]], raw.at[half, third], in_sems.at[half, third]
            )
            for third in range(3)
        ] + [pltpu.make_async_copy(upstream.at[0, :, lanes[0]], raw_up.at[half], in_sems.at[half, 3])]

    near = [feat, up, tap, par, mixed, gout]
    far = [feat_out, up_out, tap_out, par_out, mixed_out, gout_out]

    each_group(groups, lambda half: start_all(arriving(half)))
    zero_scr[...] = jnp.zeros((SUB, LANES), F32)
    zeros = [zero_scr[...]] * poles

    def prepare(half):
        spread_params(par.at[half], params, half, groups, 2 * poles + 1)
        for third in range(3):
            column = (third * groups + half) * GROUP
            spread(feat.at[half], third * padded, left, column, HALO)
            spread(feat.at[half], third * padded + rows + HALO, right, column, HALO)
            spread(tap.at[half], third * 3, taps, column, 3)
        spread(up.at[half], rows, right, (3 * groups + half) * GROUP, HALO)

    each_group(groups, prepare)
    get_lengths.wait()
    starts = segment_starts(lengths)
    fill_keep(keep, starts, base, rows)
    low, high = jnp.int32(0), jnp.int32(extended)
    for start in starts:
        at = start - base
        low = jnp.where(at < rows, jnp.maximum(low, at), low)
        high = jnp.where(at > HALO, jnp.minimum(high, at), high)

    def group(half):
        incoming = arriving(half)
        outgoing = group_copies(near, far, out_sems, half)
        feat_h, up_h, mixed_h, gout_h = feat.at[half], up.at[half], mixed.at[half], gout.at[half]
        for third in range(3):
            incoming[third].wait()
            spread_rows(feat_h, third * padded + HALO, raw.at[half, third], rows)
        incoming[3].wait()
        spread_rows(up_h, 0, raw_up.at[half], rows)
        start_all(outgoing[:4])
        taps_h = [[vec(tap.at[half], third * 3 + j) for j in range(3)] for third in range(3)]

        def product(p, carry):
            keep_one = keep[p + 1]
            keep_two = keep_one * keep[p]
            query, key, val = (
                featured(feat_h, taps_h[third], third * padded + p, keep_one, keep_two)
                for third in range(3)
            )
            put(mixed_h, p, rounded(key * val))
            put(gout_h, p, rounded(vec(up_h, p) * query))
            return carry

        lax.fori_loop(0, extended, product, 0, unroll=unroll_of(extended))
        start_all(outgoing[4:])
        decay = [jnp.exp(-jnp.exp(vec(par.at[half], m))) for m in range(poles)]

        def sweep(i, carry):
            state, adjoint = carry
            back = extended - 1 - i
            x = vec(mixed_h, i) * flag(i >= low)
            g = vec(gout_h, back) * flag(back < high)
            state = [decay[m] * state[m] + x for m in range(poles)]
            adjoint = [decay[m] * adjoint[m] + g for m in range(poles)]
            return state, adjoint

        state, adjoint = lax.fori_loop(0, rows, sweep, (zeros, zeros), unroll=8)
        for m in range(0, poles, 2):
            at = slice(m * SUB, (m + 2) * SUB)
            stack[0, at, :] = jnp.concatenate(state[m : m + 2], axis=0).astype(BF16)
            stack[1, at, :] = jnp.concatenate(adjoint[m : m + 2], axis=0).astype(BF16)
        for e in range(count):
            payload[e, half] = stack[jnp.where(e >= me, 0, 1)]

    each_group(groups, group)
    each_group(groups, lambda half: wait_all(group_copies(near, far, out_sems, half)))


def local_kernel(
    rows, groups, far_lengths, feat_in, mixed_in, gout_in, par_in, tap_in,
    key_out, val_out, conv_out, adj_out, partial_out,
    lengths, mixed, gout, par, tap, feat, key, val, conv, adj, partial, zero_scr, keep,
    length_sem, in_sems, out_sems,
):
    poles = (par.shape[1] // SUB - 1) // 2
    extended = rows + HALO
    padded = rows + 2 * HALO
    get_lengths = pltpu.make_async_copy(far_lengths, lengths, length_sem)
    get_lengths.start()
    far_in, near_in = [par_in, tap_in, feat_in, mixed_in, gout_in], [par, tap, feat, mixed, gout]
    near_out = [key, val, conv, adj, partial]
    far_out = [key_out, val_out, conv_out, adj_out, partial_out]
    each_group(groups, lambda half: start_all(group_copies(far_in, near_in, in_sems, half)))
    zero_scr[...] = jnp.zeros((SUB, LANES), F32)
    zero = zero_scr[...]
    per_pass = poles // 4
    zeros = [zero] * per_pass
    get_lengths.wait()
    fill_keep(keep, segment_starts(lengths), lax.axis_index("ctx") * rows, rows)

    def group(half):
        incoming = group_copies(far_in, near_in, in_sems, half)
        outgoing = group_copies(near_out, far_out, out_sems, half)
        feat_h, mixed_h, gout_h, par_h = feat.at[half], mixed.at[half], gout.at[half], par.at[half]
        conv_h, adj_h, key_h, val_h = conv.at[half], adj.at[half], key.at[half], val.at[half]
        wait_all(incoming)
        taps_h = [[vec(tap.at[half], third * 3 + j) for j in range(3)] for third in range(3)]

        def product(p, carry):
            keep_one = keep[p + 1]
            keep_two = keep_one * keep[p]
            put(key_h, p, featured(feat_h, taps_h[1], padded + p, keep_one, keep_two))
            put(val_h, p, featured(feat_h, taps_h[2], 2 * padded + p, keep_one, keep_two))
            return carry

        lax.fori_loop(0, extended, product, 0, unroll=unroll_of(extended))
        start_all(outgoing[:2])
        gain = vec(par_h, 2 * poles)
        for part in range(poles // per_pass):
            chosen = list(range(part * per_pass, (part + 1) * per_pass))
            decay = [jnp.exp(-jnp.exp(vec(par_h, m))) for m in chosen]
            coeff = [vec(par_h, poles + m) for m in chosen]

            def sweep(i, carry):
                state, adjoint, resid, skip = carry
                back = extended - 1 - i
                x = vec(mixed_h, i)
                g = vec(gout_h, back)
                own = vec(mixed_h, back) * flag(back < rows)
                keep_fwd = keep[i + 1]
                keep_bwd = keep[back + 2]
                state = [decay[m] * (state[m] * keep_fwd) + x for m in range(per_pass)]
                adjoint = [decay[m] * (adjoint[m] * keep_bwd) + g for m in range(per_pass)]
                resid = [resid[m] + own * adjoint[m] for m in range(per_pass)]
                forward = total_of(coeff[m] * state[m] for m in range(per_pass))
                backward = total_of(coeff[m] * adjoint[m] for m in range(per_pass))
                if part == 0:
                    put(conv_h, i, forward + gain * x)
                    put(adj_h, back, backward + gain * g)
                    skip = skip + own * g
                else:
                    put(conv_h, i, forward + vec(conv_h, i))
                    put(adj_h, back, backward + vec(adj_h, back))
                return state, adjoint, resid, skip

            _, _, resid, skip = lax.fori_loop(
                0, extended, sweep, (zeros, zeros, zeros, zero), unroll=unroll_of(extended)
            )
            for i, m in enumerate(chosen):
                put(partial.at[half], m, resid[i])
            if part == 0:
                put(partial.at[half], poles, skip)
        start_all(outgoing[2:])

    each_group(groups, group)
    each_group(groups, lambda half: wait_all(group_copies(near_out, far_out, out_sems, half)))


def finish_kernel(
    rows, groups, far_lengths, arrived, par_in, partial_in, tap_in, conv_in, adj_in, up_in,
    key_in, val_in, feat_in, grads, payload,
    lengths, par, partial, tap, conv, adj, up, key, val, feat, before, after, post, ready,
    sums, zero_scr, keep, length_sem, in_sems, out_sems,
):
    me = lax.axis_index("ctx")
    base = me * rows
    count = arrived.shape[0]
    poles = (par.shape[1] // SUB - 1) // 2
    extended = rows + HALO
    padded = rows + 2 * HALO
    get_lengths = pltpu.make_async_copy(far_lengths, lengths, length_sem)
    get_lengths.start()
    far = [par_in, partial_in, conv_in, adj_in, tap_in, up_in, key_in, val_in, feat_in]
    near = [par, partial, conv, adj, tap, up, key, val, feat]
    each_group(groups, lambda half: start_all(group_copies(far, near, in_sems, half)))

    def leaving(half):
        return [
            pltpu.make_async_copy(
                ready.at[half, third],
                grads.at[
                    0, :, pl.ds(pl.multiple_of((third * groups + half) * GROUP, GROUP), GROUP)
                ],
                out_sems.at[half, third],
            )
            for third in range(3)
        ]

    zero_scr[...] = jnp.zeros((SUB, LANES), F32)
    zero = zero_scr[...]
    get_lengths.wait()
    starts = segment_starts(lengths)
    fill_keep(keep, starts, base, rows)
    until, since = jnp.int32(extended), jnp.int32(0)
    first, last, newest = jnp.int32(0), jnp.int32(2**30), jnp.int32(0)
    for start in starts:
        at = start - base
        until = jnp.where(at >= 0, jnp.minimum(until, at), until)
        since = jnp.where(at <= extended, jnp.maximum(since, at), since)
        first = jnp.where(at <= 0, jnp.maximum(first, start), first)
        last = jnp.where(at > extended, jnp.minimum(last, start), last)
        newest = jnp.where(at <= extended, jnp.maximum(newest, start), newest)
    steps = jnp.maximum(until, extended - since)
    through = flag(newest < base + rows)
    chunk = unroll_of(extended)

    def group(half):
        incoming = group_copies(far, near, in_sems, half)
        par_h, partial_h, conv_h, adj_h = par.at[half], partial.at[half], conv.at[half], adj.at[half]
        up_h, key_h, val_h, feat_h = up.at[half], key.at[half], val.at[half], feat.at[half]
        wait_all(incoming[:2])
        per_pass = poles // 2
        zeros = [zero] * per_pass
        for part in range(2):
            chosen = list(range(part * per_pass, (part + 1) * per_pass))
            rate = [jnp.exp(vec(par_h, m)) for m in chosen]
            block = [jnp.exp(-rows * r) for r in rate]

            def arrived_states(d):
                got = []
                for m in range(chosen[0], chosen[-1] + 1, 2):
                    pair = arrived[d, half, m * SUB : (m + 2) * SUB, :].astype(F32)
                    got += [pair[:SUB], pair[SUB:]]
                return got

            def from_before(d, carry):
                joined = flag((d + 1) * rows - 1 >= first)
                got = arrived_states(d)
                return [block[i] * carry[i] + joined * got[i] for i in range(per_pass)]

            def from_after(i, carry):
                d = count - 1 - i
                joined = flag(d * rows + HALO < last)
                got = arrived_states(d)
                return [block[i] * carry[i] + joined * got[i] for i in range(per_pass)]

            state = lax.fori_loop(0, me, from_before, zeros)
            adjoint = lax.fori_loop(0, count - 1 - me, from_after, zeros)
            own = arrived_states(me)
            for i, m in enumerate(chosen):
                scale = vec(par_h, poles + m) * jnp.exp(-rate[i])
                put(before, m, scale * state[i])
                put(after, m, scale * adjoint[i])
                cross = jnp.exp(-(HALO + 1) * rate[i]) * (adjoint[i] * through)
                put(sums, (9 + m) * groups + half, vec(partial_h, m) + cross * own[i])
        put(sums, (9 + poles) * groups + half, vec(partial_h, poles))
        decay = [jnp.exp(-jnp.exp(vec(par_h, m))) for m in range(poles)]
        enter = [vec(before, m) for m in range(poles)]
        leave = [vec(after, m) for m in range(poles)]
        wait_all(incoming[2:4])

        def carried(i, carry):
            enter, leave = carry
            for step in range(chunk):
                p = chunk * i + step
                back = extended - 1 - p
                put(conv_h, p, vec(conv_h, p) + flag(p < until) * total_of(enter))
                put(adj_h, back, vec(adj_h, back) + flag(back >= since) * total_of(leave))
                enter = [decay[m] * enter[m] for m in range(poles)]
                leave = [decay[m] * leave[m] for m in range(poles)]
            return enter, leave

        lax.fori_loop(0, (steps + chunk - 1) // chunk, carried, (enter, leave))
        wait_all(incoming[4:])
        taps_h = [[vec(tap.at[half], third * 3 + j) for j in range(3)] for third in range(3)]

        def posted(p):
            keep_one = keep[p + 1]
            keep_two = keep_one * keep[p]
            conv_out = rounded(vec(conv_h, p))
            grad_mixed = rounded(vec(adj_h, p))
            now = [vec(up_h, p) * conv_out, grad_mixed * vec(val_h, p), grad_mixed * vec(key_h, p)]
            return now, [keep_one * g for g in now], [keep_two * g for g in now]

        _, _, far_two = posted(extended - 1)
        _, near_one, near_two = posted(extended - 2)

        def finish(i, carry):
            one, two, three, tap_sums, feat_now, feat_one = carry
            p = rows - 1 - i
            now, masked_one, masked_two = posted(p)
            feat_two = [vec(feat_h, third * padded + p) for third in range(3)]
            new_sums = []
            for third in range(3):
                back = (
                    taps_h[third][0] * now[third]
                    + taps_h[third][1] * one[third]
                    + taps_h[third][2] * three[third]
                )
                put(post, third * rows + p, back)
                new_sums += [
                    tap_sums[3 * third] + now[third] * feat_now[third],
                    tap_sums[3 * third + 1] + masked_one[third] * feat_one[third],
                    tap_sums[3 * third + 2] + masked_two[third] * feat_two[third],
                ]
            return masked_one, masked_two, two, new_sums, feat_one, feat_two

        feat_last = [vec(feat_h, third * padded + rows + 1) for third in range(3)]
        feat_before = [vec(feat_h, third * padded + rows) for third in range(3)]
        _, _, _, tap_sums, _, _ = lax.fori_loop(
            0,
            rows,
            finish,
            (near_one, near_two, far_two, [zero] * 9, feat_last, feat_before),
            unroll=4,
        )
        for third in range(3):
            for j in range(3):
                put(sums, (3 * j + third) * groups + half, tap_sums[3 * third + j])

        def write(i, carry):
            for third in range(3):
                for j in range(SUB):
                    value = post[pl.ds((third * rows + i * 16) * SUB + j, 16, stride=SUB), :]
                    ready[
                        half, third, pl.ds(pl.multiple_of(i * 16, 16), 16), j * LANES : (j + 1) * LANES
                    ] = value.astype(BF16)
            return carry

        lax.fori_loop(0, rows // 16, write, 0)
        start_all(leaving(half))

    each_group(groups, group)
    width = groups * SUB
    same = 9 * width
    tap_sums = sums[0:same, :].astype(BF16)
    columns = (payload.shape[1] - same) // 16 - 1
    for e in range(count):
        payload[e, 0:same, :] = tap_sums
        first = same + (e * width) // count
        for j in range(columns):
            value = sums[pl.ds(first + j, 16, stride=width), :]
            payload[e, same + 16 * j : same + 16 * (j + 1), :] = value.astype(BF16)
        last = first + poles * width
        payload[e, same + 16 * columns :, :] = sums[last : last + 16, :].astype(BF16)
    each_group(groups, lambda half: wait_all(leaving(half)))


def share_kernel(parts, out):
    mine = parts[0].astype(F32)
    for k in range(1, parts.shape[0]):
        mine = mine + parts[k].astype(F32)
    out[...] = mine.astype(BF16)


def emit_kernel(groups, scale, shares, grad_taps, resid, skip, whole):
    me = lax.axis_index("ctx")
    width = groups * SUB
    poles, per_shard = resid.shape
    mine = shares[0].astype(F32)
    for k in range(1, shares.shape[0]):
        mine = mine + shares[k].astype(F32)
    whole[...] = mine * scale
    for k in range(3 * width):
        grad_taps[:, k * LANES : (k + 1) * LANES] = whole[pl.ds(k, 3, stride=3 * width), :]
    first = 9 * width
    columns = (whole.shape[0] - first) // 16 - 1
    last = first + 16 * columns
    if per_shard >= LANES:
        for j in range(columns):
            lanes = slice(j * LANES, (j + 1) * LANES)
            resid[:, lanes] = whole[first + 16 * j : first + 16 * (j + 1), :]
            skip[:, lanes] = whole[last + j : last + j + 1, :]
    else:
        per = LANES // per_shard
        rows = whole[first : first + 16, :]
        final = whole[last : last + 1, :]
        place = lax.rem(me, per)
        chosen, chosen_last = rows[:, :per_shard], final[:, :per_shard]
        for i in range(1, per):
            lanes = slice(i * per_shard, (i + 1) * per_shard)
            chosen = jnp.where(place == i, rows[:, lanes], chosen)
            chosen_last = jnp.where(place == i, final[:, lanes], chosen_last)
        resid[...] = chosen
        skip[...] = chosen_last


def swap(block, axes):
    return lax.all_to_all(block, axes, split_axis=0, concat_axis=0, tiled=True)


def per_device(features, upstream, lengths, conv_taps, residues, log_rate, skip_gain):
    rows = features.shape[1]
    channels = upstream.shape[2]
    poles = residues.shape[0]
    ctx_count = lax.axis_size("ctx")
    total = ctx_count * lax.axis_size("dp")
    per_shard = channels // ctx_count
    groups = channels // GROUP
    grad_scale = 1.0 / math.sqrt(rows * total)
    extended = rows + HALO
    padded = rows + 2 * HALO
    state_rows = poles * SUB
    limits = pltpu.CompilerParams(vmem_limit_bytes=40 * 1024 * 1024)
    hbm = pl.BlockSpec(memory_space=pltpu.HBM)
    vmem = pl.BlockSpec(memory_space=pltpu.VMEM)

    def tall(height):
        return jax.ShapeDtypeStruct((groups, height * SUB, LANES), F32)

    def near(*heights):
        return [pltpu.VMEM((groups, height * SUB, LANES), F32) for height in heights]

    def scratch(height):
        return pltpu.VMEM((height * SUB, LANES), F32)

    def sems(*shape):
        return pltpu.SemaphoreType.DMA(shape)

    keep = pltpu.SMEM((rows + 8,), F32)
    small = pltpu.SMEM(lengths.shape, jnp.int32)

    def call(kernel, name, ins, in_specs, outs, out_specs, scratch_shapes=()):
        ins = [
            pltpu.with_memory_space_constraint(x, pltpu.HBM) if spec is hbm else x
            for x, spec in zip(ins, in_specs)
        ]
        if isinstance(outs, list):
            outs = [
                pltpu.HBM(out.shape, out.dtype) if spec is hbm else out
                for out, spec in zip(outs, out_specs)
            ]
        return pl.pallas_call(
            kernel,
            out_shape=outs,
            in_specs=in_specs,
            out_specs=out_specs,
            scratch_shapes=list(scratch_shapes),
            compiler_params=limits,
            name=name,
        )(*ins)

    edge = features[0, rows - HALO :, :]
    head = jnp.concatenate([features[0, :HALO, :], upstream[0, :HALO, :]], axis=1)
    left = shifted(edge, "ctx", 1)
    right = shifted(head, "ctx", -1)
    slab = ((2 * poles + 1) * max(1, per_shard // LANES), min(per_shard, LANES))
    params = call(
        pack_kernel,
        "pack",
        [log_rate, residues, skip_gain[None]],
        [vmem] * 3,
        jax.ShapeDtypeStruct((ctx_count,) + slab, F32),
        vmem,
        [pltpu.VMEM(slab, F32)],
    )
    params = swap(params, "ctx")

    payload, feat, up, mixed, gout, par, tap = call(
        functools.partial(ends_kernel, rows, groups),
        "ends",
        [lengths, features, upstream, left, right, conv_taps, params],
        [hbm] * 3 + [vmem] * 4,
        [jax.ShapeDtypeStruct((ctx_count, groups, state_rows, LANES), BF16)]
        + [tall(height) for height in [3 * padded] + [extended] * 3 + [2 * poles + 1, 9]],
        [vmem] + [hbm] * 6,
        [
            small,
            pltpu.VMEM((groups, 3, rows, GROUP), BF16),
            pltpu.VMEM((groups, rows, GROUP), BF16),
        ]
        + near(3 * padded, extended, extended, extended, 2 * poles + 1, 9)
        + [pltpu.VMEM((2, state_rows, LANES), BF16), scratch(1), keep]
        + [sems(), sems(groups, 4), sems(groups, 6)],
    )
    arrived = swap(payload, "ctx")
    key, val, conv, adj, partial = call(
        functools.partial(local_kernel, rows, groups),
        "local",
        [lengths, feat, mixed, gout, par, tap],
        [hbm] * 6,
        [tall(extended)] * 4 + [tall(poles + 1)],
        [hbm] * 5,
        [small]
        + near(extended, extended, 2 * poles + 1, 9, 3 * padded)
        + near(extended, extended, extended, extended, poles + 1)
        + [scratch(1), keep, sems(), sems(groups, 5), sems(groups, 5)],
    )
    used = (10 + poles) * groups * SUB
    sum_rows = 9 * groups * SUB + 16 * max(1, per_shard // LANES) + 16
    grads, sums = call(
        functools.partial(finish_kernel, rows, groups),
        "finish",
        [lengths, arrived, par, partial, tap, conv, adj, up, key, val, feat],
        [hbm, vmem] + [hbm] * 9,
        [
            jax.ShapeDtypeStruct(features.shape, BF16),
            jax.ShapeDtypeStruct((ctx_count, sum_rows, LANES), BF16),
        ],
        [hbm, vmem],
        [small]
        + near(2 * poles + 1, poles + 1, 9, extended, extended, extended, extended, extended)
        + near(3 * padded)
        + [scratch(poles), scratch(poles), scratch(3 * rows)]
        + [pltpu.VMEM((groups, 3, rows, GROUP), BF16)]
        + [pltpu.VMEM((used + 16, LANES), F32), scratch(1), keep]
        + [sems(), sems(groups, 9), sems(groups, 3)],
    )

    mine = call(
        share_kernel,
        "share",
        [swap(sums, "ctx")],
        [vmem],
        jax.ShapeDtypeStruct((sum_rows, LANES), BF16),
        vmem,
    )
    grad_taps, resid, skip = call(
        functools.partial(emit_kernel, groups, grad_scale),
        "emit",
        [lax.all_gather(mine, "dp")],
        [vmem],
        [
            jax.ShapeDtypeStruct((3, 3 * channels), F32),
            jax.ShapeDtypeStruct((poles, per_shard), F32),
            jax.ShapeDtypeStruct((1, per_shard), F32),
        ],
        [vmem] * 3,
        [pltpu.VMEM((sum_rows, LANES), F32)],
    )
    return grads, grad_taps, resid, skip.reshape(per_shard)


def solution(mesh):
    return jax.shard_map(
        per_device,
        mesh=mesh,
        in_specs=(
            P("dp", "ctx", None),
            P("dp", "ctx", None),
            P("dp", None),
            P(),
            P(None, "ctx"),
            P(None, "ctx"),
            P("ctx"),
        ),
        out_specs=(P("dp", "ctx", None), P(), P(None, "ctx"), P("ctx")),
        check_vma=False,
    )
```

```python
import functools
import math

import jax
import jax.numpy as jnp
from jax import lax
from jax.experimental import pallas as pl
from jax.experimental.pallas import tpu as pltpu
from jax.sharding import PartitionSpec as P

F32 = jnp.float32
BF16 = jnp.bfloat16
LANES = 128
SUB = 8
GROUP = SUB * LANES
HALO = 2


def shifted(block, axis, distance):
    count = lax.axis_size(axis)
    route = [(i - distance, i) for i in range(count) if 0 <= i - distance < count]
    return lax.ppermute(block, axis, route)


def vec(ref, index):
    return ref[pl.ds(pl.multiple_of(index * SUB, SUB), SUB), :]


def put(ref, index, value):
    ref[pl.ds(pl.multiple_of(index * SUB, SUB), SUB), :] = value


def spread(dst, first, src, column, row_count):
    for j in range(SUB):
        lanes = pl.ds(pl.multiple_of(column + j * LANES, LANES), LANES)
        dst[pl.ds(first * SUB + j, row_count, stride=SUB), :] = src[:, lanes].astype(F32)


def spread_rows(dst, first, src, row_count):
    def step(i, carry):
        for j in range(SUB):
            value = src[pl.ds(pl.multiple_of(i * 16, 16), 16), j * LANES : (j + 1) * LANES]
            dst[pl.ds((i * 16 + first) * SUB + j, 16, stride=SUB), :] = value.astype(F32)
        return carry

    lax.fori_loop(0, row_count // 16, step, 0)


def tiles_of(width):
    return max(1, width // LANES)


def start_kernel(
    log_rate, residues, skip_gain, features, upstream, out, edge, head,
    rates, coeffs, gains, low, high, high_up, slab, sems,
):
    rows = features.shape[1]
    copies = [
        pltpu.make_async_copy(source, target, sems.at[i])
        for i, (source, target) in enumerate(
            [
                (log_rate, rates),
                (residues, coeffs),
                (skip_gain, gains),
                (features.at[0, pl.ds(0, 16), :], low),
                (features.at[0, pl.ds(rows - 16, 16), :], high),
                (upstream.at[0, pl.ds(0, 16), :], high_up),
            ]
        )
    ]
    start_all(copies)
    poles, width = rates.shape
    per = tiles_of(width)
    slab[...] = jnp.zeros(slab.shape, F32)
    wait_all(copies[:3])
    for j in range(per):
        lanes = slice(j * LANES, min(width, (j + 1) * LANES))
        rate, gain = rates[:, lanes], gains[:, lanes]
        slab[pl.ds(j, poles, stride=per), :] = rounded(rate)
        slab[pl.ds(poles * per + j, poles, stride=per), :] = rate - rounded(rate)
        slab[pl.ds(2 * poles * per + j, poles, stride=per), :] = coeffs[:, lanes]
        slab[pl.ds(3 * poles * per + j, 1), :] = rounded(gain)
        slab[pl.ds((3 * poles + 1) * per + j, 1), :] = gain - rounded(gain)
    packed = slab[...].astype(BF16)
    for e in range(out.shape[0]):
        out[e] = packed
    wait_all(copies[3:])
    span = features.shape[2]
    for at in range(0, span, GROUP):
        lanes = slice(at, at + GROUP)
        head[:, lanes] = low[:, lanes].astype(F32)[:HALO].astype(BF16)
        edge[:, lanes] = high[:, lanes].astype(F32)[16 - HALO :].astype(BF16)
    for at in range(0, upstream.shape[2], GROUP):
        lanes = slice(at, at + GROUP)
        head[:, span + at : span + at + GROUP] = high_up[:, lanes].astype(F32)[:HALO].astype(BF16)


def spread_params(dst, par, slab, half, groups, poles):
    pieces, height, width = par.shape
    many = pieces // groups
    base = half * many
    joined = LANES // width
    per = (height - 16) // (3 * poles)
    for k in range(many // joined):
        parts = [par[base + k * joined + i].astype(F32) for i in range(joined)]
        slab[...] = parts[0] if joined == 1 else jnp.concatenate(parts, axis=1)
        for j in range(per):
            to = k * per + j

            def rows_of(piece, count=poles):
                return slab[pl.ds(piece * per + j, count, stride=per), :]

            dst[pl.ds(to, poles, stride=SUB), :] = rows_of(0) + rows_of(poles)
            dst[pl.ds(poles * SUB + to, poles, stride=SUB), :] = rows_of(2 * poles)
            gain = rows_of(3 * poles, 1) + rows_of(3 * poles + 1, 1)
            dst[pl.ds(2 * poles * SUB + to, 1), :] = gain


def segment_starts(lengths):
    starts = [jnp.int32(0)]
    for j in range(lengths.shape[1]):
        starts.append(starts[-1] + lengths[0, j])
    return starts


def fill_keep(keep, starts, base, rows):
    count = rows + HALO + 2

    def step(i, carry):
        keep[i] = jnp.float32(1.0)
        return carry

    lax.fori_loop(0, count, step, 0, unroll=4)
    for start in starts:
        at = start - base + 1

        @pl.when((at >= 0) & (at < count))
        def _():
            keep[at] = jnp.float32(0.0)


def rounded(value):
    return value.astype(BF16).astype(F32)


def flag(condition):
    return jnp.where(condition, 1.0, 0.0).astype(F32)


def total_of(terms):
    terms = list(terms)
    while len(terms) > 1:
        odd = terms[-1:] if len(terms) % 2 else []
        terms = [x + y for x, y in zip(terms[::2], terms[1::2])] + odd
    return terms[0]


def unroll_of(trips):
    return max(d for d in range(1, 14) if trips % d == 0)


def featured(feat, tap, p, keep_one, keep_two):
    return (
        tap[0] * vec(feat, p + 2)
        + tap[1] * (keep_one * vec(feat, p + 1))
        + tap[2] * (keep_two * vec(feat, p))
    )


def each_group(groups, body):
    def step(half, carry):
        body(half)
        return carry

    lax.fori_loop(0, groups, step, 0)


def group_copies(sources, targets, sems, half):
    return [
        pltpu.make_async_copy(source.at[half], target.at[half], sems.at[half, i])
        for i, (source, target) in enumerate(zip(sources, targets))
    ]


def start_all(copies):
    for copy in copies:
        copy.start()


def wait_all(copies):
    for copy in copies:
        copy.wait()


def ends_kernel(
    rows, groups, far_lengths, features, upstream, left, right, taps, params,
    payload, feat_out, up_out, mixed_out, gout_out, par_out, tap_out,
    lengths, raw, raw_up, feat, up, mixed, gout, par, tap, stack, slab, zero_scr, keep,
    length_sem, in_sems, out_sems,
):
    me = lax.axis_index("ctx")
    base = me * rows
    count = payload.shape[0]
    poles = (par.shape[1] // SUB - 1) // 2
    extended = rows + HALO
    padded = rows + 2 * HALO
    get_lengths = pltpu.make_async_copy(far_lengths, lengths, length_sem)
    get_lengths.start()

    def arriving(half):
        lanes = [
            pl.ds(pl.multiple_of((third * groups + half) * GROUP, GROUP), GROUP)
            for third in range(3)
        ]
        return [
            pltpu.make_async_copy(
                features.at[0, :, lanes[third]], raw.at[half, third], in_sems.at[half, third]
            )
            for third in range(3)
        ] + [pltpu.make_async_copy(upstream.at[0, :, lanes[0]], raw_up.at[half], in_sems.at[half, 3])]

    near = [feat, up, tap, par, mixed, gout]
    far = [feat_out, up_out, tap_out, par_out, mixed_out, gout_out]

    each_group(groups, lambda half: start_all(arriving(half)))
    zero_scr[...] = jnp.zeros((SUB, LANES), F32)
    zeros = [zero_scr[...]] * poles

    def prepare(half):
        spread_params(par.at[half], params, slab, half, groups, poles)
        for third in range(3):
            column = (third * groups + half) * GROUP
            spread(feat.at[half], third * padded, left, column, HALO)
            spread(feat.at[half], third * padded + rows + HALO, right, column, HALO)
            spread(tap.at[half], third * 3, taps, column, 3)
        spread(up.at[half], rows, right, (3 * groups + half) * GROUP, HALO)

    each_group(groups, prepare)
    get_lengths.wait()
    starts = segment_starts(lengths)
    fill_keep(keep, starts, base, rows)
    low, high = jnp.int32(0), jnp.int32(extended)
    for start in starts:
        at = start - base
        low = jnp.where(at < rows, jnp.maximum(low, at), low)
        high = jnp.where(at > HALO, jnp.minimum(high, at), high)

    def group(half):
        incoming = arriving(half)
        outgoing = group_copies(near, far, out_sems, half)
        feat_h, up_h, mixed_h, gout_h = feat.at[half], up.at[half], mixed.at[half], gout.at[half]
        for third in range(3):
            incoming[third].wait()
            spread_rows(feat_h, third * padded + HALO, raw.at[half, third], rows)
        incoming[3].wait()
        spread_rows(up_h, 0, raw_up.at[half], rows)
        start_all(outgoing[:4])
        taps_h = [[vec(tap.at[half], third * 3 + j) for j in range(3)] for third in range(3)]

        def product(p, carry):
            keep_one = keep[p + 1]
            keep_two = keep_one * keep[p]
            query, key, val = (
                featured(feat_h, taps_h[third], third * padded + p, keep_one, keep_two)
                for third in range(3)
            )
            put(mixed_h, p, rounded(key * val))
            put(gout_h, p, rounded(vec(up_h, p) * query))
            return carry

        lax.fori_loop(0, extended, product, 0, unroll=unroll_of(extended))
        start_all(outgoing[4:])
        decay = [jnp.exp(-jnp.exp(vec(par.at[half], m))) for m in range(poles)]

        def sweep(i, carry):
            state, adjoint = carry
            back = extended - 1 - i
            x = vec(mixed_h, i) * flag(i >= low)
            g = vec(gout_h, back) * flag(back < high)
            state = [decay[m] * state[m] + x for m in range(poles)]
            adjoint = [decay[m] * adjoint[m] + g for m in range(poles)]
            return state, adjoint

        state, adjoint = lax.fori_loop(0, rows, sweep, (zeros, zeros), unroll=8)
        for m in range(0, poles, 2):
            at = slice(m * SUB, (m + 2) * SUB)
            stack[0, at, :] = jnp.concatenate(state[m : m + 2], axis=0).astype(BF16)
            stack[1, at, :] = jnp.concatenate(adjoint[m : m + 2], axis=0).astype(BF16)
        for e in range(count):
            payload[e, half] = stack[jnp.where(e >= me, 0, 1)]

    each_group(groups, group)
    each_group(groups, lambda half: wait_all(group_copies(near, far, out_sems, half)))


def local_kernel(
    rows, groups, far_lengths, feat_in, mixed_in, gout_in, par_in, tap_in,
    key_out, val_out, conv_out, adj_out, partial_out,
    lengths, mixed, gout, par, tap, feat, key, val, conv, adj, partial, zero_scr, keep,
    length_sem, in_sems, out_sems,
):
    poles = (par.shape[1] // SUB - 1) // 2
    extended = rows + HALO
    padded = rows + 2 * HALO
    get_lengths = pltpu.make_async_copy(far_lengths, lengths, length_sem)
    get_lengths.start()
    far_in, near_in = [par_in, tap_in, feat_in, mixed_in, gout_in], [par, tap, feat, mixed, gout]
    near_out = [key, val, conv, adj, partial]
    far_out = [key_out, val_out, conv_out, adj_out, partial_out]
    each_group(groups, lambda half: start_all(group_copies(far_in, near_in, in_sems, half)))
    zero_scr[...] = jnp.zeros((SUB, LANES), F32)
    zero = zero_scr[...]
    per_pass = poles // 4
    zeros = [zero] * per_pass
    get_lengths.wait()
    fill_keep(keep, segment_starts(lengths), lax.axis_index("ctx") * rows, rows)

    def group(half):
        incoming = group_copies(far_in, near_in, in_sems, half)
        outgoing = group_copies(near_out, far_out, out_sems, half)
        feat_h, mixed_h, gout_h, par_h = feat.at[half], mixed.at[half], gout.at[half], par.at[half]
        conv_h, adj_h, key_h, val_h = conv.at[half], adj.at[half], key.at[half], val.at[half]
        wait_all(incoming)
        taps_h = [[vec(tap.at[half], third * 3 + j) for j in range(3)] for third in range(3)]

        def product(p, carry):
            keep_one = keep[p + 1]
            keep_two = keep_one * keep[p]
            put(key_h, p, featured(feat_h, taps_h[1], padded + p, keep_one, keep_two))
            put(val_h, p, featured(feat_h, taps_h[2], 2 * padded + p, keep_one, keep_two))
            return carry

        lax.fori_loop(0, extended, product, 0, unroll=unroll_of(extended))
        start_all(outgoing[:2])
        gain = vec(par_h, 2 * poles)
        for part in range(poles // per_pass):
            chosen = list(range(part * per_pass, (part + 1) * per_pass))
            decay = [jnp.exp(-jnp.exp(vec(par_h, m))) for m in chosen]
            coeff = [vec(par_h, poles + m) for m in chosen]

            def sweep(i, carry):
                state, adjoint, resid, skip = carry
                back = extended - 1 - i
                x = vec(mixed_h, i)
                g = vec(gout_h, back)
                own = vec(mixed_h, back) * flag(back < rows)
                keep_fwd = keep[i + 1]
                keep_bwd = keep[back + 2]
                state = [decay[m] * (state[m] * keep_fwd) + x for m in range(per_pass)]
                adjoint = [decay[m] * (adjoint[m] * keep_bwd) + g for m in range(per_pass)]
                resid = [resid[m] + own * adjoint[m] for m in range(per_pass)]
                forward = total_of(coeff[m] * state[m] for m in range(per_pass))
                backward = total_of(coeff[m] * adjoint[m] for m in range(per_pass))
                if part == 0:
                    put(conv_h, i, forward + gain * x)
                    put(adj_h, back, backward + gain * g)
                    skip = skip + own * g
                else:
                    put(conv_h, i, forward + vec(conv_h, i))
                    put(adj_h, back, backward + vec(adj_h, back))
                return state, adjoint, resid, skip

            _, _, resid, skip = lax.fori_loop(
                0, extended, sweep, (zeros, zeros, zeros, zero), unroll=unroll_of(extended)
            )
            for i, m in enumerate(chosen):
                put(partial.at[half], m, resid[i])
            if part == 0:
                put(partial.at[half], poles, skip)
        start_all(outgoing[2:])

    each_group(groups, group)
    each_group(groups, lambda half: wait_all(group_copies(near_out, far_out, out_sems, half)))


def finish_kernel(
    rows, groups, far_lengths, arrived, par_in, partial_in, tap_in, conv_in, adj_in, up_in,
    key_in, val_in, feat_in, grads, payload,
    lengths, par, partial, tap, conv, adj, up, key, val, feat, before, after, post, ready,
    sums, zero_scr, keep, length_sem, in_sems, out_sems,
):
    me = lax.axis_index("ctx")
    base = me * rows
    count = arrived.shape[0]
    poles = (par.shape[1] // SUB - 1) // 2
    extended = rows + HALO
    padded = rows + 2 * HALO
    get_lengths = pltpu.make_async_copy(far_lengths, lengths, length_sem)
    get_lengths.start()
    far = [par_in, partial_in, conv_in, adj_in, tap_in, up_in, key_in, val_in, feat_in]
    near = [par, partial, conv, adj, tap, up, key, val, feat]
    each_group(groups, lambda half: start_all(group_copies(far, near, in_sems, half)))

    def leaving(half):
        return [
            pltpu.make_async_copy(
                ready.at[half, third],
                grads.at[
                    0, :, pl.ds(pl.multiple_of((third * groups + half) * GROUP, GROUP), GROUP)
                ],
                out_sems.at[half, third],
            )
            for third in range(3)
        ]

    zero_scr[...] = jnp.zeros((SUB, LANES), F32)
    zero = zero_scr[...]
    get_lengths.wait()
    starts = segment_starts(lengths)
    fill_keep(keep, starts, base, rows)
    until, since = jnp.int32(extended), jnp.int32(0)
    first, last, newest = jnp.int32(0), jnp.int32(2**30), jnp.int32(0)
    for start in starts:
        at = start - base
        until = jnp.where(at >= 0, jnp.minimum(until, at), until)
        since = jnp.where(at <= extended, jnp.maximum(since, at), since)
        first = jnp.where(at <= 0, jnp.maximum(first, start), first)
        last = jnp.where(at > extended, jnp.minimum(last, start), last)
        newest = jnp.where(at <= extended, jnp.maximum(newest, start), newest)
    steps = jnp.maximum(until, extended - since)
    through = flag(newest < base + rows)
    chunk = unroll_of(extended)

    def group(half):
        incoming = group_copies(far, near, in_sems, half)
        par_h, partial_h, conv_h, adj_h = par.at[half], partial.at[half], conv.at[half], adj.at[half]
        up_h, key_h, val_h, feat_h = up.at[half], key.at[half], val.at[half], feat.at[half]
        wait_all(incoming[:2])
        per_pass = poles // 2
        zeros = [zero] * per_pass
        for part in range(2):
            chosen = list(range(part * per_pass, (part + 1) * per_pass))
            rate = [jnp.exp(vec(par_h, m)) for m in chosen]
            block = [jnp.exp(-rows * r) for r in rate]

            def arrived_states(d):
                got = []
                for m in range(chosen[0], chosen[-1] + 1, 2):
                    pair = arrived[d, half, m * SUB : (m + 2) * SUB, :].astype(F32)
                    got += [pair[:SUB], pair[SUB:]]
                return got

            def from_before(d, carry):
                joined = flag((d + 1) * rows - 1 >= first)
                got = arrived_states(d)
                return [block[i] * carry[i] + joined * got[i] for i in range(per_pass)]

            def from_after(i, carry):
                d = count - 1 - i
                joined = flag(d * rows + HALO < last)
                got = arrived_states(d)
                return [block[i] * carry[i] + joined * got[i] for i in range(per_pass)]

            state = lax.fori_loop(0, me, from_before, zeros)
            adjoint = lax.fori_loop(0, count - 1 - me, from_after, zeros)
            own = arrived_states(me)
            for i, m in enumerate(chosen):
                scale = vec(par_h, poles + m) * jnp.exp(-rate[i])
                put(before, m, scale * state[i])
                put(after, m, scale * adjoint[i])
                cross = jnp.exp(-(HALO + 1) * rate[i]) * (adjoint[i] * through)
                put(sums, (9 + m) * groups + half, vec(partial_h, m) + cross * own[i])
        put(sums, (9 + poles) * groups + half, vec(partial_h, poles))
        decay = [jnp.exp(-jnp.exp(vec(par_h, m))) for m in range(poles)]
        enter = [vec(before, m) for m in range(poles)]
        leave = [vec(after, m) for m in range(poles)]
        wait_all(incoming[2:4])

        def carried(i, carry):
            enter, leave = carry
            for step in range(chunk):
                p = chunk * i + step
                back = extended - 1 - p
                put(conv_h, p, vec(conv_h, p) + flag(p < until) * total_of(enter))
                put(adj_h, back, vec(adj_h, back) + flag(back >= since) * total_of(leave))
                enter = [decay[m] * enter[m] for m in range(poles)]
                leave = [decay[m] * leave[m] for m in range(poles)]
            return enter, leave

        lax.fori_loop(0, (steps + chunk - 1) // chunk, carried, (enter, leave))
        wait_all(incoming[4:])
        taps_h = [[vec(tap.at[half], third * 3 + j) for j in range(3)] for third in range(3)]

        def posted(p):
            keep_one = keep[p + 1]
            keep_two = keep_one * keep[p]
            conv_out = rounded(vec(conv_h, p))
            grad_mixed = rounded(vec(adj_h, p))
            now = [vec(up_h, p) * conv_out, grad_mixed * vec(val_h, p), grad_mixed * vec(key_h, p)]
            return now, [keep_one * g for g in now], [keep_two * g for g in now]

        _, _, far_two = posted(extended - 1)
        _, near_one, near_two = posted(extended - 2)

        def finish(i, carry):
            one, two, three, tap_sums, feat_now, feat_one = carry
            p = rows - 1 - i
            now, masked_one, masked_two = posted(p)
            feat_two = [vec(feat_h, third * padded + p) for third in range(3)]
            new_sums = []
            for third in range(3):
                back = (
                    taps_h[third][0] * now[third]
                    + taps_h[third][1] * one[third]
                    + taps_h[third][2] * three[third]
                )
                put(post, third * rows + p, back)
                new_sums += [
                    tap_sums[3 * third] + now[third] * feat_now[third],
                    tap_sums[3 * third + 1] + masked_one[third] * feat_one[third],
                    tap_sums[3 * third + 2] + masked_two[third] * feat_two[third],
                ]
            return masked_one, masked_two, two, new_sums, feat_one, feat_two

        feat_last = [vec(feat_h, third * padded + rows + 1) for third in range(3)]
        feat_before = [vec(feat_h, third * padded + rows) for third in range(3)]
        _, _, _, tap_sums, _, _ = lax.fori_loop(
            0,
            rows,
            finish,
            (near_one, near_two, far_two, [zero] * 9, feat_last, feat_before),
            unroll=4,
        )
        for third in range(3):
            for j in range(3):
                put(sums, (3 * j + third) * groups + half, tap_sums[3 * third + j])

        def write(i, carry):
            for third in range(3):
                for j in range(SUB):
                    value = post[pl.ds((third * rows + i * 16) * SUB + j, 16, stride=SUB), :]
                    ready[
                        half, third, pl.ds(pl.multiple_of(i * 16, 16), 16), j * LANES : (j + 1) * LANES
                    ] = value.astype(BF16)
            return carry

        lax.fori_loop(0, rows // 16, write, 0)
        start_all(leaving(half))

    each_group(groups, group)
    width = groups * SUB
    same = 9 * width
    tap_sums = sums[0:same, :].astype(BF16)
    columns = (payload.shape[1] - same) // 16 - 1
    for e in range(count):
        payload[e, 0:same, :] = tap_sums
        first = same + (e * width) // count
        for j in range(columns):
            value = sums[pl.ds(first + j, 16, stride=width), :]
            payload[e, same + 16 * j : same + 16 * (j + 1), :] = value.astype(BF16)
        last = first + poles * width
        payload[e, same + 16 * columns :, :] = sums[last : last + 16, :].astype(BF16)
    each_group(groups, lambda half: wait_all(leaving(half)))


def share_kernel(parts, out):
    mine = parts[0].astype(F32)
    for k in range(1, parts.shape[0]):
        mine = mine + parts[k].astype(F32)
    out[...] = mine.astype(BF16)


def emit_kernel(groups, scale, shares, grad_taps, resid, skip, whole):
    me = lax.axis_index("ctx")
    width = groups * SUB
    poles, per_shard = resid.shape
    mine = shares[0].astype(F32)
    for k in range(1, shares.shape[0]):
        mine = mine + shares[k].astype(F32)
    whole[...] = mine * scale
    for k in range(3 * width):
        grad_taps[:, k * LANES : (k + 1) * LANES] = whole[pl.ds(k, 3, stride=3 * width), :]
    first = 9 * width
    columns = (whole.shape[0] - first) // 16 - 1
    last = first + 16 * columns
    if per_shard >= LANES:
        for j in range(columns):
            lanes = slice(j * LANES, (j + 1) * LANES)
            resid[:, lanes] = whole[first + 16 * j : first + 16 * (j + 1), :]
            skip[:, lanes] = whole[last + j : last + j + 1, :]
    else:
        per = LANES // per_shard
        rows = whole[first : first + 16, :]
        final = whole[last : last + 1, :]
        place = lax.rem(me, per)
        chosen, chosen_last = rows[:, :per_shard], final[:, :per_shard]
        for i in range(1, per):
            lanes = slice(i * per_shard, (i + 1) * per_shard)
            chosen = jnp.where(place == i, rows[:, lanes], chosen)
            chosen_last = jnp.where(place == i, final[:, lanes], chosen_last)
        resid[...] = chosen
        skip[...] = chosen_last


def swap(block, axes):
    return lax.all_to_all(block, axes, split_axis=0, concat_axis=0, tiled=True)


def per_device(features, upstream, lengths, conv_taps, residues, log_rate, skip_gain):
    rows = features.shape[1]
    channels = upstream.shape[2]
    poles = residues.shape[0]
    ctx_count = lax.axis_size("ctx")
    total = ctx_count * lax.axis_size("dp")
    per_shard = channels // ctx_count
    groups = channels // GROUP
    grad_scale = 1.0 / math.sqrt(rows * total)
    extended = rows + HALO
    padded = rows + 2 * HALO
    state_rows = poles * SUB
    limits = pltpu.CompilerParams(vmem_limit_bytes=40 * 1024 * 1024)
    hbm = pl.BlockSpec(memory_space=pltpu.HBM)
    vmem = pl.BlockSpec(memory_space=pltpu.VMEM)

    def tall(height):
        return jax.ShapeDtypeStruct((groups, height * SUB, LANES), F32)

    def near(*heights):
        return [pltpu.VMEM((groups, height * SUB, LANES), F32) for height in heights]

    def scratch(height):
        return pltpu.VMEM((height * SUB, LANES), F32)

    def sems(*shape):
        return pltpu.SemaphoreType.DMA(shape)

    keep = pltpu.SMEM((rows + 8,), F32)
    small = pltpu.SMEM(lengths.shape, jnp.int32)

    def call(kernel, name, ins, in_specs, outs, out_specs, scratch_shapes=()):
        ins = [
            pltpu.with_memory_space_constraint(x, pltpu.HBM) if spec is hbm else x
            for x, spec in zip(ins, in_specs)
        ]
        if isinstance(outs, list):
            outs = [
                pltpu.HBM(out.shape, out.dtype) if spec is hbm else out
                for out, spec in zip(outs, out_specs)
            ]
        return pl.pallas_call(
            kernel,
            out_shape=outs,
            in_specs=in_specs,
            out_specs=out_specs,
            scratch_shapes=list(scratch_shapes),
            compiler_params=limits,
            name=name,
        )(*ins)

    block = (3 * poles * tiles_of(per_shard) + 16, min(per_shard, LANES))
    span = features.shape[2]
    params, edge, head = call(
        start_kernel,
        "start",
        [log_rate, residues, skip_gain[None], features, upstream],
        [hbm] * 5,
        [
            jax.ShapeDtypeStruct((ctx_count,) + block, BF16),
            jax.ShapeDtypeStruct((HALO, span), BF16),
            jax.ShapeDtypeStruct((HALO, span + channels), BF16),
        ],
        [vmem] * 3,
        [
            pltpu.VMEM((poles, per_shard), F32),
            pltpu.VMEM((poles, per_shard), F32),
            pltpu.VMEM((1, per_shard), F32),
            pltpu.VMEM((16, span), BF16),
            pltpu.VMEM((16, span), BF16),
            pltpu.VMEM((16, channels), BF16),
            pltpu.VMEM(block, F32),
            sems(6),
        ],
    )
    params = swap(params, "ctx")
    left = shifted(edge, "ctx", 1)
    right = shifted(head, "ctx", -1)

    payload, feat, up, mixed, gout, par, tap = call(
        functools.partial(ends_kernel, rows, groups),
        "ends",
        [lengths, features, upstream, left, right, conv_taps, params],
        [hbm] * 3 + [vmem] * 4,
        [jax.ShapeDtypeStruct((ctx_count, groups, state_rows, LANES), BF16)]
        + [tall(height) for height in [3 * padded] + [extended] * 3 + [2 * poles + 1, 9]],
        [vmem] + [hbm] * 6,
        [
            small,
            pltpu.VMEM((groups, 3, rows, GROUP), BF16),
            pltpu.VMEM((groups, rows, GROUP), BF16),
        ]
        + near(3 * padded, extended, extended, extended, 2 * poles + 1, 9)
        + [pltpu.VMEM((2, state_rows, LANES), BF16)]
        + [pltpu.VMEM((block[0], LANES), F32), scratch(1), keep]
        + [sems(), sems(groups, 4), sems(groups, 6)],
    )
    arrived = swap(payload, "ctx")
    key, val, conv, adj, partial = call(
        functools.partial(local_kernel, rows, groups),
        "local",
        [lengths, feat, mixed, gout, par, tap],
        [hbm] * 6,
        [tall(extended)] * 4 + [tall(poles + 1)],
        [hbm] * 5,
        [small]
        + near(extended, extended, 2 * poles + 1, 9, 3 * padded)
        + near(extended, extended, extended, extended, poles + 1)
        + [scratch(1), keep, sems(), sems(groups, 5), sems(groups, 5)],
    )
    used = (10 + poles) * groups * SUB
    sum_rows = 9 * groups * SUB + 16 * max(1, per_shard // LANES) + 16
    grads, sums = call(
        functools.partial(finish_kernel, rows, groups),
        "finish",
        [lengths, arrived, par, partial, tap, conv, adj, up, key, val, feat],
        [hbm, vmem] + [hbm] * 9,
        [
            jax.ShapeDtypeStruct(features.shape, BF16),
            jax.ShapeDtypeStruct((ctx_count, sum_rows, LANES), BF16),
        ],
        [hbm, vmem],
        [small]
        + near(2 * poles + 1, poles + 1, 9, extended, extended, extended, extended, extended)
        + near(3 * padded)
        + [scratch(poles), scratch(poles), scratch(3 * rows)]
        + [pltpu.VMEM((groups, 3, rows, GROUP), BF16)]
        + [pltpu.VMEM((used + 16, LANES), F32), scratch(1), keep]
        + [sems(), sems(groups, 9), sems(groups, 3)],
    )

    mine = call(
        share_kernel,
        "share",
        [swap(sums, "ctx")],
        [vmem],
        jax.ShapeDtypeStruct((sum_rows, LANES), BF16),
        vmem,
    )
    grad_taps, resid, skip = call(
        functools.partial(emit_kernel, groups, grad_scale),
        "emit",
        [lax.all_gather(mine, "dp")],
        [vmem],
        [
            jax.ShapeDtypeStruct((3, 3 * channels), F32),
            jax.ShapeDtypeStruct((poles, per_shard), F32),
            jax.ShapeDtypeStruct((1, per_shard), F32),
        ],
        [vmem] * 3,
        [pltpu.VMEM((sum_rows, LANES), F32)],
    )
    return grads, grad_taps, resid, skip.reshape(per_shard)


def solution(mesh):
    return jax.shard_map(
        per_device,
        mesh=mesh,
        in_specs=(
            P("dp", "ctx", None),
            P("dp", "ctx", None),
            P("dp", None),
            P(),
            P(None, "ctx"),
            P(None, "ctx"),
            P("ctx"),
        ),
        out_specs=(P("dp", "ctx", None), P(), P(None, "ctx"), P("ctx")),
        check_vma=False,
    )
```

```python
import functools
import math

import jax
import jax.numpy as jnp
from jax import lax
from jax.experimental import pallas as pl
from jax.experimental.pallas import tpu as pltpu
from jax.sharding import PartitionSpec as P

F32 = jnp.float32
BF16 = jnp.bfloat16
LANES = 128
SUB = 8
GROUP = SUB * LANES
HALO = 2


def shifted(block, axis, distance):
    count = lax.axis_size(axis)
    route = [(i - distance, i) for i in range(count) if 0 <= i - distance < count]
    return lax.ppermute(block, axis, route)


def vec(ref, index):
    return ref[pl.ds(pl.multiple_of(index * SUB, SUB), SUB), :]


def put(ref, index, value):
    ref[pl.ds(pl.multiple_of(index * SUB, SUB), SUB), :] = value


def spread(dst, first, src, column, row_count):
    for j in range(SUB):
        lanes = pl.ds(pl.multiple_of(column + j * LANES, LANES), LANES)
        dst[pl.ds(first * SUB + j, row_count, stride=SUB), :] = src[:, lanes].astype(F32)


def spread_rows(dst, first, src, row_count):
    def step(i, carry):
        for j in range(SUB):
            value = src[pl.ds(pl.multiple_of(i * 16, 16), 16), j * LANES : (j + 1) * LANES]
            dst[pl.ds((i * 16 + first) * SUB + j, 16, stride=SUB), :] = value.astype(F32)
        return carry

    lax.fori_loop(0, row_count // 16, step, 0)


def tiles_of(width):
    return max(1, width // LANES)


def start_kernel(
    log_rate, residues, skip_gain, features, upstream, out, edge, head,
    rates, coeffs, gains, low, high, high_up, slab, sems,
):
    rows = features.shape[1]
    copies = [
        pltpu.make_async_copy(source, target, sems.at[i])
        for i, (source, target) in enumerate(
            [
                (log_rate, rates),
                (residues, coeffs),
                (skip_gain, gains),
                (features.at[0, pl.ds(0, 16), :], low),
                (features.at[0, pl.ds(rows - 16, 16), :], high),
                (upstream.at[0, pl.ds(0, 16), :], high_up),
            ]
        )
    ]
    start_all(copies)
    poles, width = rates.shape
    per = tiles_of(width)
    slab[...] = jnp.zeros(slab.shape, F32)
    wait_all(copies[:3])
    for j in range(per):
        lanes = slice(j * LANES, min(width, (j + 1) * LANES))
        rate, gain = rates[:, lanes], gains[:, lanes]
        slab[pl.ds(j, poles, stride=per), :] = rounded(rate)
        slab[pl.ds(poles * per + j, poles, stride=per), :] = rate - rounded(rate)
        slab[pl.ds(2 * poles * per + j, poles, stride=per), :] = coeffs[:, lanes]
        slab[pl.ds(3 * poles * per + j, 1), :] = rounded(gain)
        slab[pl.ds((3 * poles + 1) * per + j, 1), :] = gain - rounded(gain)
    packed = slab[...].astype(BF16)
    for e in range(out.shape[0]):
        out[e] = packed
    wait_all(copies[3:])
    span = features.shape[2]
    for at in range(0, span, GROUP):
        lanes = slice(at, at + GROUP)
        head[:, lanes] = low[:, lanes].astype(F32)[:HALO].astype(BF16)
        edge[:, lanes] = high[:, lanes].astype(F32)[16 - HALO :].astype(BF16)
    for at in range(0, upstream.shape[2], GROUP):
        lanes = slice(at, at + GROUP)
        head[:, span + at : span + at + GROUP] = high_up[:, lanes].astype(F32)[:HALO].astype(BF16)


def spread_params(dst, par, slab, half, groups, poles):
    pieces, height, width = par.shape
    many = pieces // groups
    base = half * many
    joined = LANES // width
    per = (height - 16) // (3 * poles)
    for k in range(many // joined):
        parts = [par[base + k * joined + i].astype(F32) for i in range(joined)]
        slab[...] = parts[0] if joined == 1 else jnp.concatenate(parts, axis=1)
        for j in range(per):
            to = k * per + j

            def rows_of(piece, count=poles):
                return slab[pl.ds(piece * per + j, count, stride=per), :]

            dst[pl.ds(to, poles, stride=SUB), :] = rows_of(0) + rows_of(poles)
            dst[pl.ds(poles * SUB + to, poles, stride=SUB), :] = rows_of(2 * poles)
            gain = rows_of(3 * poles, 1) + rows_of(3 * poles + 1, 1)
            dst[pl.ds(2 * poles * SUB + to, 1), :] = gain


def segment_starts(lengths):
    starts = [jnp.int32(0)]
    for j in range(lengths.shape[1]):
        starts.append(starts[-1] + lengths[0, j])
    return starts


def fill_keep(keep, starts, base, rows):
    count = rows + HALO + 2

    def step(i, carry):
        keep[i] = jnp.float32(1.0)
        return carry

    lax.fori_loop(0, count, step, 0, unroll=4)
    for start in starts:
        at = start - base + 1

        @pl.when((at >= 0) & (at < count))
        def _():
            keep[at] = jnp.float32(0.0)


def rounded(value):
    return value.astype(BF16).astype(F32)


def flag(condition):
    return jnp.where(condition, 1.0, 0.0).astype(F32)


def total_of(terms):
    terms = list(terms)
    while len(terms) > 1:
        odd = terms[-1:] if len(terms) % 2 else []
        terms = [x + y for x, y in zip(terms[::2], terms[1::2])] + odd
    return terms[0]


def unroll_of(trips):
    return max(d for d in range(1, 14) if trips % d == 0)


def featured(feat, tap, p, keep_one, keep_two):
    return (
        tap[0] * vec(feat, p + 2)
        + tap[1] * (keep_one * vec(feat, p + 1))
        + tap[2] * (keep_two * vec(feat, p))
    )


def each_group(groups, body):
    def step(half, carry):
        body(half)
        return carry

    lax.fori_loop(0, groups, step, 0)


def group_copies(sources, targets, sems, half):
    return [
        pltpu.make_async_copy(source.at[half], target.at[half], sems.at[half, i])
        for i, (source, target) in enumerate(zip(sources, targets))
    ]


def start_all(copies):
    for copy in copies:
        copy.start()


def wait_all(copies):
    for copy in copies:
        copy.wait()


def ends_kernel(
    rows, groups, far_lengths, features, upstream, left, right, taps, params,
    payload, feat_out, up_out, mixed_out, gout_out, par_out, tap_out,
    lengths, raw, raw_up, feat, up, mixed, gout, par, tap, stack, slab, zero_scr, keep,
    length_sem, in_sems, out_sems,
):
    me = lax.axis_index("ctx")
    base = me * rows
    count = payload.shape[0]
    poles = (par.shape[1] // SUB - 1) // 2
    extended = rows + HALO
    padded = rows + 2 * HALO
    get_lengths = pltpu.make_async_copy(far_lengths, lengths, length_sem)
    get_lengths.start()

    def arriving(half):
        lanes = [
            pl.ds(pl.multiple_of((third * groups + half) * GROUP, GROUP), GROUP)
            for third in range(3)
        ]
        return [
            pltpu.make_async_copy(
                features.at[0, :, lanes[third]], raw.at[half, third], in_sems.at[half, third]
            )
            for third in range(3)
        ] + [pltpu.make_async_copy(upstream.at[0, :, lanes[0]], raw_up.at[half], in_sems.at[half, 3])]

    near = [feat, up, tap, par, mixed, gout]
    far = [feat_out, up_out, tap_out, par_out, mixed_out, gout_out]

    each_group(groups, lambda half: start_all(arriving(half)))
    zero_scr[...] = jnp.zeros((SUB, LANES), F32)
    zeros = [zero_scr[...]] * poles

    def prepare(half):
        spread_params(par.at[half], params, slab, half, groups, poles)
        for third in range(3):
            column = (third * groups + half) * GROUP
            spread(feat.at[half], third * padded, left, column, HALO)
            spread(feat.at[half], third * padded + rows + HALO, right, column, HALO)
            spread(tap.at[half], third * 3, taps, column, 3)
        spread(up.at[half], rows, right, (3 * groups + half) * GROUP, HALO)

    each_group(groups, prepare)
    get_lengths.wait()
    starts = segment_starts(lengths)
    fill_keep(keep, starts, base, rows)
    low, high = jnp.int32(0), jnp.int32(extended)
    for start in starts:
        at = start - base
        low = jnp.where(at < rows, jnp.maximum(low, at), low)
        high = jnp.where(at > HALO, jnp.minimum(high, at), high)

    def group(half):
        incoming = arriving(half)
        outgoing = group_copies(near, far, out_sems, half)
        feat_h, up_h, mixed_h, gout_h = feat.at[half], up.at[half], mixed.at[half], gout.at[half]
        for third in range(3):
            incoming[third].wait()
            spread_rows(feat_h, third * padded + HALO, raw.at[half, third], rows)
        incoming[3].wait()
        spread_rows(up_h, 0, raw_up.at[half], rows)
        start_all(outgoing[:4])
        taps_h = [[vec(tap.at[half], third * 3 + j) for j in range(3)] for third in range(3)]

        def product(p, carry):
            keep_one = keep[p + 1]
            keep_two = keep_one * keep[p]
            query, key, val = (
                featured(feat_h, taps_h[third], third * padded + p, keep_one, keep_two)
                for third in range(3)
            )
            put(mixed_h, p, rounded(key * val))
            put(gout_h, p, rounded(vec(up_h, p) * query))
            return carry

        lax.fori_loop(0, extended, product, 0, unroll=unroll_of(extended))
        start_all(outgoing[4:])
        decay = [jnp.exp(-jnp.exp(vec(par.at[half], m))) for m in range(poles)]

        def sweep(i, carry):
            state, adjoint = carry
            back = extended - 1 - i
            x = vec(mixed_h, i) * flag(i >= low)
            g = vec(gout_h, back) * flag(back < high)
            state = [decay[m] * state[m] + x for m in range(poles)]
            adjoint = [decay[m] * adjoint[m] + g for m in range(poles)]
            return state, adjoint

        state, adjoint = lax.fori_loop(0, rows, sweep, (zeros, zeros), unroll=8)
        for m in range(0, poles, 2):
            at = slice(m * SUB, (m + 2) * SUB)
            stack[0, at, :] = jnp.concatenate(state[m : m + 2], axis=0).astype(BF16)
            stack[1, at, :] = jnp.concatenate(adjoint[m : m + 2], axis=0).astype(BF16)
        for e in range(count):
            payload[e, half] = stack[jnp.where(e >= me, 0, 1)]

    each_group(groups, group)
    each_group(groups, lambda half: wait_all(group_copies(near, far, out_sems, half)))


def local_kernel(
    rows, groups, far_lengths, feat_in, mixed_in, gout_in, par_in, tap_in,
    key_out, val_out, conv_out, adj_out, partial_out,
    lengths, mixed, gout, par, tap, feat, key, val, conv, adj, partial, zero_scr, keep,
    length_sem, in_sems, out_sems,
):
    poles = (par.shape[1] // SUB - 1) // 2
    extended = rows + HALO
    padded = rows + 2 * HALO
    get_lengths = pltpu.make_async_copy(far_lengths, lengths, length_sem)
    get_lengths.start()
    far_in, near_in = [par_in, tap_in, feat_in, mixed_in, gout_in], [par, tap, feat, mixed, gout]
    near_out = [key, val, conv, adj, partial]
    far_out = [key_out, val_out, conv_out, adj_out, partial_out]
    each_group(groups, lambda half: start_all(group_copies(far_in, near_in, in_sems, half)))
    zero_scr[...] = jnp.zeros((SUB, LANES), F32)
    zero = zero_scr[...]
    per_pass = poles // 4
    zeros = [zero] * per_pass
    get_lengths.wait()
    fill_keep(keep, segment_starts(lengths), lax.axis_index("ctx") * rows, rows)

    def group(half):
        incoming = group_copies(far_in, near_in, in_sems, half)
        outgoing = group_copies(near_out, far_out, out_sems, half)
        feat_h, mixed_h, gout_h, par_h = feat.at[half], mixed.at[half], gout.at[half], par.at[half]
        conv_h, adj_h, key_h, val_h = conv.at[half], adj.at[half], key.at[half], val.at[half]
        wait_all(incoming)
        taps_h = [[vec(tap.at[half], third * 3 + j) for j in range(3)] for third in range(3)]

        def product(p, carry):
            keep_one = keep[p + 1]
            keep_two = keep_one * keep[p]
            put(key_h, p, featured(feat_h, taps_h[1], padded + p, keep_one, keep_two))
            put(val_h, p, featured(feat_h, taps_h[2], 2 * padded + p, keep_one, keep_two))
            return carry

        lax.fori_loop(0, extended, product, 0, unroll=unroll_of(extended))
        start_all(outgoing[:2])
        gain = vec(par_h, 2 * poles)
        for part in range(poles // per_pass):
            chosen = list(range(part * per_pass, (part + 1) * per_pass))
            decay = [jnp.exp(-jnp.exp(vec(par_h, m))) for m in chosen]
            coeff = [vec(par_h, poles + m) for m in chosen]

            def sweep(i, carry):
                state, adjoint, resid, skip = carry
                back = extended - 1 - i
                x = vec(mixed_h, i)
                g = vec(gout_h, back)
                own = vec(mixed_h, back) * flag(back < rows)
                keep_fwd = keep[i + 1]
                keep_bwd = keep[back + 2]
                state = [decay[m] * (state[m] * keep_fwd) + x for m in range(per_pass)]
                adjoint = [decay[m] * (adjoint[m] * keep_bwd) + g for m in range(per_pass)]
                resid = [resid[m] + own * adjoint[m] for m in range(per_pass)]
                forward = total_of(coeff[m] * state[m] for m in range(per_pass))
                backward = total_of(coeff[m] * adjoint[m] for m in range(per_pass))
                if part == 0:
                    put(conv_h, i, forward + gain * x)
                    put(adj_h, back, backward + gain * g)
                    skip = skip + own * g
                else:
                    put(conv_h, i, forward + vec(conv_h, i))
                    put(adj_h, back, backward + vec(adj_h, back))
                return state, adjoint, resid, skip

            _, _, resid, skip = lax.fori_loop(
                0, extended, sweep, (zeros, zeros, zeros, zero), unroll=unroll_of(extended)
            )
            for i, m in enumerate(chosen):
                put(partial.at[half], m, resid[i])
            if part == 0:
                put(partial.at[half], poles, skip)
        start_all(outgoing[2:])

    each_group(groups, group)
    each_group(groups, lambda half: wait_all(group_copies(near_out, far_out, out_sems, half)))


def posted_rows(keep, conv, adj, up, key, val):
    def posted(p):
        keep_one = keep[p + 1]
        keep_two = keep_one * keep[p]
        conv_out = rounded(vec(conv, p))
        grad_mixed = rounded(vec(adj, p))
        now = [vec(up, p) * conv_out, grad_mixed * vec(val, p), grad_mixed * vec(key, p)]
        return now, [keep_one * g for g in now], [keep_two * g for g in now]

    return posted


def sums_kernel(
    rows, groups, far_lengths, arrived, par_in, partial_in, conv_in, adj_in, up_in, key_in, val_in,
    feat_in, conv_out, adj_out, payload,
    lengths, par, partial, conv, adj, up, key, val, feat, before, after, sums, zero_scr, keep,
    length_sem, in_sems, out_sems,
):
    me = lax.axis_index("ctx")
    base = me * rows
    count = arrived.shape[0]
    poles = (par.shape[1] // SUB - 1) // 2
    extended = rows + HALO
    padded = rows + 2 * HALO
    get_lengths = pltpu.make_async_copy(far_lengths, lengths, length_sem)
    get_lengths.start()
    far = [par_in, partial_in, conv_in, adj_in, up_in, key_in, val_in, feat_in]
    near = [par, partial, conv, adj, up, key, val, feat]
    each_group(groups, lambda half: start_all(group_copies(far, near, in_sems, half)))
    zero_scr[...] = jnp.zeros((SUB, LANES), F32)
    zero = zero_scr[...]
    get_lengths.wait()
    starts = segment_starts(lengths)
    fill_keep(keep, starts, base, rows)
    until, since = jnp.int32(extended), jnp.int32(0)
    first, last, newest = jnp.int32(0), jnp.int32(2**30), jnp.int32(0)
    for start in starts:
        at = start - base
        until = jnp.where(at >= 0, jnp.minimum(until, at), until)
        since = jnp.where(at <= extended, jnp.maximum(since, at), since)
        first = jnp.where(at <= 0, jnp.maximum(first, start), first)
        last = jnp.where(at > extended, jnp.minimum(last, start), last)
        newest = jnp.where(at <= extended, jnp.maximum(newest, start), newest)
    steps = jnp.maximum(until, extended - since)
    through = flag(newest < base + rows)
    chunk = unroll_of(extended)

    def group(half):
        incoming = group_copies(far, near, in_sems, half)
        outgoing = group_copies([conv, adj], [conv_out, adj_out], out_sems, half)
        par_h, partial_h, conv_h, adj_h = par.at[half], partial.at[half], conv.at[half], adj.at[half]
        feat_h = feat.at[half]
        wait_all(incoming[:2])
        per_pass = poles // 2
        zeros = [zero] * per_pass
        for part in range(2):
            chosen = list(range(part * per_pass, (part + 1) * per_pass))
            rate = [jnp.exp(vec(par_h, m)) for m in chosen]
            block = [jnp.exp(-rows * r) for r in rate]

            def arrived_states(d):
                got = []
                for m in range(chosen[0], chosen[-1] + 1, 2):
                    pair = arrived[d, half, m * SUB : (m + 2) * SUB, :].astype(F32)
                    got += [pair[:SUB], pair[SUB:]]
                return got

            def from_before(d, carry):
                joined = flag((d + 1) * rows - 1 >= first)
                got = arrived_states(d)
                return [block[i] * carry[i] + joined * got[i] for i in range(per_pass)]

            def from_after(i, carry):
                d = count - 1 - i
                joined = flag(d * rows + HALO < last)
                got = arrived_states(d)
                return [block[i] * carry[i] + joined * got[i] for i in range(per_pass)]

            state = lax.fori_loop(0, me, from_before, zeros)
            adjoint = lax.fori_loop(0, count - 1 - me, from_after, zeros)
            own = arrived_states(me)
            for i, m in enumerate(chosen):
                scale = vec(par_h, poles + m) * jnp.exp(-rate[i])
                put(before, m, scale * state[i])
                put(after, m, scale * adjoint[i])
                cross = jnp.exp(-(HALO + 1) * rate[i]) * (adjoint[i] * through)
                put(sums, (9 + m) * groups + half, vec(partial_h, m) + cross * own[i])
        put(sums, (9 + poles) * groups + half, vec(partial_h, poles))
        decay = [jnp.exp(-jnp.exp(vec(par_h, m))) for m in range(poles)]
        enter = [vec(before, m) for m in range(poles)]
        leave = [vec(after, m) for m in range(poles)]
        wait_all(incoming[2:4])

        def carried(i, carry):
            enter, leave = carry
            for step in range(chunk):
                p = chunk * i + step
                back = extended - 1 - p
                put(conv_h, p, vec(conv_h, p) + flag(p < until) * total_of(enter))
                put(adj_h, back, vec(adj_h, back) + flag(back >= since) * total_of(leave))
                enter = [decay[m] * enter[m] for m in range(poles)]
                leave = [decay[m] * leave[m] for m in range(poles)]
            return enter, leave

        lax.fori_loop(0, (steps + chunk - 1) // chunk, carried, (enter, leave))
        start_all(outgoing)
        wait_all(incoming[4:])
        posted = posted_rows(keep, conv_h, adj_h, up.at[half], key.at[half], val.at[half])

        def tap_terms(i, carry):
            tap_sums, feat_now, feat_one = carry
            p = rows - 1 - i
            now, masked_one, masked_two = posted(p)
            feat_two = [vec(feat_h, third * padded + p) for third in range(3)]
            new_sums = []
            for third in range(3):
                new_sums += [
                    tap_sums[3 * third] + now[third] * feat_now[third],
                    tap_sums[3 * third + 1] + masked_one[third] * feat_one[third],
                    tap_sums[3 * third + 2] + masked_two[third] * feat_two[third],
                ]
            return new_sums, feat_one, feat_two

        feat_last = [vec(feat_h, third * padded + rows + 1) for third in range(3)]
        feat_before = [vec(feat_h, third * padded + rows) for third in range(3)]
        tap_sums, _, _ = lax.fori_loop(
            0, rows, tap_terms, ([zero] * 9, feat_last, feat_before), unroll=4
        )
        for third in range(3):
            for j in range(3):
                put(sums, (3 * j + third) * groups + half, tap_sums[3 * third + j])

    each_group(groups, group)
    width = groups * SUB
    same = 9 * width
    tap_sums = sums[0:same, :].astype(BF16)
    columns = (payload.shape[1] - same) // 16 - 1
    for e in range(count):
        payload[e, 0:same, :] = tap_sums
        first_row = same + (e * width) // count
        for j in range(columns):
            value = sums[pl.ds(first_row + j, 16, stride=width), :]
            payload[e, same + 16 * j : same + 16 * (j + 1), :] = value.astype(BF16)
        last_row = first_row + poles * width
        payload[e, same + 16 * columns :, :] = sums[last_row : last_row + 16, :].astype(BF16)
    each_group(
        groups,
        lambda half: wait_all(group_copies([conv, adj], [conv_out, adj_out], out_sems, half)),
    )


def grads_kernel(
    rows, groups, far_lengths, tap_in, conv_in, adj_in, up_in, key_in, val_in, grads,
    lengths, tap, conv, adj, up, key, val, post, ready, keep, length_sem, in_sems, out_sems,
):
    extended = rows + HALO
    get_lengths = pltpu.make_async_copy(far_lengths, lengths, length_sem)
    get_lengths.start()
    far = [tap_in, conv_in, adj_in, up_in, key_in, val_in]
    near = [tap, conv, adj, up, key, val]
    each_group(groups, lambda half: start_all(group_copies(far, near, in_sems, half)))

    def leaving(half):
        return [
            pltpu.make_async_copy(
                ready.at[half, third],
                grads.at[
                    0, :, pl.ds(pl.multiple_of((third * groups + half) * GROUP, GROUP), GROUP)
                ],
                out_sems.at[half, third],
            )
            for third in range(3)
        ]

    get_lengths.wait()
    fill_keep(keep, segment_starts(lengths), lax.axis_index("ctx") * rows, rows)

    def group(half):
        wait_all(group_copies(far, near, in_sems, half))
        taps_h = [[vec(tap.at[half], third * 3 + j) for j in range(3)] for third in range(3)]
        posted = posted_rows(
            keep, conv.at[half], adj.at[half], up.at[half], key.at[half], val.at[half]
        )
        _, _, far_two = posted(extended - 1)
        _, near_one, near_two = posted(extended - 2)

        def transposed(i, carry):
            one, two, three = carry
            p = rows - 1 - i
            now, masked_one, masked_two = posted(p)
            for third in range(3):
                back = (
                    taps_h[third][0] * now[third]
                    + taps_h[third][1] * one[third]
                    + taps_h[third][2] * three[third]
                )
                put(post, third * rows + p, back)
            return masked_one, masked_two, two

        lax.fori_loop(0, rows, transposed, (near_one, near_two, far_two), unroll=4)

        def write(i, carry):
            for third in range(3):
                for j in range(SUB):
                    value = post[pl.ds((third * rows + i * 16) * SUB + j, 16, stride=SUB), :]
                    lanes = slice(j * LANES, (j + 1) * LANES)
                    ready[half, third, pl.ds(pl.multiple_of(i * 16, 16), 16), lanes] = value.astype(
                        BF16
                    )
            return carry

        lax.fori_loop(0, rows // 16, write, 0, unroll=2)
        start_all(leaving(half))

    each_group(groups, group)
    each_group(groups, lambda half: wait_all(leaving(half)))


def share_kernel(parts, out):
    mine = parts[0].astype(F32)
    for k in range(1, parts.shape[0]):
        mine = mine + parts[k].astype(F32)
    out[...] = mine.astype(BF16)


def emit_kernel(groups, scale, shares, grad_taps, resid, skip, whole):
    me = lax.axis_index("ctx")
    width = groups * SUB
    poles, per_shard = resid.shape
    mine = shares[0].astype(F32)
    for k in range(1, shares.shape[0]):
        mine = mine + shares[k].astype(F32)
    whole[...] = mine * scale
    for k in range(3 * width):
        grad_taps[:, k * LANES : (k + 1) * LANES] = whole[pl.ds(k, 3, stride=3 * width), :]
    first = 9 * width
    columns = (whole.shape[0] - first) // 16 - 1
    last = first + 16 * columns
    if per_shard >= LANES:
        for j in range(columns):
            lanes = slice(j * LANES, (j + 1) * LANES)
            resid[:, lanes] = whole[first + 16 * j : first + 16 * (j + 1), :]
            skip[:, lanes] = whole[last + j : last + j + 1, :]
    else:
        per = LANES // per_shard
        rows = whole[first : first + 16, :]
        final = whole[last : last + 1, :]
        place = lax.rem(me, per)
        chosen, chosen_last = rows[:, :per_shard], final[:, :per_shard]
        for i in range(1, per):
            lanes = slice(i * per_shard, (i + 1) * per_shard)
            chosen = jnp.where(place == i, rows[:, lanes], chosen)
            chosen_last = jnp.where(place == i, final[:, lanes], chosen_last)
        resid[...] = chosen
        skip[...] = chosen_last


def swap(block, axes):
    return lax.all_to_all(block, axes, split_axis=0, concat_axis=0, tiled=True)


def per_device(features, upstream, lengths, conv_taps, residues, log_rate, skip_gain):
    rows = features.shape[1]
    channels = upstream.shape[2]
    poles = residues.shape[0]
    ctx_count = lax.axis_size("ctx")
    total = ctx_count * lax.axis_size("dp")
    per_shard = channels // ctx_count
    groups = channels // GROUP
    grad_scale = 1.0 / math.sqrt(rows * total)
    extended = rows + HALO
    padded = rows + 2 * HALO
    state_rows = poles * SUB
    limits = pltpu.CompilerParams(vmem_limit_bytes=40 * 1024 * 1024)
    hbm = pl.BlockSpec(memory_space=pltpu.HBM)
    vmem = pl.BlockSpec(memory_space=pltpu.VMEM)

    def tall(height):
        return jax.ShapeDtypeStruct((groups, height * SUB, LANES), F32)

    def near(*heights):
        return [pltpu.VMEM((groups, height * SUB, LANES), F32) for height in heights]

    def scratch(height):
        return pltpu.VMEM((height * SUB, LANES), F32)

    def sems(*shape):
        return pltpu.SemaphoreType.DMA(shape)

    keep = pltpu.SMEM((rows + 8,), F32)
    small = pltpu.SMEM(lengths.shape, jnp.int32)

    def call(kernel, name, ins, in_specs, outs, out_specs, scratch_shapes=()):
        ins = [
            pltpu.with_memory_space_constraint(x, pltpu.HBM) if spec is hbm else x
            for x, spec in zip(ins, in_specs)
        ]
        if isinstance(outs, list):
            outs = [
                pltpu.HBM(out.shape, out.dtype) if spec is hbm else out
                for out, spec in zip(outs, out_specs)
            ]
        return pl.pallas_call(
            kernel,
            out_shape=outs,
            in_specs=in_specs,
            out_specs=out_specs,
            scratch_shapes=list(scratch_shapes),
            compiler_params=limits,
            name=name,
        )(*ins)

    block = (3 * poles * tiles_of(per_shard) + 16, min(per_shard, LANES))
    span = features.shape[2]
    params, edge, head = call(
        start_kernel,
        "start",
        [log_rate, residues, skip_gain[None], features, upstream],
        [hbm] * 5,
        [
            jax.ShapeDtypeStruct((ctx_count,) + block, BF16),
            jax.ShapeDtypeStruct((HALO, span), BF16),
            jax.ShapeDtypeStruct((HALO, span + channels), BF16),
        ],
        [vmem] * 3,
        [
            pltpu.VMEM((poles, per_shard), F32),
            pltpu.VMEM((poles, per_shard), F32),
            pltpu.VMEM((1, per_shard), F32),
            pltpu.VMEM((16, span), BF16),
            pltpu.VMEM((16, span), BF16),
            pltpu.VMEM((16, channels), BF16),
            pltpu.VMEM(block, F32),
            sems(6),
        ],
    )
    params = swap(params, "ctx")
    left = shifted(edge, "ctx", 1)
    right = shifted(head, "ctx", -1)

    payload, feat, up, mixed, gout, par, tap = call(
        functools.partial(ends_kernel, rows, groups),
        "ends",
        [lengths, features, upstream, left, right, conv_taps, params],
        [hbm] * 3 + [vmem] * 4,
        [jax.ShapeDtypeStruct((ctx_count, groups, state_rows, LANES), BF16)]
        + [tall(height) for height in [3 * padded] + [extended] * 3 + [2 * poles + 1, 9]],
        [vmem] + [hbm] * 6,
        [
            small,
            pltpu.VMEM((groups, 3, rows, GROUP), BF16),
            pltpu.VMEM((groups, rows, GROUP), BF16),
        ]
        + near(3 * padded, extended, extended, extended, 2 * poles + 1, 9)
        + [pltpu.VMEM((2, state_rows, LANES), BF16)]
        + [pltpu.VMEM((block[0], LANES), F32), scratch(1), keep]
        + [sems(), sems(groups, 4), sems(groups, 6)],
    )
    arrived = swap(payload, "ctx")
    key, val, conv, adj, partial = call(
        functools.partial(local_kernel, rows, groups),
        "local",
        [lengths, feat, mixed, gout, par, tap],
        [hbm] * 6,
        [tall(extended)] * 4 + [tall(poles + 1)],
        [hbm] * 5,
        [small]
        + near(extended, extended, 2 * poles + 1, 9, 3 * padded)
        + near(extended, extended, extended, extended, poles + 1)
        + [scratch(1), keep, sems(), sems(groups, 5), sems(groups, 5)],
    )
    used = (10 + poles) * groups * SUB
    sum_rows = 9 * groups * SUB + 16 * max(1, per_shard // LANES) + 16
    conv, adj, sums = call(
        functools.partial(sums_kernel, rows, groups),
        "sums",
        [lengths, arrived, par, partial, conv, adj, up, key, val, feat],
        [hbm, vmem] + [hbm] * 8,
        [tall(extended)] * 2 + [jax.ShapeDtypeStruct((ctx_count, sum_rows, LANES), BF16)],
        [hbm, hbm, vmem],
        [small]
        + near(2 * poles + 1, poles + 1, extended, extended, extended, extended, extended)
        + near(3 * padded)
        + [scratch(poles), scratch(poles)]
        + [pltpu.VMEM((used + 16, LANES), F32), scratch(1), keep]
        + [sems(), sems(groups, 8), sems(groups, 2)],
    )
    parts = swap(sums, "ctx")
    (grads,) = call(
        functools.partial(grads_kernel, rows, groups),
        "grads",
        [lengths, tap, conv, adj, up, key, val],
        [hbm] * 7,
        [jax.ShapeDtypeStruct(features.shape, BF16)],
        [hbm],
        [small]
        + near(9, extended, extended, extended, extended, extended)
        + [scratch(3 * rows), pltpu.VMEM((groups, 3, rows, GROUP), BF16), keep]
        + [sems(), sems(groups, 6), sems(groups, 3)],
    )
    mine = call(
        share_kernel,
        "share",
        [parts],
        [vmem],
        jax.ShapeDtypeStruct((sum_rows, LANES), BF16),
        vmem,
    )
    grad_taps, resid, skip = call(
        functools.partial(emit_kernel, groups, grad_scale),
        "emit",
        [lax.all_gather(mine, "dp")],
        [vmem],
        [
            jax.ShapeDtypeStruct((3, 3 * channels), F32),
            jax.ShapeDtypeStruct((poles, per_shard), F32),
            jax.ShapeDtypeStruct((1, per_shard), F32),
        ],
        [vmem] * 3,
        [pltpu.VMEM((sum_rows, LANES), F32)],
    )
    return grads, grad_taps, resid, skip.reshape(per_shard)


def solution(mesh):
    return jax.shard_map(
        per_device,
        mesh=mesh,
        in_specs=(
            P("dp", "ctx", None),
            P("dp", "ctx", None),
            P("dp", None),
            P(),
            P(None, "ctx"),
            P(None, "ctx"),
            P("ctx"),
        ),
        out_specs=(P("dp", "ctx", None), P(), P(None, "ctx"), P("ctx")),
        check_vma=False,
    )
```

```python
import functools
import math

import jax
import jax.numpy as jnp
from jax import lax
from jax.experimental import pallas as pl
from jax.experimental.pallas import tpu as pltpu
from jax.sharding import PartitionSpec as P

F32 = jnp.float32
BF16 = jnp.bfloat16
LANES = 128
SUB = 8
GROUP = SUB * LANES
HALO = 2


def shifted(block, axis, distance):
    count = lax.axis_size(axis)
    route = [(i - distance, i) for i in range(count) if 0 <= i - distance < count]
    return lax.ppermute(block, axis, route)


def vec(ref, index):
    return ref[pl.ds(pl.multiple_of(index * SUB, SUB), SUB), :]


def put(ref, index, value):
    ref[pl.ds(pl.multiple_of(index * SUB, SUB), SUB), :] = value


def spread(dst, first, src, column, row_count):
    for j in range(SUB):
        lanes = pl.ds(pl.multiple_of(column + j * LANES, LANES), LANES)
        dst[pl.ds(first * SUB + j, row_count, stride=SUB), :] = src[:, lanes].astype(F32)


def spread_rows(dst, first, src, row_count):
    def step(i, carry):
        for j in range(SUB):
            value = src[pl.ds(pl.multiple_of(i * 16, 16), 16), j * LANES : (j + 1) * LANES]
            dst[pl.ds((i * 16 + first) * SUB + j, 16, stride=SUB), :] = value.astype(F32)
        return carry

    lax.fori_loop(0, row_count // 16, step, 0)


def tiles_of(width):
    return max(1, width // LANES)


def start_kernel(
    log_rate, residues, skip_gain, features, upstream, out, edge, head,
    rates, coeffs, gains, low, high, high_up, slab, sems,
):
    rows = features.shape[1]
    copies = [
        pltpu.make_async_copy(source, target, sems.at[i])
        for i, (source, target) in enumerate(
            [
                (log_rate, rates),
                (residues, coeffs),
                (skip_gain, gains),
                (features.at[0, pl.ds(0, 16), :], low),
                (features.at[0, pl.ds(rows - 16, 16), :], high),
                (upstream.at[0, pl.ds(0, 16), :], high_up),
            ]
        )
    ]
    start_all(copies)
    width = rates.shape[1]
    members = lax.axis_size("dp")
    poles = rates.shape[0] // members

    def mine(ref, lanes):
        value = ref[0:poles, lanes]
        for member in range(1, members):
            other = ref[member * poles : (member + 1) * poles, lanes]
            value = jnp.where(lax.axis_index("dp") == member, other, value)
        return value

    per = tiles_of(width)
    slab[...] = jnp.zeros(slab.shape, F32)
    wait_all(copies[:3])
    for j in range(per):
        lanes = slice(j * LANES, min(width, (j + 1) * LANES))
        rate, gain = mine(rates, lanes), gains[:, lanes]
        slab[pl.ds(j, poles, stride=per), :] = rounded(rate)
        slab[pl.ds(poles * per + j, poles, stride=per), :] = rate - rounded(rate)
        slab[pl.ds(2 * poles * per + j, poles, stride=per), :] = mine(coeffs, lanes)
        slab[pl.ds(3 * poles * per + j, 1), :] = rounded(gain)
        slab[pl.ds((3 * poles + 1) * per + j, 1), :] = gain - rounded(gain)
    packed = slab[...].astype(BF16)
    for e in range(out.shape[0]):
        out[e] = packed
    wait_all(copies[3:])
    span = features.shape[2]
    for at in range(0, span, GROUP):
        lanes = slice(at, at + GROUP)
        head[:, lanes] = low[:, lanes].astype(F32)[:HALO].astype(BF16)
        edge[:, lanes] = high[:, lanes].astype(F32)[16 - HALO :].astype(BF16)
    for at in range(0, upstream.shape[2], GROUP):
        lanes = slice(at, at + GROUP)
        head[:, span + at : span + at + GROUP] = high_up[:, lanes].astype(F32)[:HALO].astype(BF16)


def spread_params(dst, par, slab, half, groups, poles):
    members = lax.axis_size("dp")
    pieces = par.shape[0] // members
    width = par.shape[2]
    share = poles // members
    many = pieces // groups
    joined = LANES // width
    per = SUB * joined // many
    for member in range(members):
        base = member * pieces + half * many
        for k in range(many // joined):
            parts = [par[base + k * joined + i].astype(F32) for i in range(joined)]
            slab[...] = parts[0] if joined == 1 else jnp.concatenate(parts, axis=1)
            for j in range(per):

                def rows_of(piece, count):
                    return slab[pl.ds(piece * per + j, count, stride=per), :]

                first = member * share * SUB + k * per + j
                rates = rows_of(0, share) + rows_of(share, share)
                dst[pl.ds(first, share, stride=SUB), :] = rates
                dst[pl.ds(poles * SUB + first, share, stride=SUB), :] = rows_of(2 * share, share)
                if member == 0:
                    gain = rows_of(3 * share, 1) + rows_of(3 * share + 1, 1)
                    dst[pl.ds(2 * poles * SUB + k * per + j, 1), :] = gain


def segment_starts(lengths):
    starts = [jnp.int32(0)]
    for j in range(lengths.shape[1]):
        starts.append(starts[-1] + lengths[0, j])
    return starts


def fill_keep(keep, starts, base, rows):
    count = rows + HALO + 2

    def step(i, carry):
        keep[i] = jnp.float32(1.0)
        return carry

    lax.fori_loop(0, count, step, 0, unroll=4)
    for start in starts:
        at = start - base + 1

        @pl.when((at >= 0) & (at < count))
        def _():
            keep[at] = jnp.float32(0.0)


def rounded(value):
    return value.astype(BF16).astype(F32)


def flag(condition):
    return jnp.where(condition, 1.0, 0.0).astype(F32)


def total_of(terms):
    terms = list(terms)
    while len(terms) > 1:
        odd = terms[-1:] if len(terms) % 2 else []
        terms = [x + y for x, y in zip(terms[::2], terms[1::2])] + odd
    return terms[0]


def unroll_of(trips):
    return max(d for d in range(1, 14) if trips % d == 0)


def featured(feat, tap, p, keep_one, keep_two):
    return (
        tap[0] * vec(feat, p + 2)
        + tap[1] * (keep_one * vec(feat, p + 1))
        + tap[2] * (keep_two * vec(feat, p))
    )


def each_group(groups, body):
    def step(half, carry):
        body(half)
        return carry

    lax.fori_loop(0, groups, step, 0)


def group_copies(sources, targets, sems, half):
    return [
        pltpu.make_async_copy(source.at[half], target.at[half], sems.at[half, i])
        for i, (source, target) in enumerate(zip(sources, targets))
    ]


def start_all(copies):
    for copy in copies:
        copy.start()


def wait_all(copies):
    for copy in copies:
        copy.wait()


def ends_kernel(
    rows, groups, far_lengths, features, upstream, left, right, taps, params,
    payload, feat_out, up_out, mixed_out, gout_out, par_out, tap_out,
    lengths, raw, raw_up, feat, up, mixed, gout, par, tap, stack, slab, zero_scr, keep,
    length_sem, in_sems, out_sems,
):
    me = lax.axis_index("ctx")
    base = me * rows
    count = payload.shape[0]
    poles = (par.shape[1] // SUB - 1) // 2
    extended = rows + HALO
    padded = rows + 2 * HALO
    get_lengths = pltpu.make_async_copy(far_lengths, lengths, length_sem)
    get_lengths.start()

    def arriving(half):
        lanes = [
            pl.ds(pl.multiple_of((third * groups + half) * GROUP, GROUP), GROUP)
            for third in range(3)
        ]
        return [
            pltpu.make_async_copy(
                features.at[0, :, lanes[third]], raw.at[half, third], in_sems.at[half, third]
            )
            for third in range(3)
        ] + [pltpu.make_async_copy(upstream.at[0, :, lanes[0]], raw_up.at[half], in_sems.at[half, 3])]

    near = [feat, up, tap, par, mixed, gout]
    far = [feat_out, up_out, tap_out, par_out, mixed_out, gout_out]

    each_group(groups, lambda half: start_all(arriving(half)))
    zero_scr[...] = jnp.zeros((SUB, LANES), F32)
    zeros = [zero_scr[...]] * poles

    def prepare(half):
        spread_params(par.at[half], params, slab, half, groups, poles)
        for third in range(3):
            column = (third * groups + half) * GROUP
            spread(feat.at[half], third * padded, left, column, HALO)
            spread(feat.at[half], third * padded + rows + HALO, right, column, HALO)
            spread(tap.at[half], third * 3, taps, column, 3)
        spread(up.at[half], rows, right, (3 * groups + half) * GROUP, HALO)

    each_group(groups, prepare)
    get_lengths.wait()
    starts = segment_starts(lengths)
    fill_keep(keep, starts, base, rows)
    low, high = jnp.int32(0), jnp.int32(extended)
    for start in starts:
        at = start - base
        low = jnp.where(at < rows, jnp.maximum(low, at), low)
        high = jnp.where(at > HALO, jnp.minimum(high, at), high)

    def group(half):
        incoming = arriving(half)
        outgoing = group_copies(near, far, out_sems, half)
        feat_h, up_h, mixed_h, gout_h = feat.at[half], up.at[half], mixed.at[half], gout.at[half]
        for third in range(3):
            incoming[third].wait()
            spread_rows(feat_h, third * padded + HALO, raw.at[half, third], rows)
        incoming[3].wait()
        spread_rows(up_h, 0, raw_up.at[half], rows)
        start_all(outgoing[:4])
        taps_h = [[vec(tap.at[half], third * 3 + j) for j in range(3)] for third in range(3)]

        def product(p, carry):
            keep_one = keep[p + 1]
            keep_two = keep_one * keep[p]
            query, key, val = (
                featured(feat_h, taps_h[third], third * padded + p, keep_one, keep_two)
                for third in range(3)
            )
            put(mixed_h, p, rounded(key * val))
            put(gout_h, p, rounded(vec(up_h, p) * query))
            return carry

        lax.fori_loop(0, extended, product, 0, unroll=unroll_of(extended))
        start_all(outgoing[4:])
        decay = [jnp.exp(-jnp.exp(vec(par.at[half], m))) for m in range(poles)]

        def sweep(i, carry):
            state, adjoint = carry
            back = extended - 1 - i
            x = vec(mixed_h, i) * flag(i >= low)
            g = vec(gout_h, back) * flag(back < high)
            state = [decay[m] * state[m] + x for m in range(poles)]
            adjoint = [decay[m] * adjoint[m] + g for m in range(poles)]
            return state, adjoint

        state, adjoint = lax.fori_loop(0, rows, sweep, (zeros, zeros), unroll=8)
        for m in range(0, poles, 2):
            at = slice(m * SUB, (m + 2) * SUB)
            stack[0, at, :] = jnp.concatenate(state[m : m + 2], axis=0).astype(BF16)
            stack[1, at, :] = jnp.concatenate(adjoint[m : m + 2], axis=0).astype(BF16)
        for e in range(count):
            payload[e, half] = stack[jnp.where(e >= me, 0, 1)]

    each_group(groups, group)
    each_group(groups, lambda half: wait_all(group_copies(near, far, out_sems, half)))


def local_kernel(
    rows, groups, far_lengths, feat_in, mixed_in, gout_in, par_in, tap_in,
    key_out, val_out, conv_out, adj_out, partial_out,
    lengths, mixed, gout, par, tap, feat, key, val, conv, adj, partial, zero_scr, keep,
    length_sem, in_sems, out_sems,
):
    poles = (par.shape[1] // SUB - 1) // 2
    extended = rows + HALO
    padded = rows + 2 * HALO
    get_lengths = pltpu.make_async_copy(far_lengths, lengths, length_sem)
    get_lengths.start()
    far_in, near_in = [par_in, tap_in, feat_in, mixed_in, gout_in], [par, tap, feat, mixed, gout]
    near_out = [key, val, conv, adj, partial]
    far_out = [key_out, val_out, conv_out, adj_out, partial_out]
    each_group(groups, lambda half: start_all(group_copies(far_in, near_in, in_sems, half)))
    zero_scr[...] = jnp.zeros((SUB, LANES), F32)
    zero = zero_scr[...]
    per_pass = poles // 4
    zeros = [zero] * per_pass
    get_lengths.wait()
    fill_keep(keep, segment_starts(lengths), lax.axis_index("ctx") * rows, rows)

    def group(half):
        incoming = group_copies(far_in, near_in, in_sems, half)
        outgoing = group_copies(near_out, far_out, out_sems, half)
        feat_h, mixed_h, gout_h, par_h = feat.at[half], mixed.at[half], gout.at[half], par.at[half]
        conv_h, adj_h, key_h, val_h = conv.at[half], adj.at[half], key.at[half], val.at[half]
        wait_all(incoming)
        taps_h = [[vec(tap.at[half], third * 3 + j) for j in range(3)] for third in range(3)]

        def product(p, carry):
            keep_one = keep[p + 1]
            keep_two = keep_one * keep[p]
            put(key_h, p, featured(feat_h, taps_h[1], padded + p, keep_one, keep_two))
            put(val_h, p, featured(feat_h, taps_h[2], 2 * padded + p, keep_one, keep_two))
            return carry

        lax.fori_loop(0, extended, product, 0, unroll=unroll_of(extended))
        start_all(outgoing[:2])
        gain = vec(par_h, 2 * poles)
        for part in range(poles // per_pass):
            chosen = list(range(part * per_pass, (part + 1) * per_pass))
            decay = [jnp.exp(-jnp.exp(vec(par_h, m))) for m in chosen]
            coeff = [vec(par_h, poles + m) for m in chosen]

            def sweep(i, carry, inside=True):
                state, adjoint, resid, skip = carry
                back = extended - 1 - i
                x = vec(mixed_h, i)
                g = vec(gout_h, back)
                keep_fwd = keep[i + 1]
                keep_bwd = keep[back + 2]
                state = [decay[m] * (state[m] * keep_fwd) + x for m in range(per_pass)]
                adjoint = [decay[m] * (adjoint[m] * keep_bwd) + g for m in range(per_pass)]
                forward = total_of(coeff[m] * state[m] for m in range(per_pass))
                backward = total_of(coeff[m] * adjoint[m] for m in range(per_pass))
                if inside:
                    own = vec(mixed_h, back)
                    resid = [resid[m] + own * adjoint[m] for m in range(per_pass)]
                if part == 0:
                    put(conv_h, i, forward + gain * x)
                    put(adj_h, back, backward + gain * g)
                    if inside:
                        skip = skip + own * g
                else:
                    put(conv_h, i, forward + vec(conv_h, i))
                    put(adj_h, back, backward + vec(adj_h, back))
                return state, adjoint, resid, skip

            carry = (zeros, zeros, zeros, zero)
            for i in range(HALO):
                carry = sweep(i, carry, inside=False)
            _, _, resid, skip = lax.fori_loop(HALO, extended, sweep, carry, unroll=16)
            for i, m in enumerate(chosen):
                put(partial.at[half], m, resid[i])
            if part == 0:
                put(partial.at[half], poles, skip)
        start_all(outgoing[2:])

    each_group(groups, group)
    each_group(groups, lambda half: wait_all(group_copies(near_out, far_out, out_sems, half)))


def posted_rows(keep, conv, adj, up, key, val):
    def posted(p):
        keep_one = keep[p + 1]
        keep_two = keep_one * keep[p]
        conv_out = rounded(vec(conv, p))
        grad_mixed = rounded(vec(adj, p))
        now = [vec(up, p) * conv_out, grad_mixed * vec(val, p), grad_mixed * vec(key, p)]
        return now, [keep_one * g for g in now], [keep_two * g for g in now]

    return posted


def sums_kernel(
    rows, groups, far_lengths, arrived, par_in, partial_in, conv_in, adj_in, up_in, key_in, val_in,
    feat_in, conv_out, adj_out, payload,
    lengths, par, partial, conv, adj, up, key, val, feat, before, after, sums, zero_scr, keep,
    length_sem, in_sems, out_sems,
):
    me = lax.axis_index("ctx")
    base = me * rows
    count = arrived.shape[0]
    poles = (par.shape[1] // SUB - 1) // 2
    extended = rows + HALO
    padded = rows + 2 * HALO
    get_lengths = pltpu.make_async_copy(far_lengths, lengths, length_sem)
    get_lengths.start()
    far = [par_in, partial_in, conv_in, adj_in, up_in, key_in, val_in, feat_in]
    near = [par, partial, conv, adj, up, key, val, feat]
    each_group(groups, lambda half: start_all(group_copies(far, near, in_sems, half)))
    zero_scr[...] = jnp.zeros((SUB, LANES), F32)
    zero = zero_scr[...]
    get_lengths.wait()
    starts = segment_starts(lengths)
    fill_keep(keep, starts, base, rows)
    until, since = jnp.int32(extended), jnp.int32(0)
    first, last, newest = jnp.int32(0), jnp.int32(2**30), jnp.int32(0)
    for start in starts:
        at = start - base
        until = jnp.where(at >= 0, jnp.minimum(until, at), until)
        since = jnp.where(at <= extended, jnp.maximum(since, at), since)
        first = jnp.where(at <= 0, jnp.maximum(first, start), first)
        last = jnp.where(at > extended, jnp.minimum(last, start), last)
        newest = jnp.where(at <= extended, jnp.maximum(newest, start), newest)
    steps = jnp.maximum(until, extended - since)
    through = flag(newest < base + rows)
    chunk = unroll_of(extended)

    def group(half):
        incoming = group_copies(far, near, in_sems, half)
        outgoing = group_copies([conv, adj], [conv_out, adj_out], out_sems, half)
        par_h, partial_h, conv_h, adj_h = par.at[half], partial.at[half], conv.at[half], adj.at[half]
        feat_h = feat.at[half]
        wait_all(incoming[:2])
        per_pass = poles // 2
        zeros = [zero] * per_pass
        for part in range(2):
            chosen = list(range(part * per_pass, (part + 1) * per_pass))
            rate = [jnp.exp(vec(par_h, m)) for m in chosen]
            block = [jnp.exp(-rows * r) for r in rate]

            def arrived_states(d):
                got = []
                for m in range(chosen[0], chosen[-1] + 1, 2):
                    pair = arrived[d, half, m * SUB : (m + 2) * SUB, :].astype(F32)
                    got += [pair[:SUB], pair[SUB:]]
                return got

            def from_before(d, carry):
                joined = flag((d + 1) * rows - 1 >= first)
                got = arrived_states(d)
                return [block[i] * carry[i] + joined * got[i] for i in range(per_pass)]

            def from_after(i, carry):
                d = count - 1 - i
                joined = flag(d * rows + HALO < last)
                got = arrived_states(d)
                return [block[i] * carry[i] + joined * got[i] for i in range(per_pass)]

            state = lax.fori_loop(0, me, from_before, zeros)
            adjoint = lax.fori_loop(0, count - 1 - me, from_after, zeros)
            own = arrived_states(me)
            for i, m in enumerate(chosen):
                scale = vec(par_h, poles + m) * jnp.exp(-rate[i])
                put(before, m, scale * state[i])
                put(after, m, scale * adjoint[i])
                cross = jnp.exp(-(HALO + 1) * rate[i]) * (adjoint[i] * through)
                put(sums, (9 + m) * groups + half, vec(partial_h, m) + cross * own[i])
        put(sums, (9 + poles) * groups + half, vec(partial_h, poles))
        decay = [jnp.exp(-jnp.exp(vec(par_h, m))) for m in range(poles)]
        enter = [vec(before, m) for m in range(poles)]
        leave = [vec(after, m) for m in range(poles)]
        wait_all(incoming[2:4])

        def carried(i, carry):
            enter, leave = carry
            for step in range(chunk):
                p = chunk * i + step
                back = extended - 1 - p
                put(conv_h, p, vec(conv_h, p) + flag(p < until) * total_of(enter))
                put(adj_h, back, vec(adj_h, back) + flag(back >= since) * total_of(leave))
                enter = [decay[m] * enter[m] for m in range(poles)]
                leave = [decay[m] * leave[m] for m in range(poles)]
            return enter, leave

        lax.fori_loop(0, (steps + chunk - 1) // chunk, carried, (enter, leave))
        start_all(outgoing)
        wait_all(incoming[4:])
        posted = posted_rows(keep, conv_h, adj_h, up.at[half], key.at[half], val.at[half])

        def tap_terms(i, carry):
            tap_sums, feat_now, feat_one = carry
            p = rows - 1 - i
            now, masked_one, masked_two = posted(p)
            feat_two = [vec(feat_h, third * padded + p) for third in range(3)]
            new_sums = []
            for third in range(3):
                new_sums += [
                    tap_sums[3 * third] + now[third] * feat_now[third],
                    tap_sums[3 * third + 1] + masked_one[third] * feat_one[third],
                    tap_sums[3 * third + 2] + masked_two[third] * feat_two[third],
                ]
            return new_sums, feat_one, feat_two

        feat_last = [vec(feat_h, third * padded + rows + 1) for third in range(3)]
        feat_before = [vec(feat_h, third * padded + rows) for third in range(3)]
        tap_sums, _, _ = lax.fori_loop(
            0, rows, tap_terms, ([zero] * 9, feat_last, feat_before), unroll=4
        )
        for third in range(3):
            for j in range(3):
                put(sums, (3 * j + third) * groups + half, tap_sums[3 * third + j])

    each_group(groups, group)
    width = groups * SUB
    same = 9 * width
    tap_sums = sums[0:same, :].astype(BF16)
    columns = (payload.shape[1] - same) // 16 - 1
    for e in range(count):
        payload[e, 0:same, :] = tap_sums
        first_row = same + (e * width) // count
        for j in range(columns):
            value = sums[pl.ds(first_row + j, 16, stride=width), :]
            payload[e, same + 16 * j : same + 16 * (j + 1), :] = value.astype(BF16)
        last_row = first_row + poles * width
        payload[e, same + 16 * columns :, :] = sums[last_row : last_row + 16, :].astype(BF16)
    each_group(
        groups,
        lambda half: wait_all(group_copies([conv, adj], [conv_out, adj_out], out_sems, half)),
    )


def grads_kernel(
    rows, groups, far_lengths, tap_in, conv_in, adj_in, up_in, key_in, val_in, grads,
    lengths, tap, conv, adj, up, key, val, post, ready, keep, length_sem, in_sems, out_sems,
):
    extended = rows + HALO
    get_lengths = pltpu.make_async_copy(far_lengths, lengths, length_sem)
    get_lengths.start()
    far = [tap_in, conv_in, adj_in, up_in, key_in, val_in]
    near = [tap, conv, adj, up, key, val]
    each_group(groups, lambda half: start_all(group_copies(far, near, in_sems, half)))

    def leaving(half):
        return [
            pltpu.make_async_copy(
                ready.at[half, third],
                grads.at[
                    0, :, pl.ds(pl.multiple_of((third * groups + half) * GROUP, GROUP), GROUP)
                ],
                out_sems.at[half, third],
            )
            for third in range(3)
        ]

    get_lengths.wait()
    fill_keep(keep, segment_starts(lengths), lax.axis_index("ctx") * rows, rows)

    def group(half):
        wait_all(group_copies(far, near, in_sems, half))
        taps_h = [[vec(tap.at[half], third * 3 + j) for j in range(3)] for third in range(3)]
        posted = posted_rows(
            keep, conv.at[half], adj.at[half], up.at[half], key.at[half], val.at[half]
        )
        _, _, far_two = posted(extended - 1)
        _, near_one, near_two = posted(extended - 2)

        def transposed(i, carry):
            one, two, three = carry
            p = rows - 1 - i
            now, masked_one, masked_two = posted(p)
            for third in range(3):
                back = (
                    taps_h[third][0] * now[third]
                    + taps_h[third][1] * one[third]
                    + taps_h[third][2] * three[third]
                )
                put(post, third * rows + p, back)
            return masked_one, masked_two, two

        lax.fori_loop(0, rows, transposed, (near_one, near_two, far_two), unroll=4)

        def write(i, carry):
            for third in range(3):
                for j in range(SUB):
                    value = post[pl.ds((third * rows + i * 16) * SUB + j, 16, stride=SUB), :]
                    lanes = slice(j * LANES, (j + 1) * LANES)
                    ready[half, third, pl.ds(pl.multiple_of(i * 16, 16), 16), lanes] = value.astype(
                        BF16
                    )
            return carry

        lax.fori_loop(0, rows // 16, write, 0, unroll=2)
        start_all(leaving(half))

    each_group(groups, group)
    each_group(groups, lambda half: wait_all(leaving(half)))


def share_kernel(parts, out):
    mine = parts[0].astype(F32)
    for k in range(1, parts.shape[0]):
        mine = mine + parts[k].astype(F32)
    out[...] = mine.astype(BF16)


def emit_kernel(groups, scale, shares, grad_taps, resid, skip, whole):
    me = lax.axis_index("ctx")
    width = groups * SUB
    poles, per_shard = resid.shape
    mine = shares[0].astype(F32)
    for k in range(1, shares.shape[0]):
        mine = mine + shares[k].astype(F32)
    whole[...] = mine * scale
    for k in range(3 * width):
        grad_taps[:, k * LANES : (k + 1) * LANES] = whole[pl.ds(k, 3, stride=3 * width), :]
    first = 9 * width
    columns = (whole.shape[0] - first) // 16 - 1
    last = first + 16 * columns
    if per_shard >= LANES:
        for j in range(columns):
            lanes = slice(j * LANES, (j + 1) * LANES)
            resid[:, lanes] = whole[first + 16 * j : first + 16 * (j + 1), :]
            skip[:, lanes] = whole[last + j : last + j + 1, :]
    else:
        per = LANES // per_shard
        rows = whole[first : first + 16, :]
        final = whole[last : last + 1, :]
        place = lax.rem(me, per)
        chosen, chosen_last = rows[:, :per_shard], final[:, :per_shard]
        for i in range(1, per):
            lanes = slice(i * per_shard, (i + 1) * per_shard)
            chosen = jnp.where(place == i, rows[:, lanes], chosen)
            chosen_last = jnp.where(place == i, final[:, lanes], chosen_last)
        resid[...] = chosen
        skip[...] = chosen_last


def swap(block, axes):
    return lax.all_to_all(block, axes, split_axis=0, concat_axis=0, tiled=True)


def per_device(features, upstream, lengths, conv_taps, residues, log_rate, skip_gain):
    rows = features.shape[1]
    channels = upstream.shape[2]
    poles = residues.shape[0]
    ctx_count = lax.axis_size("ctx")
    total = ctx_count * lax.axis_size("dp")
    per_shard = channels // ctx_count
    groups = channels // GROUP
    grad_scale = 1.0 / math.sqrt(rows * total)
    extended = rows + HALO
    padded = rows + 2 * HALO
    state_rows = poles * SUB
    limits = pltpu.CompilerParams(vmem_limit_bytes=40 * 1024 * 1024)
    hbm = pl.BlockSpec(memory_space=pltpu.HBM)
    vmem = pl.BlockSpec(memory_space=pltpu.VMEM)

    def tall(height):
        return jax.ShapeDtypeStruct((groups, height * SUB, LANES), F32)

    def near(*heights):
        return [pltpu.VMEM((groups, height * SUB, LANES), F32) for height in heights]

    def scratch(height):
        return pltpu.VMEM((height * SUB, LANES), F32)

    def sems(*shape):
        return pltpu.SemaphoreType.DMA(shape)

    keep = pltpu.SMEM((rows + 8,), F32)
    small = pltpu.SMEM(lengths.shape, jnp.int32)

    def call(kernel, name, ins, in_specs, outs, out_specs, scratch_shapes=()):
        ins = [
            pltpu.with_memory_space_constraint(x, pltpu.HBM) if spec is hbm else x
            for x, spec in zip(ins, in_specs)
        ]
        if isinstance(outs, list):
            outs = [
                pltpu.HBM(out.shape, out.dtype) if spec is hbm else out
                for out, spec in zip(outs, out_specs)
            ]
        return pl.pallas_call(
            kernel,
            out_shape=outs,
            in_specs=in_specs,
            out_specs=out_specs,
            scratch_shapes=list(scratch_shapes),
            compiler_params=limits,
            name=name,
        )(*ins)

    block_rows = (3 * poles // lax.axis_size("dp") + 2) * tiles_of(per_shard)
    block = (-(-block_rows // 16) * 16, min(per_shard, LANES))
    span = features.shape[2]
    params, edge, head = call(
        start_kernel,
        "start",
        [log_rate, residues, skip_gain[None], features, upstream],
        [hbm] * 5,
        [
            jax.ShapeDtypeStruct((total,) + block, BF16),
            jax.ShapeDtypeStruct((HALO, span), BF16),
            jax.ShapeDtypeStruct((HALO, span + channels), BF16),
        ],
        [vmem] * 3,
        [
            pltpu.VMEM((poles, per_shard), F32),
            pltpu.VMEM((poles, per_shard), F32),
            pltpu.VMEM((1, per_shard), F32),
            pltpu.VMEM((16, span), BF16),
            pltpu.VMEM((16, span), BF16),
            pltpu.VMEM((16, channels), BF16),
            pltpu.VMEM(block, F32),
            sems(6),
        ],
    )
    params = swap(params, ("dp", "ctx"))
    left = shifted(edge, "ctx", 1)
    right = shifted(head, "ctx", -1)

    payload, feat, up, mixed, gout, par, tap = call(
        functools.partial(ends_kernel, rows, groups),
        "ends",
        [lengths, features, upstream, left, right, conv_taps, params],
        [hbm] * 3 + [vmem] * 4,
        [jax.ShapeDtypeStruct((ctx_count, groups, state_rows, LANES), BF16)]
        + [tall(height) for height in [3 * padded] + [extended] * 3 + [2 * poles + 1, 9]],
        [vmem] + [hbm] * 6,
        [
            small,
            pltpu.VMEM((groups, 3, rows, GROUP), BF16),
            pltpu.VMEM((groups, rows, GROUP), BF16),
        ]
        + near(3 * padded, extended, extended, extended, 2 * poles + 1, 9)
        + [pltpu.VMEM((2, state_rows, LANES), BF16)]
        + [pltpu.VMEM((block[0], LANES), F32), scratch(1), keep]
        + [sems(), sems(groups, 4), sems(groups, 6)],
    )
    arrived = swap(payload, "ctx")
    key, val, conv, adj, partial = call(
        functools.partial(local_kernel, rows, groups),
        "local",
        [lengths, feat, mixed, gout, par, tap],
        [hbm] * 6,
        [tall(extended)] * 4 + [tall(poles + 1)],
        [hbm] * 5,
        [small]
        + near(extended, extended, 2 * poles + 1, 9, 3 * padded)
        + near(extended, extended, extended, extended, poles + 1)
        + [scratch(1), keep, sems(), sems(groups, 5), sems(groups, 5)],
    )
    used = (10 + poles) * groups * SUB
    sum_rows = 9 * groups * SUB + 16 * max(1, per_shard // LANES) + 16
    conv, adj, sums = call(
        functools.partial(sums_kernel, rows, groups),
        "sums",
        [lengths, arrived, par, partial, conv, adj, up, key, val, feat],
        [hbm, vmem] + [hbm] * 8,
        [tall(extended)] * 2 + [jax.ShapeDtypeStruct((ctx_count, sum_rows, LANES), BF16)],
        [hbm, hbm, vmem],
        [small]
        + near(2 * poles + 1, poles + 1, extended, extended, extended, extended, extended)
        + near(3 * padded)
        + [scratch(poles), scratch(poles)]
        + [pltpu.VMEM((used + 16, LANES), F32), scratch(1), keep]
        + [sems(), sems(groups, 8), sems(groups, 2)],
    )
    parts = swap(sums, "ctx")
    (grads,) = call(
        functools.partial(grads_kernel, rows, groups),
        "grads",
        [lengths, tap, conv, adj, up, key, val],
        [hbm] * 7,
        [jax.ShapeDtypeStruct(features.shape, BF16)],
        [hbm],
        [small]
        + near(9, extended, extended, extended, extended, extended)
        + [scratch(3 * rows), pltpu.VMEM((groups, 3, rows, GROUP), BF16), keep]
        + [sems(), sems(groups, 6), sems(groups, 3)],
    )
    mine = call(
        share_kernel,
        "share",
        [parts],
        [vmem],
        jax.ShapeDtypeStruct((sum_rows, LANES), BF16),
        vmem,
    )
    grad_taps, resid, skip = call(
        functools.partial(emit_kernel, groups, grad_scale),
        "emit",
        [lax.all_gather(mine, "dp")],
        [vmem],
        [
            jax.ShapeDtypeStruct((3, 3 * channels), F32),
            jax.ShapeDtypeStruct((poles, per_shard), F32),
            jax.ShapeDtypeStruct((1, per_shard), F32),
        ],
        [vmem] * 3,
        [pltpu.VMEM((sum_rows, LANES), F32)],
    )
    return grads, grad_taps, resid, skip.reshape(per_shard)


def solution(mesh):
    return jax.shard_map(
        per_device,
        mesh=mesh,
        in_specs=(
            P("dp", "ctx", None),
            P("dp", "ctx", None),
            P("dp", None),
            P(),
            P(None, "ctx"),
            P(None, "ctx"),
            P("ctx"),
        ),
        out_specs=(P("dp", "ctx", None), P(), P(None, "ctx"), P("ctx")),
        check_vma=False,
    )
```

```python
import functools
import math

import jax
import jax.numpy as jnp
from jax import lax
from jax.experimental import pallas as pl
from jax.experimental.pallas import tpu as pltpu
from jax.sharding import PartitionSpec as P

F32 = jnp.float32
BF16 = jnp.bfloat16
LANES = 128
SUB = 8
GROUP = SUB * LANES
HALO = 2


def shifted(block, axis, distance):
    count = lax.axis_size(axis)
    route = [(i - distance, i) for i in range(count) if 0 <= i - distance < count]
    return lax.ppermute(block, axis, route)


def vec(ref, index):
    return ref[pl.ds(pl.multiple_of(index * SUB, SUB), SUB), :]


def put(ref, index, value):
    ref[pl.ds(pl.multiple_of(index * SUB, SUB), SUB), :] = value


def spread(dst, first, src, column, row_count):
    for j in range(SUB):
        lanes = pl.ds(pl.multiple_of(column + j * LANES, LANES), LANES)
        dst[pl.ds(first * SUB + j, row_count, stride=SUB), :] = src[:, lanes].astype(F32)


def spread_rows(dst, first, src, row_count):
    def step(i, carry):
        for j in range(SUB):
            value = src[pl.ds(pl.multiple_of(i * 16, 16), 16), j * LANES : (j + 1) * LANES]
            dst[pl.ds((i * 16 + first) * SUB + j, 16, stride=SUB), :] = value.astype(F32)
        return carry

    lax.fori_loop(0, row_count // 16, step, 0)


def tiles_of(width):
    return max(1, width // LANES)


def start_kernel(
    log_rate, residues, skip_gain, features, upstream, out, edge, head,
    rates, coeffs, gains, low, high, high_up, slab, sems,
):
    rows = features.shape[1]
    copies = [
        pltpu.make_async_copy(source, target, sems.at[i])
        for i, (source, target) in enumerate(
            [
                (log_rate, rates),
                (residues, coeffs),
                (skip_gain, gains),
                (features.at[0, pl.ds(0, 16), :], low),
                (features.at[0, pl.ds(rows - 16, 16), :], high),
                (upstream.at[0, pl.ds(0, 16), :], high_up),
            ]
        )
    ]
    start_all(copies)
    width = rates.shape[1]
    members = lax.axis_size("dp")
    poles = rates.shape[0] // members

    def mine(ref, lanes):
        value = ref[0:poles, lanes]
        for member in range(1, members):
            other = ref[member * poles : (member + 1) * poles, lanes]
            value = jnp.where(lax.axis_index("dp") == member, other, value)
        return value

    per = tiles_of(width)
    slab[...] = jnp.zeros(slab.shape, F32)
    wait_all(copies[:3])
    for j in range(per):
        lanes = slice(j * LANES, min(width, (j + 1) * LANES))
        rate, gain = mine(rates, lanes), gains[:, lanes]
        slab[pl.ds(j, poles, stride=per), :] = rounded(rate)
        slab[pl.ds(poles * per + j, poles, stride=per), :] = rate - rounded(rate)
        slab[pl.ds(2 * poles * per + j, poles, stride=per), :] = mine(coeffs, lanes)
        slab[pl.ds(3 * poles * per + j, 1), :] = rounded(gain)
        slab[pl.ds((3 * poles + 1) * per + j, 1), :] = gain - rounded(gain)
    packed = slab[...].astype(BF16)
    for e in range(out.shape[0]):
        out[e] = packed
    wait_all(copies[3:])
    span = features.shape[2]
    for at in range(0, span, GROUP):
        lanes = slice(at, at + GROUP)
        head[:, lanes] = low[:, lanes].astype(F32)[:HALO].astype(BF16)
        edge[:, lanes] = high[:, lanes].astype(F32)[16 - HALO :].astype(BF16)
    for at in range(0, upstream.shape[2], GROUP):
        lanes = slice(at, at + GROUP)
        head[:, span + at : span + at + GROUP] = high_up[:, lanes].astype(F32)[:HALO].astype(BF16)


def spread_params(dst, par, slab, half, groups, poles):
    members = lax.axis_size("dp")
    pieces = par.shape[0] // members
    width = par.shape[2]
    share = poles // members
    many = pieces // groups
    joined = LANES // width
    per = SUB * joined // many
    for member in range(members):
        base = member * pieces + half * many
        for k in range(many // joined):
            parts = [par[base + k * joined + i].astype(F32) for i in range(joined)]
            slab[...] = parts[0] if joined == 1 else jnp.concatenate(parts, axis=1)
            for j in range(per):

                def rows_of(piece, count):
                    return slab[pl.ds(piece * per + j, count, stride=per), :]

                first = member * share * SUB + k * per + j
                rates = rows_of(0, share) + rows_of(share, share)
                dst[pl.ds(first, share, stride=SUB), :] = rates
                dst[pl.ds(poles * SUB + first, share, stride=SUB), :] = rows_of(2 * share, share)
                if member == 0:
                    gain = rows_of(3 * share, 1) + rows_of(3 * share + 1, 1)
                    dst[pl.ds(2 * poles * SUB + k * per + j, 1), :] = gain


def segment_starts(lengths):
    starts = [jnp.int32(0)]
    for j in range(lengths.shape[1]):
        starts.append(starts[-1] + lengths[0, j])
    return starts


def fill_keep(keep, starts, base, rows):
    count = rows + HALO + 2

    def step(i, carry):
        keep[i] = jnp.float32(1.0)
        return carry

    lax.fori_loop(0, count, step, 0, unroll=4)
    for start in starts:
        at = start - base + 1

        @pl.when((at >= 0) & (at < count))
        def _():
            keep[at] = jnp.float32(0.0)


def rounded(value):
    return value.astype(BF16).astype(F32)


def flag(condition):
    return jnp.where(condition, 1.0, 0.0).astype(F32)


def total_of(terms):
    terms = list(terms)
    while len(terms) > 1:
        odd = terms[-1:] if len(terms) % 2 else []
        terms = [x + y for x, y in zip(terms[::2], terms[1::2])] + odd
    return terms[0]


def unroll_of(trips):
    return max(d for d in range(1, 14) if trips % d == 0)


def featured(feat, tap, p, keep_one, keep_two):
    return (
        tap[0] * vec(feat, p + 2)
        + tap[1] * (keep_one * vec(feat, p + 1))
        + tap[2] * (keep_two * vec(feat, p))
    )


def each_group(groups, body):
    def step(half, carry):
        body(half)
        return carry

    lax.fori_loop(0, groups, step, 0)


def group_copies(sources, targets, sems, half):
    return [
        pltpu.make_async_copy(source.at[half], target.at[half], sems.at[half, i])
        for i, (source, target) in enumerate(zip(sources, targets))
    ]


def start_all(copies):
    for copy in copies:
        copy.start()


def wait_all(copies):
    for copy in copies:
        copy.wait()


def ends_kernel(
    rows, groups, far_lengths, features, upstream, left, right, taps, params,
    payload, feat_out, up_out, mixed_out, gout_out, par_out, tap_out, key_out, val_out,
    lengths, raw, raw_up, feat, up, mixed, gout, par, tap, key_scr, val_scr, stack, slab, zero_scr, keep,
    length_sem, in_sems, out_sems,
):
    me = lax.axis_index("ctx")
    base = me * rows
    count = payload.shape[0]
    poles = (par.shape[1] // SUB - 1) // 2
    extended = rows + HALO
    padded = rows + 2 * HALO
    get_lengths = pltpu.make_async_copy(far_lengths, lengths, length_sem)
    get_lengths.start()

    def arriving(half):
        lanes = [
            pl.ds(pl.multiple_of((third * groups + half) * GROUP, GROUP), GROUP)
            for third in range(3)
        ]
        return [
            pltpu.make_async_copy(
                features.at[0, :, lanes[third]], raw.at[half, third], in_sems.at[half, third]
            )
            for third in range(3)
        ] + [pltpu.make_async_copy(upstream.at[0, :, lanes[0]], raw_up.at[half], in_sems.at[half, 3])]

    near = [feat, up, tap, par, mixed, gout, key_scr, val_scr]
    far = [feat_out, up_out, tap_out, par_out, mixed_out, gout_out, key_out, val_out]

    each_group(groups, lambda half: start_all(arriving(half)))
    zero_scr[...] = jnp.zeros((SUB, LANES), F32)
    zeros = [zero_scr[...]] * poles

    def prepare(half):
        spread_params(par.at[half], params, slab, half, groups, poles)
        for third in range(3):
            column = (third * groups + half) * GROUP
            spread(feat.at[half], third * padded, left, column, HALO)
            spread(feat.at[half], third * padded + rows + HALO, right, column, HALO)
            spread(tap.at[half], third * 3, taps, column, 3)
        spread(up.at[half], rows, right, (3 * groups + half) * GROUP, HALO)

    each_group(groups, prepare)
    get_lengths.wait()
    starts = segment_starts(lengths)
    fill_keep(keep, starts, base, rows)
    low, high = jnp.int32(0), jnp.int32(extended)
    for start in starts:
        at = start - base
        low = jnp.where(at < rows, jnp.maximum(low, at), low)
        high = jnp.where(at > HALO, jnp.minimum(high, at), high)

    def group(half):
        incoming = arriving(half)
        outgoing = group_copies(near, far, out_sems, half)
        feat_h, up_h, mixed_h, gout_h = feat.at[half], up.at[half], mixed.at[half], gout.at[half]
        for third in range(3):
            incoming[third].wait()
            spread_rows(feat_h, third * padded + HALO, raw.at[half, third], rows)
        incoming[3].wait()
        spread_rows(up_h, 0, raw_up.at[half], rows)
        start_all(outgoing[:4])
        taps_h = [[vec(tap.at[half], third * 3 + j) for j in range(3)] for third in range(3)]

        def product(p, carry):
            keep_one = keep[p + 1]
            keep_two = keep_one * keep[p]
            query, key, val = (
                featured(feat_h, taps_h[third], third * padded + p, keep_one, keep_two)
                for third in range(3)
            )
            put(mixed_h, p, rounded(key * val))
            put(gout_h, p, rounded(vec(up_h, p) * query))
            put(key_scr.at[half], p, key)
            put(val_scr.at[half], p, val)
            return carry

        lax.fori_loop(0, extended, product, 0, unroll=unroll_of(extended))
        start_all(outgoing[4:])
        decay = [jnp.exp(-jnp.exp(vec(par.at[half], m))) for m in range(poles)]

        def sweep(i, carry):
            state, adjoint = carry
            back = extended - 1 - i
            x = vec(mixed_h, i) * flag(i >= low)
            g = vec(gout_h, back) * flag(back < high)
            state = [decay[m] * state[m] + x for m in range(poles)]
            adjoint = [decay[m] * adjoint[m] + g for m in range(poles)]
            return state, adjoint

        state, adjoint = lax.fori_loop(0, rows, sweep, (zeros, zeros), unroll=8)
        for m in range(0, poles, 2):
            at = slice(m * SUB, (m + 2) * SUB)
            stack[0, at, :] = jnp.concatenate(state[m : m + 2], axis=0).astype(BF16)
            stack[1, at, :] = jnp.concatenate(adjoint[m : m + 2], axis=0).astype(BF16)
        for e in range(count):
            payload[e, half] = stack[jnp.where(e >= me, 0, 1)]

    each_group(groups, group)
    each_group(groups, lambda half: wait_all(group_copies(near, far, out_sems, half)))


def local_kernel(
    rows, groups, far_lengths, mixed_in, gout_in, par_in, conv_out, adj_out, partial_out,
    lengths, mixed, gout, par, conv, adj, partial, zero_scr, keep,
    length_sem, in_sems, out_sems,
):
    poles = (par.shape[1] // SUB - 1) // 2
    extended = rows + HALO
    get_lengths = pltpu.make_async_copy(far_lengths, lengths, length_sem)
    get_lengths.start()
    far_in, near_in = [par_in, mixed_in, gout_in], [par, mixed, gout]
    near_out, far_out = [conv, adj, partial], [conv_out, adj_out, partial_out]
    each_group(groups, lambda half: start_all(group_copies(far_in, near_in, in_sems, half)))
    zero_scr[...] = jnp.zeros((SUB, LANES), F32)
    zero = zero_scr[...]
    per_pass = poles // 4
    zeros = [zero] * per_pass
    get_lengths.wait()
    fill_keep(keep, segment_starts(lengths), lax.axis_index("ctx") * rows, rows)

    def group(half):
        incoming = group_copies(far_in, near_in, in_sems, half)
        outgoing = group_copies(near_out, far_out, out_sems, half)
        mixed_h, gout_h, par_h = mixed.at[half], gout.at[half], par.at[half]
        conv_h, adj_h = conv.at[half], adj.at[half]
        wait_all(incoming)
        gain = vec(par_h, 2 * poles)
        for part in range(poles // per_pass):
            chosen = list(range(part * per_pass, (part + 1) * per_pass))
            decay = [jnp.exp(-jnp.exp(vec(par_h, m))) for m in chosen]
            coeff = [vec(par_h, poles + m) for m in chosen]

            def sweep(i, carry, inside=True):
                state, adjoint, resid, skip = carry
                back = extended - 1 - i
                x = vec(mixed_h, i)
                g = vec(gout_h, back)
                keep_fwd = keep[i + 1]
                keep_bwd = keep[back + 2]
                state = [decay[m] * (state[m] * keep_fwd) + x for m in range(per_pass)]
                adjoint = [decay[m] * (adjoint[m] * keep_bwd) + g for m in range(per_pass)]
                forward = total_of(coeff[m] * state[m] for m in range(per_pass))
                backward = total_of(coeff[m] * adjoint[m] for m in range(per_pass))
                if inside:
                    own = vec(mixed_h, back)
                    resid = [resid[m] + own * adjoint[m] for m in range(per_pass)]
                if part == 0:
                    put(conv_h, i, forward + gain * x)
                    put(adj_h, back, backward + gain * g)
                    if inside:
                        skip = skip + own * g
                else:
                    put(conv_h, i, forward + vec(conv_h, i))
                    put(adj_h, back, backward + vec(adj_h, back))
                return state, adjoint, resid, skip

            carry = (zeros, zeros, zeros, zero)
            for i in range(HALO):
                carry = sweep(i, carry, inside=False)
            _, _, resid, skip = lax.fori_loop(HALO, extended, sweep, carry, unroll=32)
            for i, m in enumerate(chosen):
                put(partial.at[half], m, resid[i])
            if part == 0:
                put(partial.at[half], poles, skip)
        start_all(outgoing)

    each_group(groups, group)
    each_group(groups, lambda half: wait_all(group_copies(near_out, far_out, out_sems, half)))


def posted_rows(keep, conv, adj, up, key, val):
    def posted(p):
        keep_one = keep[p + 1]
        keep_two = keep_one * keep[p]
        conv_out = rounded(vec(conv, p))
        grad_mixed = rounded(vec(adj, p))
        now = [vec(up, p) * conv_out, grad_mixed * vec(val, p), grad_mixed * vec(key, p)]
        return now, [keep_one * g for g in now], [keep_two * g for g in now]

    return posted


def sums_kernel(
    rows, groups, far_lengths, arrived, par_in, partial_in, conv_in, adj_in, up_in, key_in, val_in,
    feat_in, conv_out, adj_out, payload,
    lengths, par, partial, conv, adj, up, key, val, feat, before, after, sums, zero_scr, keep,
    length_sem, in_sems, out_sems,
):
    me = lax.axis_index("ctx")
    base = me * rows
    count = arrived.shape[0]
    poles = (par.shape[1] // SUB - 1) // 2
    extended = rows + HALO
    padded = rows + 2 * HALO
    get_lengths = pltpu.make_async_copy(far_lengths, lengths, length_sem)
    get_lengths.start()
    far = [par_in, partial_in, conv_in, adj_in, up_in, key_in, val_in, feat_in]
    near = [par, partial, conv, adj, up, key, val, feat]
    each_group(groups, lambda half: start_all(group_copies(far, near, in_sems, half)))
    zero_scr[...] = jnp.zeros((SUB, LANES), F32)
    zero = zero_scr[...]
    get_lengths.wait()
    starts = segment_starts(lengths)
    fill_keep(keep, starts, base, rows)
    until, since = jnp.int32(extended), jnp.int32(0)
    first, last, newest = jnp.int32(0), jnp.int32(2**30), jnp.int32(0)
    for start in starts:
        at = start - base
        until = jnp.where(at >= 0, jnp.minimum(until, at), until)
        since = jnp.where(at <= extended, jnp.maximum(since, at), since)
        first = jnp.where(at <= 0, jnp.maximum(first, start), first)
        last = jnp.where(at > extended, jnp.minimum(last, start), last)
        newest = jnp.where(at <= extended, jnp.maximum(newest, start), newest)
    steps = jnp.maximum(until, extended - since)
    through = flag(newest < base + rows)
    chunk = unroll_of(extended)

    def group(half):
        incoming = group_copies(far, near, in_sems, half)
        outgoing = group_copies([conv, adj], [conv_out, adj_out], out_sems, half)
        par_h, partial_h, conv_h, adj_h = par.at[half], partial.at[half], conv.at[half], adj.at[half]
        feat_h = feat.at[half]
        wait_all(incoming[:2])
        per_pass = poles // 2
        zeros = [zero] * per_pass
        for part in range(2):
            chosen = list(range(part * per_pass, (part + 1) * per_pass))
            rate = [jnp.exp(vec(par_h, m)) for m in chosen]
            block = [jnp.exp(-rows * r) for r in rate]

            def arrived_states(d):
                got = []
                for m in range(chosen[0], chosen[-1] + 1, 2):
                    pair = arrived[d, half, m * SUB : (m + 2) * SUB, :].astype(F32)
                    got += [pair[:SUB], pair[SUB:]]
                return got

            def from_before(d, carry):
                joined = flag((d + 1) * rows - 1 >= first)
                got = arrived_states(d)
                return [block[i] * carry[i] + joined * got[i] for i in range(per_pass)]

            def from_after(i, carry):
                d = count - 1 - i
                joined = flag(d * rows + HALO < last)
                got = arrived_states(d)
                return [block[i] * carry[i] + joined * got[i] for i in range(per_pass)]

            state = lax.fori_loop(0, me, from_before, zeros)
            adjoint = lax.fori_loop(0, count - 1 - me, from_after, zeros)
            own = arrived_states(me)
            for i, m in enumerate(chosen):
                scale = vec(par_h, poles + m) * jnp.exp(-rate[i])
                put(before, m, scale * state[i])
                put(after, m, scale * adjoint[i])
                cross = jnp.exp(-(HALO + 1) * rate[i]) * (adjoint[i] * through)
                put(sums, (9 + m) * groups + half, vec(partial_h, m) + cross * own[i])
        put(sums, (9 + poles) * groups + half, vec(partial_h, poles))
        decay = [jnp.exp(-jnp.exp(vec(par_h, m))) for m in range(poles)]
        enter = [vec(before, m) for m in range(poles)]
        leave = [vec(after, m) for m in range(poles)]
        wait_all(incoming[2:4])

        def carried(i, carry):
            enter, leave = carry
            for step in range(chunk):
                p = chunk * i + step
                back = extended - 1 - p
                put(conv_h, p, vec(conv_h, p) + flag(p < until) * total_of(enter))
                put(adj_h, back, vec(adj_h, back) + flag(back >= since) * total_of(leave))
                enter = [decay[m] * enter[m] for m in range(poles)]
                leave = [decay[m] * leave[m] for m in range(poles)]
            return enter, leave

        lax.fori_loop(0, (steps + chunk - 1) // chunk, carried, (enter, leave))
        start_all(outgoing)
        wait_all(incoming[4:])
        posted = posted_rows(keep, conv_h, adj_h, up.at[half], key.at[half], val.at[half])

        def tap_terms(i, carry):
            tap_sums, feat_now, feat_one = carry
            p = rows - 1 - i
            now, masked_one, masked_two = posted(p)
            feat_two = [vec(feat_h, third * padded + p) for third in range(3)]
            new_sums = []
            for third in range(3):
                new_sums += [
                    tap_sums[3 * third] + now[third] * feat_now[third],
                    tap_sums[3 * third + 1] + masked_one[third] * feat_one[third],
                    tap_sums[3 * third + 2] + masked_two[third] * feat_two[third],
                ]
            return new_sums, feat_one, feat_two

        feat_last = [vec(feat_h, third * padded + rows + 1) for third in range(3)]
        feat_before = [vec(feat_h, third * padded + rows) for third in range(3)]
        tap_sums, _, _ = lax.fori_loop(
            0, rows, tap_terms, ([zero] * 9, feat_last, feat_before), unroll=4
        )
        for third in range(3):
            for j in range(3):
                put(sums, (3 * j + third) * groups + half, tap_sums[3 * third + j])

    each_group(groups, group)
    width = groups * SUB
    same = 9 * width
    tap_sums = sums[0:same, :].astype(BF16)
    columns = (payload.shape[1] - same) // 16 - 1
    for e in range(count):
        payload[e, 0:same, :] = tap_sums
        first_row = same + (e * width) // count
        for j in range(columns):
            value = sums[pl.ds(first_row + j, 16, stride=width), :]
            payload[e, same + 16 * j : same + 16 * (j + 1), :] = value.astype(BF16)
        last_row = first_row + poles * width
        payload[e, same + 16 * columns :, :] = sums[last_row : last_row + 16, :].astype(BF16)
    each_group(
        groups,
        lambda half: wait_all(group_copies([conv, adj], [conv_out, adj_out], out_sems, half)),
    )


def grads_kernel(
    rows, groups, far_lengths, tap_in, conv_in, adj_in, up_in, key_in, val_in, grads,
    lengths, tap, conv, adj, up, key, val, post, ready, keep, length_sem, in_sems, out_sems,
):
    extended = rows + HALO
    get_lengths = pltpu.make_async_copy(far_lengths, lengths, length_sem)
    get_lengths.start()
    far = [tap_in, conv_in, adj_in, up_in, key_in, val_in]
    near = [tap, conv, adj, up, key, val]
    each_group(groups, lambda half: start_all(group_copies(far, near, in_sems, half)))

    def leaving(half):
        return [
            pltpu.make_async_copy(
                ready.at[half, third],
                grads.at[
                    0, :, pl.ds(pl.multiple_of((third * groups + half) * GROUP, GROUP), GROUP)
                ],
                out_sems.at[half, third],
            )
            for third in range(3)
        ]

    get_lengths.wait()
    fill_keep(keep, segment_starts(lengths), lax.axis_index("ctx") * rows, rows)

    def group(half):
        wait_all(group_copies(far, near, in_sems, half))
        taps_h = [[vec(tap.at[half], third * 3 + j) for j in range(3)] for third in range(3)]
        posted = posted_rows(
            keep, conv.at[half], adj.at[half], up.at[half], key.at[half], val.at[half]
        )
        _, _, far_two = posted(extended - 1)
        _, near_one, near_two = posted(extended - 2)

        def transposed(i, carry):
            one, two, three = carry
            p = rows - 1 - i
            now, masked_one, masked_two = posted(p)
            for third in range(3):
                back = (
                    taps_h[third][0] * now[third]
                    + taps_h[third][1] * one[third]
                    + taps_h[third][2] * three[third]
                )
                put(post, third * rows + p, back)
            return masked_one, masked_two, two

        lax.fori_loop(0, rows, transposed, (near_one, near_two, far_two), unroll=4)

        def write(i, carry):
            for third in range(3):
                for j in range(SUB):
                    value = post[pl.ds((third * rows + i * 16) * SUB + j, 16, stride=SUB), :]
                    lanes = slice(j * LANES, (j + 1) * LANES)
                    ready[half, third, pl.ds(pl.multiple_of(i * 16, 16), 16), lanes] = value.astype(
                        BF16
                    )
            return carry

        lax.fori_loop(0, rows // 16, write, 0, unroll=2)
        start_all(leaving(half))

    each_group(groups, group)
    each_group(groups, lambda half: wait_all(leaving(half)))


def share_kernel(parts, out):
    mine = parts[0].astype(F32)
    for k in range(1, parts.shape[0]):
        mine = mine + parts[k].astype(F32)
    out[...] = mine.astype(BF16)


def emit_kernel(groups, scale, shares, grad_taps, resid, skip, whole):
    me = lax.axis_index("ctx")
    width = groups * SUB
    poles, per_shard = resid.shape
    mine = shares[0].astype(F32)
    for k in range(1, shares.shape[0]):
        mine = mine + shares[k].astype(F32)
    whole[...] = mine * scale
    for k in range(3 * width):
        grad_taps[:, k * LANES : (k + 1) * LANES] = whole[pl.ds(k, 3, stride=3 * width), :]
    first = 9 * width
    columns = (whole.shape[0] - first) // 16 - 1
    last = first + 16 * columns
    if per_shard >= LANES:
        for j in range(columns):
            lanes = slice(j * LANES, (j + 1) * LANES)
            resid[:, lanes] = whole[first + 16 * j : first + 16 * (j + 1), :]
            skip[:, lanes] = whole[last + j : last + j + 1, :]
    else:
        per = LANES // per_shard
        rows = whole[first : first + 16, :]
        final = whole[last : last + 1, :]
        place = lax.rem(me, per)
        chosen, chosen_last = rows[:, :per_shard], final[:, :per_shard]
        for i in range(1, per):
            lanes = slice(i * per_shard, (i + 1) * per_shard)
            chosen = jnp.where(place == i, rows[:, lanes], chosen)
            chosen_last = jnp.where(place == i, final[:, lanes], chosen_last)
        resid[...] = chosen
        skip[...] = chosen_last


def swap(block, axes):
    return lax.all_to_all(block, axes, split_axis=0, concat_axis=0, tiled=True)


def per_device(features, upstream, lengths, conv_taps, residues, log_rate, skip_gain):
    rows = features.shape[1]
    channels = upstream.shape[2]
    poles = residues.shape[0]
    ctx_count = lax.axis_size("ctx")
    total = ctx_count * lax.axis_size("dp")
    per_shard = channels // ctx_count
    groups = channels // GROUP
    grad_scale = 1.0 / math.sqrt(rows * total)
    extended = rows + HALO
    padded = rows + 2 * HALO
    state_rows = poles * SUB
    limits = pltpu.CompilerParams(vmem_limit_bytes=40 * 1024 * 1024)
    hbm = pl.BlockSpec(memory_space=pltpu.HBM)
    vmem = pl.BlockSpec(memory_space=pltpu.VMEM)

    def tall(height):
        return jax.ShapeDtypeStruct((groups, height * SUB, LANES), F32)

    def near(*heights):
        return [pltpu.VMEM((groups, height * SUB, LANES), F32) for height in heights]

    def scratch(height):
        return pltpu.VMEM((height * SUB, LANES), F32)

    def sems(*shape):
        return pltpu.SemaphoreType.DMA(shape)

    keep = pltpu.SMEM((rows + 8,), F32)
    small = pltpu.SMEM(lengths.shape, jnp.int32)

    def call(kernel, name, ins, in_specs, outs, out_specs, scratch_shapes=()):
        ins = [
            pltpu.with_memory_space_constraint(x, pltpu.HBM) if spec is hbm else x
            for x, spec in zip(ins, in_specs)
        ]
        if isinstance(outs, list):
            outs = [
                pltpu.HBM(out.shape, out.dtype) if spec is hbm else out
                for out, spec in zip(outs, out_specs)
            ]
        return pl.pallas_call(
            kernel,
            out_shape=outs,
            in_specs=in_specs,
            out_specs=out_specs,
            scratch_shapes=list(scratch_shapes),
            compiler_params=limits,
            name=name,
        )(*ins)

    block_rows = (3 * poles // lax.axis_size("dp") + 2) * tiles_of(per_shard)
    block = (-(-block_rows // 16) * 16, min(per_shard, LANES))
    span = features.shape[2]
    params, edge, head = call(
        start_kernel,
        "start",
        [log_rate, residues, skip_gain[None], features, upstream],
        [hbm] * 5,
        [
            jax.ShapeDtypeStruct((total,) + block, BF16),
            jax.ShapeDtypeStruct((HALO, span), BF16),
            jax.ShapeDtypeStruct((HALO, span + channels), BF16),
        ],
        [vmem] * 3,
        [
            pltpu.VMEM((poles, per_shard), F32),
            pltpu.VMEM((poles, per_shard), F32),
            pltpu.VMEM((1, per_shard), F32),
            pltpu.VMEM((16, span), BF16),
            pltpu.VMEM((16, span), BF16),
            pltpu.VMEM((16, channels), BF16),
            pltpu.VMEM(block, F32),
            sems(6),
        ],
    )
    params = swap(params, ("dp", "ctx"))
    left = shifted(edge, "ctx", 1)
    right = shifted(head, "ctx", -1)

    payload, feat, up, mixed, gout, par, tap, key, val = call(
        functools.partial(ends_kernel, rows, groups),
        "ends",
        [lengths, features, upstream, left, right, conv_taps, params],
        [hbm] * 3 + [vmem] * 4,
        [jax.ShapeDtypeStruct((ctx_count, groups, state_rows, LANES), BF16)]
        + [tall(height) for height in [3 * padded] + [extended] * 3 + [2 * poles + 1, 9]]
        + [tall(extended)] * 2,
        [vmem] + [hbm] * 8,
        [
            small,
            pltpu.VMEM((groups, 3, rows, GROUP), BF16),
            pltpu.VMEM((groups, rows, GROUP), BF16),
        ]
        + near(3 * padded, extended, extended, extended, 2 * poles + 1, 9, extended, extended)
        + [pltpu.VMEM((2, state_rows, LANES), BF16)]
        + [pltpu.VMEM((block[0], LANES), F32), scratch(1), keep]
        + [sems(), sems(groups, 4), sems(groups, 8)],
    )
    arrived = swap(payload, "ctx")
    conv, adj, partial = call(
        functools.partial(local_kernel, rows, groups),
        "local",
        [lengths, mixed, gout, par],
        [hbm] * 4,
        [tall(extended)] * 2 + [tall(poles + 1)],
        [hbm] * 3,
        [small]
        + near(extended, extended, 2 * poles + 1, extended, extended, poles + 1)
        + [scratch(1), keep, sems(), sems(groups, 3), sems(groups, 3)],
    )
    used = (10 + poles) * groups * SUB
    sum_rows = 9 * groups * SUB + 16 * max(1, per_shard // LANES) + 16
    conv, adj, sums = call(
        functools.partial(sums_kernel, rows, groups),
        "sums",
        [lengths, arrived, par, partial, conv, adj, up, key, val, feat],
        [hbm, vmem] + [hbm] * 8,
        [tall(extended)] * 2 + [jax.ShapeDtypeStruct((ctx_count, sum_rows, LANES), BF16)],
        [hbm, hbm, vmem],
        [small]
        + near(2 * poles + 1, poles + 1, extended, extended, extended, extended, extended)
        + near(3 * padded)
        + [scratch(poles), scratch(poles)]
        + [pltpu.VMEM((used + 16, LANES), F32), scratch(1), keep]
        + [sems(), sems(groups, 8), sems(groups, 2)],
    )
    parts = swap(sums, "ctx")
    (grads,) = call(
        functools.partial(grads_kernel, rows, groups),
        "grads",
        [lengths, tap, conv, adj, up, key, val],
        [hbm] * 7,
        [jax.ShapeDtypeStruct(features.shape, BF16)],
        [hbm],
        [small]
        + near(9, extended, extended, extended, extended, extended)
        + [scratch(3 * rows), pltpu.VMEM((groups, 3, rows, GROUP), BF16), keep]
        + [sems(), sems(groups, 6), sems(groups, 3)],
    )
    mine = call(
        share_kernel,
        "share",
        [parts],
        [vmem],
        jax.ShapeDtypeStruct((sum_rows, LANES), BF16),
        vmem,
    )
    grad_taps, resid, skip = call(
        functools.partial(emit_kernel, groups, grad_scale),
        "emit",
        [lax.all_gather(mine, "dp")],
        [vmem],
        [
            jax.ShapeDtypeStruct((3, 3 * channels), F32),
            jax.ShapeDtypeStruct((poles, per_shard), F32),
            jax.ShapeDtypeStruct((1, per_shard), F32),
        ],
        [vmem] * 3,
        [pltpu.VMEM((sum_rows, LANES), F32)],
    )
    return grads, grad_taps, resid, skip.reshape(per_shard)


def solution(mesh):
    return jax.shard_map(
        per_device,
        mesh=mesh,
        in_specs=(
            P("dp", "ctx", None),
            P("dp", "ctx", None),
            P("dp", None),
            P(),
            P(None, "ctx"),
            P(None, "ctx"),
            P("ctx"),
        ),
        out_specs=(P("dp", "ctx", None), P(), P(None, "ctx"), P("ctx")),
        check_vma=False,
    )
```

```python
import functools
import math

import jax
import jax.numpy as jnp
from jax import lax
from jax.experimental import pallas as pl
from jax.experimental.pallas import tpu as pltpu
from jax.sharding import PartitionSpec as P

F32 = jnp.float32
BF16 = jnp.bfloat16
LANES = 128
SUB = 8
GROUP = SUB * LANES
HALO = 2


def shifted(block, axis, distance):
    count = lax.axis_size(axis)
    route = [(i - distance, i) for i in range(count) if 0 <= i - distance < count]
    return lax.ppermute(block, axis, route)


def vec(ref, index):
    return ref[pl.ds(pl.multiple_of(index * SUB, SUB), SUB), :]


def put(ref, index, value):
    ref[pl.ds(pl.multiple_of(index * SUB, SUB), SUB), :] = value


def spread(dst, first, src, column, row_count):
    for j in range(SUB):
        lanes = pl.ds(pl.multiple_of(column + j * LANES, LANES), LANES)
        dst[pl.ds(first * SUB + j, row_count, stride=SUB), :] = src[:, lanes].astype(F32)


def spread_rows(dst, first, src, row_count):
    def step(i, carry):
        for j in range(SUB):
            value = src[pl.ds(pl.multiple_of(i * 16, 16), 16), j * LANES : (j + 1) * LANES]
            dst[pl.ds((i * 16 + first) * SUB + j, 16, stride=SUB), :] = value.astype(F32)
        return carry

    lax.fori_loop(0, row_count // 16, step, 0)


def tiles_of(width):
    return max(1, width // LANES)


def start_kernel(
    log_rate, residues, skip_gain, features, upstream, out, edge, head,
    rates, coeffs, gains, low, high, high_up, slab, sems,
):
    rows = features.shape[1]
    copies = [
        pltpu.make_async_copy(source, target, sems.at[i])
        for i, (source, target) in enumerate(
            [
                (log_rate, rates),
                (residues, coeffs),
                (skip_gain, gains),
                (features.at[0, pl.ds(0, 16), :], low),
                (features.at[0, pl.ds(rows - 16, 16), :], high),
                (upstream.at[0, pl.ds(0, 16), :], high_up),
            ]
        )
    ]
    start_all(copies)
    poles, width = rates.shape
    per = tiles_of(width)
    slab[...] = jnp.zeros(slab.shape, F32)
    wait_all(copies[:3])
    for j in range(per):
        lanes = slice(j * LANES, min(width, (j + 1) * LANES))
        rate, gain = rates[:, lanes], gains[:, lanes]
        slab[pl.ds(j, poles, stride=per), :] = rounded(rate)
        slab[pl.ds(poles * per + j, poles, stride=per), :] = rate - rounded(rate)
        slab[pl.ds(2 * poles * per + j, poles, stride=per), :] = coeffs[:, lanes]
        slab[pl.ds(3 * poles * per + j, 1), :] = rounded(gain)
        slab[pl.ds((3 * poles + 1) * per + j, 1), :] = gain - rounded(gain)
    packed = slab[...].astype(BF16)
    for e in range(out.shape[0]):
        out[e] = packed
    wait_all(copies[3:])
    span = features.shape[2]
    for at in range(0, span, GROUP):
        lanes = slice(at, at + GROUP)
        head[:, lanes] = low[:, lanes].astype(F32)[:HALO].astype(BF16)
        edge[:, lanes] = high[:, lanes].astype(F32)[16 - HALO :].astype(BF16)
    for at in range(0, upstream.shape[2], GROUP):
        lanes = slice(at, at + GROUP)
        head[:, span + at : span + at + GROUP] = high_up[:, lanes].astype(F32)[:HALO].astype(BF16)


def spread_params(dst, par, slab, half, groups, poles):
    pieces, height, width = par.shape
    many = pieces // groups
    base = half * many
    joined = LANES // width
    per = height // (3 * poles)
    for k in range(many // joined):
        parts = [par[base + k * joined + i].astype(F32) for i in range(joined)]
        slab[...] = parts[0] if joined == 1 else jnp.concatenate(parts, axis=1)
        for j in range(per):
            to = k * per + j

            def rows_of(piece, count=poles):
                return slab[pl.ds(piece * per + j, count, stride=per), :]

            dst[pl.ds(to, poles, stride=SUB), :] = rows_of(0) + rows_of(poles)
            dst[pl.ds(poles * SUB + to, poles, stride=SUB), :] = rows_of(2 * poles)
            gain = rows_of(3 * poles, 1) + rows_of(3 * poles + 1, 1)
            dst[pl.ds(2 * poles * SUB + to, 1), :] = gain


def segment_starts(lengths):
    starts = [jnp.int32(0)]
    for j in range(lengths.shape[1]):
        starts.append(starts[-1] + lengths[0, j])
    return starts


def fill_keep(keep, starts, base, rows):
    count = rows + HALO + 2

    def step(i, carry):
        keep[i] = jnp.float32(1.0)
        return carry

    lax.fori_loop(0, count, step, 0, unroll=4)
    for start in starts:
        at = start - base + 1

        @pl.when((at >= 0) & (at < count))
        def _():
            keep[at] = jnp.float32(0.0)


def rounded(value):
    return value.astype(BF16).astype(F32)


def flag(condition):
    return jnp.where(condition, 1.0, 0.0).astype(F32)


def total_of(terms):
    terms = list(terms)
    while len(terms) > 1:
        odd = terms[-1:] if len(terms) % 2 else []
        terms = [x + y for x, y in zip(terms[::2], terms[1::2])] + odd
    return terms[0]


def unroll_of(trips):
    return max(d for d in range(1, 14) if trips % d == 0)


def featured(feat, tap, p, keep_one, keep_two):
    return (
        tap[0] * vec(feat, p + 2)
        + tap[1] * (keep_one * vec(feat, p + 1))
        + tap[2] * (keep_two * vec(feat, p))
    )


def each_group(groups, body):
    def step(half, carry):
        body(half)
        return carry

    lax.fori_loop(0, groups, step, 0)


def group_copies(sources, targets, sems, half):
    return [
        pltpu.make_async_copy(source.at[half], target.at[half], sems.at[half, i])
        for i, (source, target) in enumerate(zip(sources, targets))
    ]


def start_all(copies):
    for copy in copies:
        copy.start()


def wait_all(copies):
    for copy in copies:
        copy.wait()


def ends_kernel(
    rows, groups, far_lengths, features, upstream, left, right, taps, params,
    payload, feat_out, up_out, mixed_out, gout_out, par_out, tap_out, key_out, val_out,
    lengths, raw, raw_up, feat, up, mixed, gout, par, tap, key_scr, val_scr, stack, slab, zero_scr, keep,
    length_sem, in_sems, out_sems,
):
    me = lax.axis_index("ctx")
    base = me * rows
    count = payload.shape[0]
    poles = (par.shape[1] // SUB - 1) // 2
    extended = rows + HALO
    padded = rows + 2 * HALO
    get_lengths = pltpu.make_async_copy(far_lengths, lengths, length_sem)
    get_lengths.start()

    def arriving(half):
        lanes = [
            pl.ds(pl.multiple_of((third * groups + half) * GROUP, GROUP), GROUP)
            for third in range(3)
        ]
        return [
            pltpu.make_async_copy(
                features.at[0, :, lanes[third]], raw.at[half, third], in_sems.at[half, third]
            )
            for third in range(3)
        ] + [pltpu.make_async_copy(upstream.at[0, :, lanes[0]], raw_up.at[half], in_sems.at[half, 3])]

    near = [feat, up, tap, par, mixed, gout, key_scr, val_scr]
    far = [feat_out, up_out, tap_out, par_out, mixed_out, gout_out, key_out, val_out]

    each_group(groups, lambda half: start_all(arriving(half)))
    zero_scr[...] = jnp.zeros((SUB, LANES), F32)
    zeros = [zero_scr[...]] * poles

    def prepare(half):
        spread_params(par.at[half], params, slab, half, groups, poles)
        for third in range(3):
            column = (third * groups + half) * GROUP
            spread(feat.at[half], third * padded, left, column, HALO)
            spread(feat.at[half], third * padded + rows + HALO, right, column, HALO)
            spread(tap.at[half], third * 3, taps, column, 3)
        spread(up.at[half], rows, right, (3 * groups + half) * GROUP, HALO)

    each_group(groups, prepare)
    get_lengths.wait()
    starts = segment_starts(lengths)
    fill_keep(keep, starts, base, rows)
    low, high = jnp.int32(0), jnp.int32(extended)
    for start in starts:
        at = start - base
        low = jnp.where(at < rows, jnp.maximum(low, at), low)
        high = jnp.where(at > HALO, jnp.minimum(high, at), high)

    def group(half):
        incoming = arriving(half)
        outgoing = group_copies(near, far, out_sems, half)
        feat_h, up_h, mixed_h, gout_h = feat.at[half], up.at[half], mixed.at[half], gout.at[half]
        for third in range(3):
            incoming[third].wait()
            spread_rows(feat_h, third * padded + HALO, raw.at[half, third], rows)
        incoming[3].wait()
        spread_rows(up_h, 0, raw_up.at[half], rows)
        start_all(outgoing[:4])
        taps_h = [[vec(tap.at[half], third * 3 + j) for j in range(3)] for third in range(3)]

        def product(p, carry):
            keep_one = keep[p + 1]
            keep_two = keep_one * keep[p]
            query, key, val = (
                featured(feat_h, taps_h[third], third * padded + p, keep_one, keep_two)
                for third in range(3)
            )
            put(mixed_h, p, rounded(key * val))
            put(gout_h, p, rounded(vec(up_h, p) * query))
            put(key_scr.at[half], p, key)
            put(val_scr.at[half], p, val)
            return carry

        lax.fori_loop(0, extended, product, 0, unroll=unroll_of(extended))
        start_all(outgoing[4:])
        decay = [jnp.exp(-jnp.exp(vec(par.at[half], m))) for m in range(poles)]

        def sweep(i, carry):
            state, adjoint = carry
            back = extended - 1 - i
            x = vec(mixed_h, i) * flag(i >= low)
            g = vec(gout_h, back) * flag(back < high)
            state = [decay[m] * state[m] + x for m in range(poles)]
            adjoint = [decay[m] * adjoint[m] + g for m in range(poles)]
            return state, adjoint

        state, adjoint = lax.fori_loop(0, rows, sweep, (zeros, zeros), unroll=8)
        for m in range(0, poles, 2):
            at = slice(m * SUB, (m + 2) * SUB)
            stack[0, at, :] = jnp.concatenate(state[m : m + 2], axis=0).astype(BF16)
            stack[1, at, :] = jnp.concatenate(adjoint[m : m + 2], axis=0).astype(BF16)
        for e in range(count):
            payload[e, half] = stack[jnp.where(e >= me, 0, 1)]

    each_group(groups, group)
    each_group(groups, lambda half: wait_all(group_copies(near, far, out_sems, half)))


def local_kernel(
    rows, groups, far_lengths, mixed_in, gout_in, par_in, conv_out, adj_out, partial_out,
    lengths, mixed, gout, par, conv, adj, partial, zero_scr, keep,
    length_sem, in_sems, out_sems,
):
    poles = (par.shape[1] // SUB - 1) // 2
    extended = rows + HALO
    get_lengths = pltpu.make_async_copy(far_lengths, lengths, length_sem)
    get_lengths.start()
    far_in, near_in = [par_in, mixed_in, gout_in], [par, mixed, gout]
    near_out, far_out = [conv, adj, partial], [conv_out, adj_out, partial_out]
    each_group(groups, lambda half: start_all(group_copies(far_in, near_in, in_sems, half)))
    zero_scr[...] = jnp.zeros((SUB, LANES), F32)
    zero = zero_scr[...]
    per_pass = poles // 4
    zeros = [zero] * per_pass
    get_lengths.wait()
    fill_keep(keep, segment_starts(lengths), lax.axis_index("ctx") * rows, rows)

    def group(half):
        incoming = group_copies(far_in, near_in, in_sems, half)
        outgoing = group_copies(near_out, far_out, out_sems, half)
        mixed_h, gout_h, par_h = mixed.at[half], gout.at[half], par.at[half]
        conv_h, adj_h = conv.at[half], adj.at[half]
        wait_all(incoming)
        gain = vec(par_h, 2 * poles)
        for part in range(poles // per_pass):
            chosen = list(range(part * per_pass, (part + 1) * per_pass))
            decay = [jnp.exp(-jnp.exp(vec(par_h, m))) for m in chosen]
            coeff = [vec(par_h, poles + m) for m in chosen]

            def sweep(i, carry, inside=True):
                state, adjoint, resid, skip = carry
                back = extended - 1 - i
                x = vec(mixed_h, i)
                g = vec(gout_h, back)
                keep_fwd = keep[i + 1]
                keep_bwd = keep[back + 2]
                state = [decay[m] * (state[m] * keep_fwd) + x for m in range(per_pass)]
                adjoint = [decay[m] * (adjoint[m] * keep_bwd) + g for m in range(per_pass)]
                forward = total_of(coeff[m] * state[m] for m in range(per_pass))
                backward = total_of(coeff[m] * adjoint[m] for m in range(per_pass))
                if inside:
                    own = vec(mixed_h, back)
                    resid = [resid[m] + own * adjoint[m] for m in range(per_pass)]
                if part == 0:
                    put(conv_h, i, forward + gain * x)
                    put(adj_h, back, backward + gain * g)
                    if inside:
                        skip = skip + own * g
                else:
                    put(conv_h, i, forward + vec(conv_h, i))
                    put(adj_h, back, backward + vec(adj_h, back))
                return state, adjoint, resid, skip

            carry = (zeros, zeros, zeros, zero)
            for i in range(HALO):
                carry = sweep(i, carry, inside=False)
            _, _, resid, skip = lax.fori_loop(HALO, extended, sweep, carry, unroll=32)
            for i, m in enumerate(chosen):
                put(partial.at[half], m, resid[i])
            if part == 0:
                put(partial.at[half], poles, skip)
        start_all(outgoing)

    each_group(groups, group)
    each_group(groups, lambda half: wait_all(group_copies(near_out, far_out, out_sems, half)))


def posted_rows(keep, conv, adj, up, key, val):
    def posted(p):
        keep_one = keep[p + 1]
        keep_two = keep_one * keep[p]
        conv_out = rounded(vec(conv, p))
        grad_mixed = rounded(vec(adj, p))
        now = [vec(up, p) * conv_out, grad_mixed * vec(val, p), grad_mixed * vec(key, p)]
        return now, [keep_one * g for g in now], [keep_two * g for g in now]

    return posted


def sums_kernel(
    rows, groups, far_lengths, arrived, par_in, partial_in, conv_in, adj_in, up_in, key_in, val_in,
    feat_in, conv_out, adj_out, payload,
    lengths, par, partial, conv, adj, up, key, val, feat, before, after, sums, zero_scr, keep,
    length_sem, in_sems, out_sems,
):
    me = lax.axis_index("ctx")
    base = me * rows
    count = arrived.shape[0]
    poles = (par.shape[1] // SUB - 1) // 2
    extended = rows + HALO
    padded = rows + 2 * HALO
    get_lengths = pltpu.make_async_copy(far_lengths, lengths, length_sem)
    get_lengths.start()
    far = [par_in, partial_in, conv_in, adj_in, up_in, key_in, val_in, feat_in]
    near = [par, partial, conv, adj, up, key, val, feat]
    each_group(groups, lambda half: start_all(group_copies(far, near, in_sems, half)))
    zero_scr[...] = jnp.zeros((SUB, LANES), F32)
    zero = zero_scr[...]
    get_lengths.wait()
    starts = segment_starts(lengths)
    fill_keep(keep, starts, base, rows)
    until, since = jnp.int32(extended), jnp.int32(0)
    first, last, newest = jnp.int32(0), jnp.int32(2**30), jnp.int32(0)
    for start in starts:
        at = start - base
        until = jnp.where(at >= 0, jnp.minimum(until, at), until)
        since = jnp.where(at <= extended, jnp.maximum(since, at), since)
        first = jnp.where(at <= 0, jnp.maximum(first, start), first)
        last = jnp.where(at > extended, jnp.minimum(last, start), last)
        newest = jnp.where(at <= extended, jnp.maximum(newest, start), newest)
    steps = jnp.maximum(until, extended - since)
    through = flag(newest < base + rows)
    chunk = unroll_of(extended)

    def group(half):
        incoming = group_copies(far, near, in_sems, half)
        outgoing = group_copies([conv, adj], [conv_out, adj_out], out_sems, half)
        par_h, partial_h, conv_h, adj_h = par.at[half], partial.at[half], conv.at[half], adj.at[half]
        feat_h = feat.at[half]
        wait_all(incoming[:2])
        per_pass = poles // 2
        zeros = [zero] * per_pass
        for part in range(2):
            chosen = list(range(part * per_pass, (part + 1) * per_pass))
            rate = [jnp.exp(vec(par_h, m)) for m in chosen]
            block = [jnp.exp(-rows * r) for r in rate]

            def arrived_states(d):
                got = []
                for m in range(chosen[0], chosen[-1] + 1, 2):
                    pair = arrived[d, half, m * SUB : (m + 2) * SUB, :].astype(F32)
                    got += [pair[:SUB], pair[SUB:]]
                return got

            def from_before(d, carry):
                joined = flag((d + 1) * rows - 1 >= first)
                got = arrived_states(d)
                return [block[i] * carry[i] + joined * got[i] for i in range(per_pass)]

            def from_after(i, carry):
                d = count - 1 - i
                joined = flag(d * rows + HALO < last)
                got = arrived_states(d)
                return [block[i] * carry[i] + joined * got[i] for i in range(per_pass)]

            state = lax.fori_loop(0, me, from_before, zeros)
            adjoint = lax.fori_loop(0, count - 1 - me, from_after, zeros)
            own = arrived_states(me)
            for i, m in enumerate(chosen):
                scale = vec(par_h, poles + m) * jnp.exp(-rate[i])
                put(before, m, scale * state[i])
                put(after, m, scale * adjoint[i])
                cross = jnp.exp(-(HALO + 1) * rate[i]) * (adjoint[i] * through)
                put(sums, (9 + m) * groups + half, vec(partial_h, m) + cross * own[i])
        put(sums, (9 + poles) * groups + half, vec(partial_h, poles))
        decay = [jnp.exp(-jnp.exp(vec(par_h, m))) for m in range(poles)]
        enter = [vec(before, m) for m in range(poles)]
        leave = [vec(after, m) for m in range(poles)]
        wait_all(incoming[2:4])

        def carried(i, carry):
            enter, leave = carry
            for step in range(chunk):
                p = chunk * i + step
                back = extended - 1 - p
                put(conv_h, p, vec(conv_h, p) + flag(p < until) * total_of(enter))
                put(adj_h, back, vec(adj_h, back) + flag(back >= since) * total_of(leave))
                enter = [decay[m] * enter[m] for m in range(poles)]
                leave = [decay[m] * leave[m] for m in range(poles)]
            return enter, leave

        lax.fori_loop(0, (steps + chunk - 1) // chunk, carried, (enter, leave))
        start_all(outgoing)
        wait_all(incoming[4:])
        posted = posted_rows(keep, conv_h, adj_h, up.at[half], key.at[half], val.at[half])

        def tap_terms(i, carry):
            tap_sums, feat_now, feat_one = carry
            p = rows - 1 - i
            now, masked_one, masked_two = posted(p)
            feat_two = [vec(feat_h, third * padded + p) for third in range(3)]
            new_sums = []
            for third in range(3):
                new_sums += [
                    tap_sums[3 * third] + now[third] * feat_now[third],
                    tap_sums[3 * third + 1] + masked_one[third] * feat_one[third],
                    tap_sums[3 * third + 2] + masked_two[third] * feat_two[third],
                ]
            return new_sums, feat_one, feat_two

        feat_last = [vec(feat_h, third * padded + rows + 1) for third in range(3)]
        feat_before = [vec(feat_h, third * padded + rows) for third in range(3)]
        tap_sums, _, _ = lax.fori_loop(
            0, rows, tap_terms, ([zero] * 9, feat_last, feat_before), unroll=4
        )
        for third in range(3):
            for j in range(3):
                put(sums, (3 * j + third) * groups + half, tap_sums[3 * third + j])

    each_group(groups, group)
    width = groups * SUB
    same = 9 * width
    tap_sums = sums[0:same, :].astype(BF16)
    columns = (payload.shape[1] - same) // 16
    for e in range(count):
        payload[e, 0:same, :] = tap_sums
        first_row = same + (e * width) // count
        for j in range(columns):
            value = sums[pl.ds(first_row + j, 16, stride=width), :]
            payload[e, same + 16 * j : same + 16 * (j + 1), :] = value.astype(BF16)
        last_row = first_row + poles * width
        payload[e, same + 16 * columns :, :] = sums[last_row : last_row + SUB, :].astype(BF16)
    each_group(
        groups,
        lambda half: wait_all(group_copies([conv, adj], [conv_out, adj_out], out_sems, half)),
    )


def grads_kernel(
    rows, groups, far_lengths, tap_in, conv_in, adj_in, up_in, key_in, val_in, grads,
    lengths, tap, conv, adj, up, key, val, post, ready, keep, length_sem, in_sems, out_sems,
):
    extended = rows + HALO
    get_lengths = pltpu.make_async_copy(far_lengths, lengths, length_sem)
    get_lengths.start()
    far = [tap_in, conv_in, adj_in, up_in, key_in, val_in]
    near = [tap, conv, adj, up, key, val]
    each_group(groups, lambda half: start_all(group_copies(far, near, in_sems, half)))

    def leaving(half):
        return [
            pltpu.make_async_copy(
                ready.at[half, third],
                grads.at[
                    0, :, pl.ds(pl.multiple_of((third * groups + half) * GROUP, GROUP), GROUP)
                ],
                out_sems.at[half, third],
            )
            for third in range(3)
        ]

    get_lengths.wait()
    fill_keep(keep, segment_starts(lengths), lax.axis_index("ctx") * rows, rows)

    def group(half):
        wait_all(group_copies(far, near, in_sems, half))
        taps_h = [[vec(tap.at[half], third * 3 + j) for j in range(3)] for third in range(3)]
        posted = posted_rows(
            keep, conv.at[half], adj.at[half], up.at[half], key.at[half], val.at[half]
        )
        _, _, far_two = posted(extended - 1)
        _, near_one, near_two = posted(extended - 2)

        def transposed(i, carry):
            one, two, three = carry
            p = rows - 1 - i
            now, masked_one, masked_two = posted(p)
            for third in range(3):
                back = (
                    taps_h[third][0] * now[third]
                    + taps_h[third][1] * one[third]
                    + taps_h[third][2] * three[third]
                )
                put(post, third * rows + p, back)
            return masked_one, masked_two, two

        lax.fori_loop(0, rows, transposed, (near_one, near_two, far_two), unroll=4)

        def write(i, carry):
            for third in range(3):
                for j in range(SUB):
                    value = post[pl.ds((third * rows + i * 16) * SUB + j, 16, stride=SUB), :]
                    lanes = slice(j * LANES, (j + 1) * LANES)
                    ready[half, third, pl.ds(pl.multiple_of(i * 16, 16), 16), lanes] = value.astype(
                        BF16
                    )
            return carry

        lax.fori_loop(0, rows // 16, write, 0, unroll=2)
        start_all(leaving(half))

    each_group(groups, group)
    each_group(groups, lambda half: wait_all(leaving(half)))


def share_kernel(parts, out):
    mine = parts[0].astype(F32)
    for k in range(1, parts.shape[0]):
        mine = mine + parts[k].astype(F32)
    out[...] = mine.astype(BF16)


def emit_kernel(groups, scale, shares, grad_taps, resid, skip, whole):
    me = lax.axis_index("ctx")
    width = groups * SUB
    poles, per_shard = resid.shape
    mine = shares[0].astype(F32)
    for k in range(1, shares.shape[0]):
        mine = mine + shares[k].astype(F32)
    whole[...] = mine * scale
    for k in range(3 * width):
        grad_taps[:, k * LANES : (k + 1) * LANES] = whole[pl.ds(k, 3, stride=3 * width), :]
    first = 9 * width
    columns = (whole.shape[0] - first) // 16
    last = first + 16 * columns
    if per_shard >= LANES:
        for j in range(columns):
            lanes = slice(j * LANES, (j + 1) * LANES)
            resid[:, lanes] = whole[first + 16 * j : first + 16 * (j + 1), :]
            skip[:, lanes] = whole[last + j : last + j + 1, :]
    else:
        per = LANES // per_shard
        rows = whole[first : first + 16, :]
        final = whole[last : last + 1, :]
        place = lax.rem(me, per)
        chosen, chosen_last = rows[:, :per_shard], final[:, :per_shard]
        for i in range(1, per):
            lanes = slice(i * per_shard, (i + 1) * per_shard)
            chosen = jnp.where(place == i, rows[:, lanes], chosen)
            chosen_last = jnp.where(place == i, final[:, lanes], chosen_last)
        resid[...] = chosen
        skip[...] = chosen_last


def swap(block, axes):
    return lax.all_to_all(block, axes, split_axis=0, concat_axis=0, tiled=True)


def per_device(features, upstream, lengths, conv_taps, residues, log_rate, skip_gain):
    rows = features.shape[1]
    channels = upstream.shape[2]
    poles = residues.shape[0]
    ctx_count = lax.axis_size("ctx")
    total = ctx_count * lax.axis_size("dp")
    per_shard = channels // ctx_count
    groups = channels // GROUP
    grad_scale = 1.0 / math.sqrt(rows * total)
    extended = rows + HALO
    padded = rows + 2 * HALO
    state_rows = poles * SUB
    limits = pltpu.CompilerParams(vmem_limit_bytes=40 * 1024 * 1024)
    hbm = pl.BlockSpec(memory_space=pltpu.HBM)
    vmem = pl.BlockSpec(memory_space=pltpu.VMEM)

    def tall(height):
        return jax.ShapeDtypeStruct((groups, height * SUB, LANES), F32)

    def near(*heights):
        return [pltpu.VMEM((groups, height * SUB, LANES), F32) for height in heights]

    def scratch(height):
        return pltpu.VMEM((height * SUB, LANES), F32)

    def sems(*shape):
        return pltpu.SemaphoreType.DMA(shape)

    keep = pltpu.SMEM((rows + 8,), F32)
    small = pltpu.SMEM(lengths.shape, jnp.int32)

    def call(kernel, name, ins, in_specs, outs, out_specs, scratch_shapes=()):
        ins = [
            pltpu.with_memory_space_constraint(x, pltpu.HBM) if spec is hbm else x
            for x, spec in zip(ins, in_specs)
        ]
        if isinstance(outs, list):
            outs = [
                pltpu.HBM(out.shape, out.dtype) if spec is hbm else out
                for out, spec in zip(outs, out_specs)
            ]
        return pl.pallas_call(
            kernel,
            out_shape=outs,
            in_specs=in_specs,
            out_specs=out_specs,
            scratch_shapes=list(scratch_shapes),
            compiler_params=limits,
            name=name,
        )(*ins)

    block_rows = (3 * poles + 2) * tiles_of(per_shard)
    block = (-(-block_rows // SUB) * SUB, min(per_shard, LANES))
    span = features.shape[2]
    params, edge, head = call(
        start_kernel,
        "start",
        [log_rate, residues, skip_gain[None], features, upstream],
        [hbm] * 5,
        [
            jax.ShapeDtypeStruct((ctx_count,) + block, BF16),
            jax.ShapeDtypeStruct((HALO, span), BF16),
            jax.ShapeDtypeStruct((HALO, span + channels), BF16),
        ],
        [vmem] * 3,
        [
            pltpu.VMEM((poles, per_shard), F32),
            pltpu.VMEM((poles, per_shard), F32),
            pltpu.VMEM((1, per_shard), F32),
            pltpu.VMEM((16, span), BF16),
            pltpu.VMEM((16, span), BF16),
            pltpu.VMEM((16, channels), BF16),
            pltpu.VMEM(block, F32),
            sems(6),
        ],
    )
    params = swap(params, "ctx")
    left = shifted(edge, "ctx", 1)
    right = shifted(head, "ctx", -1)

    payload, feat, up, mixed, gout, par, tap, key, val = call(
        functools.partial(ends_kernel, rows, groups),
        "ends",
        [lengths, features, upstream, left, right, conv_taps, params],
        [hbm] * 3 + [vmem] * 4,
        [jax.ShapeDtypeStruct((ctx_count, groups, state_rows, LANES), BF16)]
        + [tall(height) for height in [3 * padded] + [extended] * 3 + [2 * poles + 1, 9]]
        + [tall(extended)] * 2,
        [vmem] + [hbm] * 8,
        [
            small,
            pltpu.VMEM((groups, 3, rows, GROUP), BF16),
            pltpu.VMEM((groups, rows, GROUP), BF16),
        ]
        + near(3 * padded, extended, extended, extended, 2 * poles + 1, 9, extended, extended)
        + [pltpu.VMEM((2, state_rows, LANES), BF16)]
        + [pltpu.VMEM((block[0], LANES), F32), scratch(1), keep]
        + [sems(), sems(groups, 4), sems(groups, 8)],
    )
    arrived = swap(payload, "ctx")
    conv, adj, partial = call(
        functools.partial(local_kernel, rows, groups),
        "local",
        [lengths, mixed, gout, par],
        [hbm] * 4,
        [tall(extended)] * 2 + [tall(poles + 1)],
        [hbm] * 3,
        [small]
        + near(extended, extended, 2 * poles + 1, extended, extended, poles + 1)
        + [scratch(1), keep, sems(), sems(groups, 3), sems(groups, 3)],
    )
    used = (10 + poles) * groups * SUB
    sum_rows = 9 * groups * SUB + 16 * tiles_of(per_shard) + SUB
    conv, adj, sums = call(
        functools.partial(sums_kernel, rows, groups),
        "sums",
        [lengths, arrived, par, partial, conv, adj, up, key, val, feat],
        [hbm, vmem] + [hbm] * 8,
        [tall(extended)] * 2 + [jax.ShapeDtypeStruct((ctx_count, sum_rows, LANES), BF16)],
        [hbm, hbm, vmem],
        [small]
        + near(2 * poles + 1, poles + 1, extended, extended, extended, extended, extended)
        + near(3 * padded)
        + [scratch(poles), scratch(poles)]
        + [pltpu.VMEM((used + 16, LANES), F32), scratch(1), keep]
        + [sems(), sems(groups, 8), sems(groups, 2)],
    )
    parts = swap(sums, "ctx")
    (grads,) = call(
        functools.partial(grads_kernel, rows, groups),
        "grads",
        [lengths, tap, conv, adj, up, key, val],
        [hbm] * 7,
        [jax.ShapeDtypeStruct(features.shape, BF16)],
        [hbm],
        [small]
        + near(9, extended, extended, extended, extended, extended)
        + [scratch(3 * rows), pltpu.VMEM((groups, 3, rows, GROUP), BF16), keep]
        + [sems(), sems(groups, 6), sems(groups, 3)],
    )
    mine = call(
        share_kernel,
        "share",
        [parts],
        [vmem],
        jax.ShapeDtypeStruct((sum_rows, LANES), BF16),
        vmem,
    )
    grad_taps, resid, skip = call(
        functools.partial(emit_kernel, groups, grad_scale),
        "emit",
        [lax.all_gather(mine, "dp")],
        [vmem],
        [
            jax.ShapeDtypeStruct((3, 3 * channels), F32),
            jax.ShapeDtypeStruct((poles, per_shard), F32),
            jax.ShapeDtypeStruct((1, per_shard), F32),
        ],
        [vmem] * 3,
        [pltpu.VMEM((sum_rows, LANES), F32)],
    )
    return grads, grad_taps, resid, skip.reshape(per_shard)


def solution(mesh):
    return jax.shard_map(
        per_device,
        mesh=mesh,
        in_specs=(
            P("dp", "ctx", None),
            P("dp", "ctx", None),
            P("dp", None),
            P(),
            P(None, "ctx"),
            P(None, "ctx"),
            P("ctx"),
        ),
        out_specs=(P("dp", "ctx", None), P(), P(None, "ctx"), P("ctx")),
        check_vma=False,
    )
```

```python
import functools
import math

import jax
import jax.numpy as jnp
from jax import lax
from jax.experimental import pallas as pl
from jax.experimental.pallas import tpu as pltpu
from jax.sharding import PartitionSpec as P

F32 = jnp.float32
BF16 = jnp.bfloat16
LANES = 128
SUB = 8
GROUP = SUB * LANES
HALO = 2


def shifted(block, axis, distance):
    count = lax.axis_size(axis)
    route = [(i - distance, i) for i in range(count) if 0 <= i - distance < count]
    return lax.ppermute(block, axis, route)


def vec(ref, index):
    return ref[pl.ds(pl.multiple_of(index * SUB, SUB), SUB), :]


def put(ref, index, value):
    ref[pl.ds(pl.multiple_of(index * SUB, SUB), SUB), :] = value


def spread(dst, first, src, column, row_count):
    for j in range(SUB):
        lanes = pl.ds(pl.multiple_of(column + j * LANES, LANES), LANES)
        dst[pl.ds(first * SUB + j, row_count, stride=SUB), :] = src[:, lanes].astype(F32)


def spread_rows(dst, first, src, row_count):
    def step(i, carry):
        for j in range(SUB):
            value = src[pl.ds(pl.multiple_of(i * 16, 16), 16), j * LANES : (j + 1) * LANES]
            dst[pl.ds((i * 16 + first) * SUB + j, 16, stride=SUB), :] = value.astype(F32)
        return carry

    lax.fori_loop(0, row_count // 16, step, 0)


def tiles_of(width):
    return max(1, width // LANES)


def start_kernel(
    log_rate, residues, skip_gain, features, upstream, out, edge, head,
    rates, coeffs, gains, low, high, high_up, slab, sems,
):
    rows = features.shape[1]
    copies = [
        pltpu.make_async_copy(source, target, sems.at[i])
        for i, (source, target) in enumerate(
            [
                (log_rate, rates),
                (residues, coeffs),
                (skip_gain, gains),
                (features.at[0, pl.ds(0, 16), :], low),
                (features.at[0, pl.ds(rows - 16, 16), :], high),
                (upstream.at[0, pl.ds(0, 16), :], high_up),
            ]
        )
    ]
    start_all(copies)
    poles, width = rates.shape
    per = tiles_of(width)
    slab[...] = jnp.zeros(slab.shape, F32)
    wait_all(copies[:3])
    for j in range(per):
        lanes = slice(j * LANES, min(width, (j + 1) * LANES))
        rate, gain = rates[:, lanes], gains[:, lanes]
        slab[pl.ds(j, poles, stride=per), :] = rounded(rate)
        slab[pl.ds(poles * per + j, poles, stride=per), :] = rate - rounded(rate)
        slab[pl.ds(2 * poles * per + j, poles, stride=per), :] = coeffs[:, lanes]
        slab[pl.ds(3 * poles * per + j, 1), :] = rounded(gain)
        slab[pl.ds((3 * poles + 1) * per + j, 1), :] = gain - rounded(gain)
    packed = slab[...].astype(BF16)
    for e in range(out.shape[0]):
        out[e] = packed
    wait_all(copies[3:])
    span = features.shape[2]
    for at in range(0, span, GROUP):
        lanes = slice(at, at + GROUP)
        head[:, lanes] = low[:, lanes].astype(F32)[:HALO].astype(BF16)
        edge[:, lanes] = high[:, lanes].astype(F32)[16 - HALO :].astype(BF16)
    for at in range(0, upstream.shape[2], GROUP):
        lanes = slice(at, at + GROUP)
        head[:, span + at : span + at + GROUP] = high_up[:, lanes].astype(F32)[:HALO].astype(BF16)


def spread_params(dst, par, slab, half, groups, poles):
    pieces, height, width = par.shape
    many = pieces // groups
    base = half * many
    joined = LANES // width
    per = height // (3 * poles)
    for k in range(many // joined):
        parts = [par[base + k * joined + i].astype(F32) for i in range(joined)]
        slab[...] = parts[0] if joined == 1 else jnp.concatenate(parts, axis=1)
        for j in range(per):
            to = k * per + j

            def rows_of(piece, count=poles):
                return slab[pl.ds(piece * per + j, count, stride=per), :]

            dst[pl.ds(to, poles, stride=SUB), :] = rows_of(0) + rows_of(poles)
            dst[pl.ds(poles * SUB + to, poles, stride=SUB), :] = rows_of(2 * poles)
            gain = rows_of(3 * poles, 1) + rows_of(3 * poles + 1, 1)
            dst[pl.ds(2 * poles * SUB + to, 1), :] = gain


def segment_starts(lengths):
    starts = [jnp.int32(0)]
    for j in range(lengths.shape[1]):
        starts.append(starts[-1] + lengths[0, j])
    return starts


def fill_keep(keep, starts, base, rows):
    count = rows + HALO + 2

    def step(i, carry):
        keep[i] = jnp.float32(1.0)
        return carry

    lax.fori_loop(0, count, step, 0, unroll=4)
    for start in starts:
        at = start - base + 1

        @pl.when((at >= 0) & (at < count))
        def _():
            keep[at] = jnp.float32(0.0)


def rounded(value):
    return value.astype(BF16).astype(F32)


def flag(condition):
    return jnp.where(condition, 1.0, 0.0).astype(F32)


def total_of(terms):
    terms = list(terms)
    while len(terms) > 1:
        odd = terms[-1:] if len(terms) % 2 else []
        terms = [x + y for x, y in zip(terms[::2], terms[1::2])] + odd
    return terms[0]


def unroll_of(trips):
    return max(d for d in range(1, 14) if trips % d == 0)


def featured(feat, tap, p, keep_one, keep_two):
    return (
        tap[0] * vec(feat, p + 2)
        + tap[1] * (keep_one * vec(feat, p + 1))
        + tap[2] * (keep_two * vec(feat, p))
    )


def each_group(groups, body):
    def step(half, carry):
        body(half)
        return carry

    lax.fori_loop(0, groups, step, 0)


def group_copies(sources, targets, sems, half):
    return [
        pltpu.make_async_copy(source.at[half], target.at[half], sems.at[half, i])
        for i, (source, target) in enumerate(zip(sources, targets))
    ]


def start_all(copies):
    for copy in copies:
        copy.start()


def wait_all(copies):
    for copy in copies:
        copy.wait()


def features_kernel(
    rows, groups, far_lengths, features, upstream, left, right, taps,
    mixed, gout, feat_out, up_out, mixed_out, gout_out, tap_out, key_out, val_out,
    lengths, raw, raw_up, feat, up, tap, key_scr, val_scr, keep,
    length_sem, in_sems, out_sems,
):
    extended = rows + HALO
    padded = rows + 2 * HALO
    get_lengths = pltpu.make_async_copy(far_lengths, lengths, length_sem)
    get_lengths.start()

    def arriving(half):
        lanes = [
            pl.ds(pl.multiple_of((third * groups + half) * GROUP, GROUP), GROUP)
            for third in range(3)
        ]
        return [
            pltpu.make_async_copy(
                features.at[0, :, lanes[third]], raw.at[half, third], in_sems.at[half, third]
            )
            for third in range(3)
        ] + [pltpu.make_async_copy(upstream.at[0, :, lanes[0]], raw_up.at[half], in_sems.at[half, 3])]

    near = [feat, up, tap, mixed, gout, key_scr, val_scr]
    far = [feat_out, up_out, tap_out, mixed_out, gout_out, key_out, val_out]

    each_group(groups, lambda half: start_all(arriving(half)))

    def prepare(half):
        for third in range(3):
            column = (third * groups + half) * GROUP
            spread(feat.at[half], third * padded, left, column, HALO)
            spread(feat.at[half], third * padded + rows + HALO, right, column, HALO)
            spread(tap.at[half], third * 3, taps, column, 3)
        spread(up.at[half], rows, right, (3 * groups + half) * GROUP, HALO)

    each_group(groups, prepare)
    get_lengths.wait()
    fill_keep(keep, segment_starts(lengths), lax.axis_index("ctx") * rows, rows)

    def group(half):
        incoming = arriving(half)
        outgoing = group_copies(near, far, out_sems, half)
        feat_h, up_h, mixed_h, gout_h = feat.at[half], up.at[half], mixed.at[half], gout.at[half]
        for third in range(3):
            incoming[third].wait()
            spread_rows(feat_h, third * padded + HALO, raw.at[half, third], rows)
        incoming[3].wait()
        spread_rows(up_h, 0, raw_up.at[half], rows)
        start_all(outgoing[:3])
        taps_h = [[vec(tap.at[half], third * 3 + j) for j in range(3)] for third in range(3)]

        def product(p, carry):
            keep_one = keep[p + 1]
            keep_two = keep_one * keep[p]
            query, key, val = (
                featured(feat_h, taps_h[third], third * padded + p, keep_one, keep_two)
                for third in range(3)
            )
            put(mixed_h, p, rounded(key * val))
            put(gout_h, p, rounded(vec(up_h, p) * query))
            put(key_scr.at[half], p, key)
            put(val_scr.at[half], p, val)
            return carry

        lax.fori_loop(0, extended, product, 0, unroll=unroll_of(extended))
        start_all(outgoing[3:])

    each_group(groups, group)
    each_group(groups, lambda half: wait_all(group_copies(near, far, out_sems, half)))


def ends_kernel(
    rows, groups, far_lengths, params, mixed, gout, payload, par_out,
    lengths, par, stack, slab, zero_scr, length_sem, out_sems,
):
    me = lax.axis_index("ctx")
    base = me * rows
    count = payload.shape[0]
    poles = (par.shape[1] // SUB - 1) // 2
    extended = rows + HALO
    get_lengths = pltpu.make_async_copy(far_lengths, lengths, length_sem)
    get_lengths.start()
    zero_scr[...] = jnp.zeros((SUB, LANES), F32)
    zeros = [zero_scr[...]] * poles

    def prepare(half):
        spread_params(par.at[half], params, slab, half, groups, poles)
        start_all(group_copies([par], [par_out], out_sems, half))

    each_group(groups, prepare)
    get_lengths.wait()
    low, high = jnp.int32(0), jnp.int32(extended)
    for start in segment_starts(lengths):
        at = start - base
        low = jnp.where(at < rows, jnp.maximum(low, at), low)
        high = jnp.where(at > HALO, jnp.minimum(high, at), high)

    def group(half):
        mixed_h, gout_h = mixed.at[half], gout.at[half]
        decay = [jnp.exp(-jnp.exp(vec(par.at[half], m))) for m in range(poles)]

        def sweep(i, carry):
            state, adjoint = carry
            back = extended - 1 - i
            x = vec(mixed_h, i) * flag(i >= low)
            g = vec(gout_h, back) * flag(back < high)
            state = [decay[m] * state[m] + x for m in range(poles)]
            adjoint = [decay[m] * adjoint[m] + g for m in range(poles)]
            return state, adjoint

        state, adjoint = lax.fori_loop(0, rows, sweep, (zeros, zeros), unroll=8)
        for m in range(0, poles, 2):
            at = slice(m * SUB, (m + 2) * SUB)
            stack[0, at, :] = jnp.concatenate(state[m : m + 2], axis=0).astype(BF16)
            stack[1, at, :] = jnp.concatenate(adjoint[m : m + 2], axis=0).astype(BF16)
        for e in range(count):
            payload[e, half] = stack[jnp.where(e >= me, 0, 1)]

    each_group(groups, group)
    each_group(groups, lambda half: wait_all(group_copies([par], [par_out], out_sems, half)))


def local_kernel(
    rows, groups, far_lengths, mixed_in, gout_in, par_in, conv_out, adj_out, partial_out,
    lengths, mixed, gout, par, conv, adj, partial, zero_scr, keep,
    length_sem, in_sems, out_sems,
):
    poles = (par.shape[1] // SUB - 1) // 2
    extended = rows + HALO
    get_lengths = pltpu.make_async_copy(far_lengths, lengths, length_sem)
    get_lengths.start()
    far_in, near_in = [par_in, mixed_in, gout_in], [par, mixed, gout]
    near_out, far_out = [conv, adj, partial], [conv_out, adj_out, partial_out]
    each_group(groups, lambda half: start_all(group_copies(far_in, near_in, in_sems, half)))
    zero_scr[...] = jnp.zeros((SUB, LANES), F32)
    zero = zero_scr[...]
    per_pass = poles // 4
    zeros = [zero] * per_pass
    get_lengths.wait()
    fill_keep(keep, segment_starts(lengths), lax.axis_index("ctx") * rows, rows)

    def group(half):
        incoming = group_copies(far_in, near_in, in_sems, half)
        outgoing = group_copies(near_out, far_out, out_sems, half)
        mixed_h, gout_h, par_h = mixed.at[half], gout.at[half], par.at[half]
        conv_h, adj_h = conv.at[half], adj.at[half]
        wait_all(incoming)
        gain = vec(par_h, 2 * poles)
        for part in range(poles // per_pass):
            chosen = list(range(part * per_pass, (part + 1) * per_pass))
            decay = [jnp.exp(-jnp.exp(vec(par_h, m))) for m in chosen]
            coeff = [vec(par_h, poles + m) for m in chosen]

            def sweep(i, carry, inside=True):
                state, adjoint, resid, skip = carry
                back = extended - 1 - i
                x = vec(mixed_h, i)
                g = vec(gout_h, back)
                keep_fwd = keep[i + 1]
                keep_bwd = keep[back + 2]
                state = [decay[m] * (state[m] * keep_fwd) + x for m in range(per_pass)]
                adjoint = [decay[m] * (adjoint[m] * keep_bwd) + g for m in range(per_pass)]
                forward = total_of(coeff[m] * state[m] for m in range(per_pass))
                backward = total_of(coeff[m] * adjoint[m] for m in range(per_pass))
                if inside:
                    own = vec(mixed_h, back)
                    resid = [resid[m] + own * adjoint[m] for m in range(per_pass)]
                if part == 0:
                    put(conv_h, i, forward + gain * x)
                    put(adj_h, back, backward + gain * g)
                    if inside:
                        skip = skip + own * g
                else:
                    put(conv_h, i, forward + vec(conv_h, i))
                    put(adj_h, back, backward + vec(adj_h, back))
                return state, adjoint, resid, skip

            carry = (zeros, zeros, zeros, zero)
            for i in range(HALO):
                carry = sweep(i, carry, inside=False)
            _, _, resid, skip = lax.fori_loop(HALO, extended, sweep, carry, unroll=32)
            for i, m in enumerate(chosen):
                put(partial.at[half], m, resid[i])
            if part == 0:
                put(partial.at[half], poles, skip)
        start_all(outgoing)

    each_group(groups, group)
    each_group(groups, lambda half: wait_all(group_copies(near_out, far_out, out_sems, half)))


def posted_rows(keep, conv, adj, up, key, val):
    def posted(p):
        keep_one = keep[p + 1]
        keep_two = keep_one * keep[p]
        conv_out = rounded(vec(conv, p))
        grad_mixed = rounded(vec(adj, p))
        now = [vec(up, p) * conv_out, grad_mixed * vec(val, p), grad_mixed * vec(key, p)]
        return now, [keep_one * g for g in now], [keep_two * g for g in now]

    return posted


def sums_kernel(
    rows, groups, far_lengths, arrived, par_in, partial_in, conv_in, adj_in, up_in, key_in, val_in,
    feat_in, conv_out, adj_out, payload,
    lengths, par, partial, conv, adj, up, key, val, feat, before, after, sums, zero_scr, keep,
    length_sem, in_sems, out_sems,
):
    me = lax.axis_index("ctx")
    base = me * rows
    count = arrived.shape[0]
    poles = (par.shape[1] // SUB - 1) // 2
    extended = rows + HALO
    padded = rows + 2 * HALO
    get_lengths = pltpu.make_async_copy(far_lengths, lengths, length_sem)
    get_lengths.start()
    far = [par_in, partial_in, conv_in, adj_in, up_in, key_in, val_in, feat_in]
    near = [par, partial, conv, adj, up, key, val, feat]
    each_group(groups, lambda half: start_all(group_copies(far, near, in_sems, half)))
    zero_scr[...] = jnp.zeros((SUB, LANES), F32)
    zero = zero_scr[...]
    get_lengths.wait()
    starts = segment_starts(lengths)
    fill_keep(keep, starts, base, rows)
    until, since = jnp.int32(extended), jnp.int32(0)
    first, last, newest = jnp.int32(0), jnp.int32(2**30), jnp.int32(0)
    for start in starts:
        at = start - base
        until = jnp.where(at >= 0, jnp.minimum(until, at), until)
        since = jnp.where(at <= extended, jnp.maximum(since, at), since)
        first = jnp.where(at <= 0, jnp.maximum(first, start), first)
        last = jnp.where(at > extended, jnp.minimum(last, start), last)
        newest = jnp.where(at <= extended, jnp.maximum(newest, start), newest)
    steps = jnp.maximum(until, extended - since)
    through = flag(newest < base + rows)
    chunk = unroll_of(extended)

    def group(half):
        incoming = group_copies(far, near, in_sems, half)
        outgoing = group_copies([conv, adj], [conv_out, adj_out], out_sems, half)
        par_h, partial_h, conv_h, adj_h = par.at[half], partial.at[half], conv.at[half], adj.at[half]
        feat_h = feat.at[half]
        wait_all(incoming[:2])
        per_pass = poles // 2
        zeros = [zero] * per_pass
        for part in range(2):
            chosen = list(range(part * per_pass, (part + 1) * per_pass))
            rate = [jnp.exp(vec(par_h, m)) for m in chosen]
            block = [jnp.exp(-rows * r) for r in rate]

            def arrived_states(d):
                got = []
                for m in range(chosen[0], chosen[-1] + 1, 2):
                    pair = arrived[d, half, m * SUB : (m + 2) * SUB, :].astype(F32)
                    got += [pair[:SUB], pair[SUB:]]
                return got

            def from_before(d, carry):
                joined = flag((d + 1) * rows - 1 >= first)
                got = arrived_states(d)
                return [block[i] * carry[i] + joined * got[i] for i in range(per_pass)]

            def from_after(i, carry):
                d = count - 1 - i
                joined = flag(d * rows + HALO < last)
                got = arrived_states(d)
                return [block[i] * carry[i] + joined * got[i] for i in range(per_pass)]

            state = lax.fori_loop(0, me, from_before, zeros)
            adjoint = lax.fori_loop(0, count - 1 - me, from_after, zeros)
            own = arrived_states(me)
            for i, m in enumerate(chosen):
                scale = vec(par_h, poles + m) * jnp.exp(-rate[i])
                put(before, m, scale * state[i])
                put(after, m, scale * adjoint[i])
                cross = jnp.exp(-(HALO + 1) * rate[i]) * (adjoint[i] * through)
                put(sums, (9 + m) * groups + half, vec(partial_h, m) + cross * own[i])
        put(sums, (9 + poles) * groups + half, vec(partial_h, poles))
        decay = [jnp.exp(-jnp.exp(vec(par_h, m))) for m in range(poles)]
        enter = [vec(before, m) for m in range(poles)]
        leave = [vec(after, m) for m in range(poles)]
        wait_all(incoming[2:4])

        def carried(i, carry):
            enter, leave = carry
            for step in range(chunk):
                p = chunk * i + step
                back = extended - 1 - p
                put(conv_h, p, vec(conv_h, p) + flag(p < until) * total_of(enter))
                put(adj_h, back, vec(adj_h, back) + flag(back >= since) * total_of(leave))
                enter = [decay[m] * enter[m] for m in range(poles)]
                leave = [decay[m] * leave[m] for m in range(poles)]
            return enter, leave

        lax.fori_loop(0, (steps + chunk - 1) // chunk, carried, (enter, leave))
        start_all(outgoing)
        wait_all(incoming[4:])
        posted = posted_rows(keep, conv_h, adj_h, up.at[half], key.at[half], val.at[half])

        def tap_terms(i, carry):
            tap_sums, feat_now, feat_one = carry
            p = rows - 1 - i
            now, masked_one, masked_two = posted(p)
            feat_two = [vec(feat_h, third * padded + p) for third in range(3)]
            new_sums = []
            for third in range(3):
                new_sums += [
                    tap_sums[3 * third] + now[third] * feat_now[third],
                    tap_sums[3 * third + 1] + masked_one[third] * feat_one[third],
                    tap_sums[3 * third + 2] + masked_two[third] * feat_two[third],
                ]
            return new_sums, feat_one, feat_two

        feat_last = [vec(feat_h, third * padded + rows + 1) for third in range(3)]
        feat_before = [vec(feat_h, third * padded + rows) for third in range(3)]
        tap_sums, _, _ = lax.fori_loop(
            0, rows, tap_terms, ([zero] * 9, feat_last, feat_before), unroll=4
        )
        for third in range(3):
            for j in range(3):
                put(sums, (3 * j + third) * groups + half, tap_sums[3 * third + j])

    each_group(groups, group)
    width = groups * SUB
    same = 9 * width
    tap_sums = sums[0:same, :].astype(BF16)
    columns = (payload.shape[1] - same) // 16
    for e in range(count):
        payload[e, 0:same, :] = tap_sums
        first_row = same + (e * width) // count
        for j in range(columns):
            value = sums[pl.ds(first_row + j, 16, stride=width), :]
            payload[e, same + 16 * j : same + 16 * (j + 1), :] = value.astype(BF16)
        last_row = first_row + poles * width
        payload[e, same + 16 * columns :, :] = sums[last_row : last_row + SUB, :].astype(BF16)
    each_group(
        groups,
        lambda half: wait_all(group_copies([conv, adj], [conv_out, adj_out], out_sems, half)),
    )


def grads_kernel(
    rows, groups, far_lengths, tap_in, conv_in, adj_in, up_in, key_in, val_in, grads,
    lengths, tap, conv, adj, up, key, val, post, ready, keep, length_sem, in_sems, out_sems,
):
    extended = rows + HALO
    get_lengths = pltpu.make_async_copy(far_lengths, lengths, length_sem)
    get_lengths.start()
    far = [tap_in, conv_in, adj_in, up_in, key_in, val_in]
    near = [tap, conv, adj, up, key, val]
    each_group(groups, lambda half: start_all(group_copies(far, near, in_sems, half)))

    def leaving(half):
        return [
            pltpu.make_async_copy(
                ready.at[half, third],
                grads.at[
                    0, :, pl.ds(pl.multiple_of((third * groups + half) * GROUP, GROUP), GROUP)
                ],
                out_sems.at[half, third],
            )
            for third in range(3)
        ]

    get_lengths.wait()
    fill_keep(keep, segment_starts(lengths), lax.axis_index("ctx") * rows, rows)

    def group(half):
        wait_all(group_copies(far, near, in_sems, half))
        taps_h = [[vec(tap.at[half], third * 3 + j) for j in range(3)] for third in range(3)]
        posted = posted_rows(
            keep, conv.at[half], adj.at[half], up.at[half], key.at[half], val.at[half]
        )
        _, _, far_two = posted(extended - 1)
        _, near_one, near_two = posted(extended - 2)

        def transposed(i, carry):
            one, two, three = carry
            p = rows - 1 - i
            now, masked_one, masked_two = posted(p)
            for third in range(3):
                back = (
                    taps_h[third][0] * now[third]
                    + taps_h[third][1] * one[third]
                    + taps_h[third][2] * three[third]
                )
                put(post, third * rows + p, back)
            return masked_one, masked_two, two

        lax.fori_loop(0, rows, transposed, (near_one, near_two, far_two), unroll=4)

        def write(i, carry):
            for third in range(3):
                for j in range(SUB):
                    value = post[pl.ds((third * rows + i * 16) * SUB + j, 16, stride=SUB), :]
                    lanes = slice(j * LANES, (j + 1) * LANES)
                    ready[half, third, pl.ds(pl.multiple_of(i * 16, 16), 16), lanes] = value.astype(
                        BF16
                    )
            return carry

        lax.fori_loop(0, rows // 16, write, 0, unroll=2)
        start_all(leaving(half))

    each_group(groups, group)
    each_group(groups, lambda half: wait_all(leaving(half)))


def share_kernel(parts, out):
    mine = parts[0].astype(F32)
    for k in range(1, parts.shape[0]):
        mine = mine + parts[k].astype(F32)
    out[...] = mine.astype(BF16)


def emit_kernel(groups, scale, shares, grad_taps, resid, skip, whole):
    me = lax.axis_index("ctx")
    width = groups * SUB
    poles, per_shard = resid.shape
    mine = shares[0].astype(F32)
    for k in range(1, shares.shape[0]):
        mine = mine + shares[k].astype(F32)
    whole[...] = mine * scale
    for k in range(3 * width):
        grad_taps[:, k * LANES : (k + 1) * LANES] = whole[pl.ds(k, 3, stride=3 * width), :]
    first = 9 * width
    columns = (whole.shape[0] - first) // 16
    last = first + 16 * columns
    if per_shard >= LANES:
        for j in range(columns):
            lanes = slice(j * LANES, (j + 1) * LANES)
            resid[:, lanes] = whole[first + 16 * j : first + 16 * (j + 1), :]
            skip[:, lanes] = whole[last + j : last + j + 1, :]
    else:
        per = LANES // per_shard
        rows = whole[first : first + 16, :]
        final = whole[last : last + 1, :]
        place = lax.rem(me, per)
        chosen, chosen_last = rows[:, :per_shard], final[:, :per_shard]
        for i in range(1, per):
            lanes = slice(i * per_shard, (i + 1) * per_shard)
            chosen = jnp.where(place == i, rows[:, lanes], chosen)
            chosen_last = jnp.where(place == i, final[:, lanes], chosen_last)
        resid[...] = chosen
        skip[...] = chosen_last


def swap(block, axes):
    return lax.all_to_all(block, axes, split_axis=0, concat_axis=0, tiled=True)


def per_device(features, upstream, lengths, conv_taps, residues, log_rate, skip_gain):
    rows = features.shape[1]
    channels = upstream.shape[2]
    poles = residues.shape[0]
    ctx_count = lax.axis_size("ctx")
    total = ctx_count * lax.axis_size("dp")
    per_shard = channels // ctx_count
    groups = channels // GROUP
    grad_scale = 1.0 / math.sqrt(rows * total)
    extended = rows + HALO
    padded = rows + 2 * HALO
    state_rows = poles * SUB
    limits = pltpu.CompilerParams(vmem_limit_bytes=40 * 1024 * 1024)
    hbm = pl.BlockSpec(memory_space=pltpu.HBM)
    vmem = pl.BlockSpec(memory_space=pltpu.VMEM)

    def tall(height):
        return jax.ShapeDtypeStruct((groups, height * SUB, LANES), F32)

    def near(*heights):
        return [pltpu.VMEM((groups, height * SUB, LANES), F32) for height in heights]

    def scratch(height):
        return pltpu.VMEM((height * SUB, LANES), F32)

    def sems(*shape):
        return pltpu.SemaphoreType.DMA(shape)

    keep = pltpu.SMEM((rows + 8,), F32)
    small = pltpu.SMEM(lengths.shape, jnp.int32)

    def call(kernel, name, ins, in_specs, outs, out_specs, scratch_shapes=(), cost=None):
        ins = [
            pltpu.with_memory_space_constraint(x, pltpu.HBM) if spec is hbm else x
            for x, spec in zip(ins, in_specs)
        ]
        if isinstance(outs, list):
            outs = [
                pltpu.HBM(out.shape, out.dtype) if spec is hbm else out
                for out, spec in zip(outs, out_specs)
            ]
        return pl.pallas_call(
            kernel,
            out_shape=outs,
            in_specs=in_specs,
            out_specs=out_specs,
            scratch_shapes=list(scratch_shapes),
            compiler_params=limits,
            cost_estimate=cost,
            name=name,
        )(*ins)

    block_rows = (3 * poles + 2) * tiles_of(per_shard)
    block = (-(-block_rows // SUB) * SUB, min(per_shard, LANES))
    span = features.shape[2]
    params, edge, head = call(
        start_kernel,
        "start",
        [log_rate, residues, skip_gain[None], features, upstream],
        [hbm] * 5,
        [
            jax.ShapeDtypeStruct((ctx_count,) + block, BF16),
            jax.ShapeDtypeStruct((HALO, span), BF16),
            jax.ShapeDtypeStruct((HALO, span + channels), BF16),
        ],
        [vmem] * 3,
        [
            pltpu.VMEM((poles, per_shard), F32),
            pltpu.VMEM((poles, per_shard), F32),
            pltpu.VMEM((1, per_shard), F32),
            pltpu.VMEM((16, span), BF16),
            pltpu.VMEM((16, span), BF16),
            pltpu.VMEM((16, channels), BF16),
            pltpu.VMEM(block, F32),
            sems(6),
        ],
    )
    params = swap(params, "ctx")
    left = shifted(edge, "ctx", 1)
    right = shifted(head, "ctx", -1)

    near_mixed, near_gout, feat, up, mixed, gout, tap, key, val = call(
        functools.partial(features_kernel, rows, groups),
        "features",
        [lengths, features, upstream, left, right, conv_taps],
        [hbm] * 3 + [vmem] * 3,
        [tall(extended)] * 2
        + [tall(3 * padded)]
        + [tall(extended)] * 3
        + [tall(9)]
        + [tall(extended)] * 2,
        [vmem] * 2 + [hbm] * 7,
        [
            small,
            pltpu.VMEM((groups, 3, rows, GROUP), BF16),
            pltpu.VMEM((groups, rows, GROUP), BF16),
        ]
        + near(3 * padded, extended, 9, extended, extended)
        + [keep, sems(), sems(groups, 4), sems(groups, 7)],
        pl.CostEstimate(flops=5 * 10**9, bytes_accessed=4 * 10**7, transcendentals=0),
    )
    state_rows = poles * SUB
    payload, par = call(
        functools.partial(ends_kernel, rows, groups),
        "ends",
        [lengths, params, near_mixed, near_gout],
        [hbm] + [vmem] * 3,
        [
            jax.ShapeDtypeStruct((ctx_count, groups, state_rows, LANES), BF16),
            tall(2 * poles + 1),
        ],
        [vmem, hbm],
        [small]
        + near(2 * poles + 1)
        + [pltpu.VMEM((2, state_rows, LANES), BF16)]
        + [pltpu.VMEM((block[0], LANES), F32), scratch(1)]
        + [sems(), sems(groups, 1)],
    )
    arrived = swap(payload, "ctx")
    conv, adj, partial = call(
        functools.partial(local_kernel, rows, groups),
        "local",
        [lengths, mixed, gout, par],
        [hbm] * 4,
        [tall(extended)] * 2 + [tall(poles + 1)],
        [hbm] * 3,
        [small]
        + near(extended, extended, 2 * poles + 1, extended, extended, poles + 1)
        + [scratch(1), keep, sems(), sems(groups, 3), sems(groups, 3)],
    )
    used = (10 + poles) * groups * SUB
    sum_rows = 9 * groups * SUB + 16 * tiles_of(per_shard) + SUB
    conv, adj, sums = call(
        functools.partial(sums_kernel, rows, groups),
        "sums",
        [lengths, arrived, par, partial, conv, adj, up, key, val, feat],
        [hbm, vmem] + [hbm] * 8,
        [tall(extended)] * 2 + [jax.ShapeDtypeStruct((ctx_count, sum_rows, LANES), BF16)],
        [hbm, hbm, vmem],
        [small]
        + near(2 * poles + 1, poles + 1, extended, extended, extended, extended, extended)
        + near(3 * padded)
        + [scratch(poles), scratch(poles)]
        + [pltpu.VMEM((used + 16, LANES), F32), scratch(1), keep]
        + [sems(), sems(groups, 8), sems(groups, 2)],
    )
    parts = swap(sums, "ctx")
    (grads,) = call(
        functools.partial(grads_kernel, rows, groups),
        "grads",
        [lengths, tap, conv, adj, up, key, val],
        [hbm] * 7,
        [jax.ShapeDtypeStruct(features.shape, BF16)],
        [hbm],
        [small]
        + near(9, extended, extended, extended, extended, extended)
        + [scratch(3 * rows), pltpu.VMEM((groups, 3, rows, GROUP), BF16), keep]
        + [sems(), sems(groups, 6), sems(groups, 3)],
    )
    mine = call(
        share_kernel,
        "share",
        [parts],
        [vmem],
        jax.ShapeDtypeStruct((sum_rows, LANES), BF16),
        vmem,
    )
    grad_taps, resid, skip = call(
        functools.partial(emit_kernel, groups, grad_scale),
        "emit",
        [lax.all_gather(mine, "dp")],
        [vmem],
        [
            jax.ShapeDtypeStruct((3, 3 * channels), F32),
            jax.ShapeDtypeStruct((poles, per_shard), F32),
            jax.ShapeDtypeStruct((1, per_shard), F32),
        ],
        [vmem] * 3,
        [pltpu.VMEM((sum_rows, LANES), F32)],
    )
    return grads, grad_taps, resid, skip.reshape(per_shard)


def solution(mesh):
    return jax.shard_map(
        per_device,
        mesh=mesh,
        in_specs=(
            P("dp", "ctx", None),
            P("dp", "ctx", None),
            P("dp", None),
            P(),
            P(None, "ctx"),
            P(None, "ctx"),
            P("ctx"),
        ),
        out_specs=(P("dp", "ctx", None), P(), P(None, "ctx"), P("ctx")),
        check_vma=False,
    )
```

```python
import functools
import math

import jax
import jax.numpy as jnp
from jax import lax
from jax.experimental import pallas as pl
from jax.experimental.pallas import tpu as pltpu
from jax.sharding import PartitionSpec as P

F32 = jnp.float32
BF16 = jnp.bfloat16
LANES = 128
SUB = 8
GROUP = SUB * LANES
HALO = 2


def shifted(block, axis, distance):
    count = lax.axis_size(axis)
    route = [(i - distance, i) for i in range(count) if 0 <= i - distance < count]
    return lax.ppermute(block, axis, route)


def vec(ref, index):
    return ref[pl.ds(pl.multiple_of(index * SUB, SUB), SUB), :]


def put(ref, index, value):
    ref[pl.ds(pl.multiple_of(index * SUB, SUB), SUB), :] = value


def spread(dst, first, src, column, row_count):
    for j in range(SUB):
        lanes = pl.ds(pl.multiple_of(column + j * LANES, LANES), LANES)
        dst[pl.ds(first * SUB + j, row_count, stride=SUB), :] = src[:, lanes].astype(F32)


def spread_rows(dst, first, src, row_count):
    def step(i, carry):
        for j in range(SUB):
            value = src[pl.ds(pl.multiple_of(i * 16, 16), 16), j * LANES : (j + 1) * LANES]
            dst[pl.ds((i * 16 + first) * SUB + j, 16, stride=SUB), :] = value.astype(F32)
        return carry

    lax.fori_loop(0, row_count // 16, step, 0)


def tiles_of(width):
    return max(1, width // LANES)


def start_kernel(
    log_rate, residues, skip_gain, features, upstream, out, edge, head,
    rates, coeffs, gains, low, high, high_up, slab, sems,
):
    rows = features.shape[1]
    copies = [
        pltpu.make_async_copy(source, target, sems.at[i])
        for i, (source, target) in enumerate(
            [
                (log_rate, rates),
                (residues, coeffs),
                (skip_gain, gains),
                (features.at[0, pl.ds(0, 16), :], low),
                (features.at[0, pl.ds(rows - 16, 16), :], high),
                (upstream.at[0, pl.ds(0, 16), :], high_up),
            ]
        )
    ]
    start_all(copies)
    poles, width = rates.shape
    per = tiles_of(width)
    slab[...] = jnp.zeros(slab.shape, F32)
    wait_all(copies[:3])
    for j in range(per):
        lanes = slice(j * LANES, min(width, (j + 1) * LANES))
        rate, gain = rates[:, lanes], gains[:, lanes]
        slab[pl.ds(j, poles, stride=per), :] = rounded(rate)
        slab[pl.ds(poles * per + j, poles, stride=per), :] = rate - rounded(rate)
        slab[pl.ds(2 * poles * per + j, poles, stride=per), :] = coeffs[:, lanes]
        slab[pl.ds(3 * poles * per + j, 1), :] = rounded(gain)
        slab[pl.ds((3 * poles + 1) * per + j, 1), :] = gain - rounded(gain)
    packed = slab[...].astype(BF16)
    for e in range(out.shape[0]):
        out[e] = packed
    wait_all(copies[3:])
    span = features.shape[2]
    for at in range(0, span, GROUP):
        lanes = slice(at, at + GROUP)
        head[:, lanes] = low[:, lanes].astype(F32)[:HALO].astype(BF16)
        edge[:, lanes] = high[:, lanes].astype(F32)[16 - HALO :].astype(BF16)
    for at in range(0, upstream.shape[2], GROUP):
        lanes = slice(at, at + GROUP)
        head[:, span + at : span + at + GROUP] = high_up[:, lanes].astype(F32)[:HALO].astype(BF16)


def spread_params(dst, par, slab, half, groups, poles):
    pieces, height, width = par.shape
    many = pieces // groups
    base = half * many
    joined = LANES // width
    per = height // (3 * poles)
    for k in range(many // joined):
        parts = [par[base + k * joined + i].astype(F32) for i in range(joined)]
        slab[...] = parts[0] if joined == 1 else jnp.concatenate(parts, axis=1)
        for j in range(per):
            to = k * per + j

            def rows_of(piece, count=poles):
                return slab[pl.ds(piece * per + j, count, stride=per), :]

            dst[pl.ds(to, poles, stride=SUB), :] = rows_of(0) + rows_of(poles)
            dst[pl.ds(poles * SUB + to, poles, stride=SUB), :] = rows_of(2 * poles)
            gain = rows_of(3 * poles, 1) + rows_of(3 * poles + 1, 1)
            dst[pl.ds(2 * poles * SUB + to, 1), :] = gain


def segment_starts(lengths):
    starts = [jnp.int32(0)]
    for j in range(lengths.shape[1]):
        starts.append(starts[-1] + lengths[0, j])
    return starts


def fill_keep(keep, starts, base, rows):
    count = rows + HALO + 2

    def step(i, carry):
        keep[i] = jnp.float32(1.0)
        return carry

    lax.fori_loop(0, count, step, 0, unroll=4)
    for start in starts:
        at = start - base + 1

        @pl.when((at >= 0) & (at < count))
        def _():
            keep[at] = jnp.float32(0.0)


def rounded(value):
    return value.astype(BF16).astype(F32)


def flag(condition):
    return jnp.where(condition, 1.0, 0.0).astype(F32)


def total_of(terms):
    terms = list(terms)
    while len(terms) > 1:
        odd = terms[-1:] if len(terms) % 2 else []
        terms = [x + y for x, y in zip(terms[::2], terms[1::2])] + odd
    return terms[0]


def unroll_of(trips):
    return max(d for d in range(1, 14) if trips % d == 0)


def featured(feat, tap, p, keep_one, keep_two):
    return (
        tap[0] * vec(feat, p + 2)
        + tap[1] * (keep_one * vec(feat, p + 1))
        + tap[2] * (keep_two * vec(feat, p))
    )


def each_group(groups, body):
    def step(half, carry):
        body(half)
        return carry

    lax.fori_loop(0, groups, step, 0)


def group_copies(sources, targets, sems, half):
    return [
        pltpu.make_async_copy(source.at[half], target.at[half], sems.at[half, i])
        for i, (source, target) in enumerate(zip(sources, targets))
    ]


def start_all(copies):
    for copy in copies:
        copy.start()


def wait_all(copies):
    for copy in copies:
        copy.wait()


def features_kernel(
    rows, groups, far_lengths, features, upstream, left, right, taps,
    last_mixed, first_gout, feat_out, up_out, mixed_out, gout_out, tap_out, key_out, val_out,
    lengths, raw, raw_up, feat, up, mixed, gout, tap, key_scr, val_scr, keep,
    length_sem, in_sems, out_sems,
):
    extended = rows + HALO
    padded = rows + 2 * HALO
    get_lengths = pltpu.make_async_copy(far_lengths, lengths, length_sem)
    get_lengths.start()

    def arriving(half):
        lanes = [
            pl.ds(pl.multiple_of((third * groups + half) * GROUP, GROUP), GROUP)
            for third in range(3)
        ]
        return [
            pltpu.make_async_copy(
                features.at[0, :, lanes[third]], raw.at[half, third], in_sems.at[half, third]
            )
            for third in range(3)
        ] + [pltpu.make_async_copy(upstream.at[0, :, lanes[0]], raw_up.at[half], in_sems.at[half, 3])]

    near = [feat, up, tap, mixed, gout, key_scr, val_scr]
    far = [feat_out, up_out, tap_out, mixed_out, gout_out, key_out, val_out]

    each_group(groups, lambda half: start_all(arriving(half)))

    def prepare(half):
        for third in range(3):
            column = (third * groups + half) * GROUP
            spread(feat.at[half], third * padded, left, column, HALO)
            spread(feat.at[half], third * padded + rows + HALO, right, column, HALO)
            spread(tap.at[half], third * 3, taps, column, 3)
        spread(up.at[half], rows, right, (3 * groups + half) * GROUP, HALO)

    each_group(groups, prepare)
    get_lengths.wait()
    base = lax.axis_index("ctx") * rows
    starts = segment_starts(lengths)
    fill_keep(keep, starts, base, rows)
    low, high = jnp.int32(0), jnp.int32(extended)
    for start in starts:
        at = start - base
        low = jnp.where(at < rows, jnp.maximum(low, at), low)
        high = jnp.where(at > HALO, jnp.minimum(high, at), high)

    def group(half):
        incoming = arriving(half)
        outgoing = group_copies(near, far, out_sems, half)
        feat_h, up_h, mixed_h, gout_h = feat.at[half], up.at[half], mixed.at[half], gout.at[half]
        for third in range(3):
            incoming[third].wait()
            spread_rows(feat_h, third * padded + HALO, raw.at[half, third], rows)
        incoming[3].wait()
        spread_rows(up_h, 0, raw_up.at[half], rows)
        start_all(outgoing[:3])
        taps_h = [[vec(tap.at[half], third * 3 + j) for j in range(3)] for third in range(3)]

        def product(p, carry):
            keep_one = keep[p + 1]
            keep_two = keep_one * keep[p]
            query, key, val = (
                featured(feat_h, taps_h[third], third * padded + p, keep_one, keep_two)
                for third in range(3)
            )
            x = rounded(key * val)
            g = rounded(vec(up_h, p) * query)
            put(mixed_h, p, x)
            put(gout_h, p, g)
            put(last_mixed.at[half], p, x * flag(p >= low))
            put(first_gout.at[half], p, g * flag(p < high))
            put(key_scr.at[half], p, key)
            put(val_scr.at[half], p, val)
            return carry

        lax.fori_loop(0, extended, product, 0, unroll=unroll_of(extended))
        start_all(outgoing[3:])

    each_group(groups, group)
    each_group(groups, lambda half: wait_all(group_copies(near, far, out_sems, half)))


def ends_kernel(
    rows, groups, params, mixed, gout, payload, par_out, par, stack, slab, zero_scr, out_sems
):
    me = lax.axis_index("ctx")
    count = payload.shape[0]
    poles = (par.shape[1] // SUB - 1) // 2
    extended = rows + HALO
    zero_scr[...] = jnp.zeros((SUB, LANES), F32)
    zeros = [zero_scr[...]] * poles

    def prepare(half):
        spread_params(par.at[half], params, slab, half, groups, poles)
        start_all(group_copies([par], [par_out], out_sems, half))

    each_group(groups, prepare)

    def group(half):
        mixed_h, gout_h = mixed.at[half], gout.at[half]
        decay = [jnp.exp(-jnp.exp(vec(par.at[half], m))) for m in range(poles)]

        def sweep(i, carry):
            state, adjoint = carry
            back = extended - 1 - i
            x = vec(mixed_h, i)
            g = vec(gout_h, back)
            state = [decay[m] * state[m] + x for m in range(poles)]
            adjoint = [decay[m] * adjoint[m] + g for m in range(poles)]
            return state, adjoint

        state, adjoint = lax.fori_loop(0, rows, sweep, (zeros, zeros), unroll=8)
        for m in range(0, poles, 2):
            at = slice(m * SUB, (m + 2) * SUB)
            stack[0, at, :] = jnp.concatenate(state[m : m + 2], axis=0).astype(BF16)
            stack[1, at, :] = jnp.concatenate(adjoint[m : m + 2], axis=0).astype(BF16)
        for e in range(count):
            payload[e, half] = stack[jnp.where(e >= me, 0, 1)]

    each_group(groups, group)
    each_group(groups, lambda half: wait_all(group_copies([par], [par_out], out_sems, half)))


def local_kernel(
    rows, groups, far_lengths, mixed_in, gout_in, par_in, conv_out, adj_out, partial_out,
    lengths, mixed, gout, par, conv, adj, partial, zero_scr, keep,
    length_sem, in_sems, out_sems,
):
    poles = (par.shape[1] // SUB - 1) // 2
    extended = rows + HALO
    get_lengths = pltpu.make_async_copy(far_lengths, lengths, length_sem)
    get_lengths.start()
    far_in, near_in = [par_in, mixed_in, gout_in], [par, mixed, gout]
    near_out, far_out = [conv, adj, partial], [conv_out, adj_out, partial_out]
    each_group(groups, lambda half: start_all(group_copies(far_in, near_in, in_sems, half)))
    zero_scr[...] = jnp.zeros((SUB, LANES), F32)
    zero = zero_scr[...]
    per_pass = poles // 4
    zeros = [zero] * per_pass
    get_lengths.wait()
    fill_keep(keep, segment_starts(lengths), lax.axis_index("ctx") * rows, rows)

    def group(half):
        incoming = group_copies(far_in, near_in, in_sems, half)
        outgoing = group_copies(near_out, far_out, out_sems, half)
        mixed_h, gout_h, par_h = mixed.at[half], gout.at[half], par.at[half]
        conv_h, adj_h = conv.at[half], adj.at[half]
        wait_all(incoming)
        gain = vec(par_h, 2 * poles)
        for part in range(poles // per_pass):
            chosen = list(range(part * per_pass, (part + 1) * per_pass))
            decay = [jnp.exp(-jnp.exp(vec(par_h, m))) for m in chosen]
            coeff = [vec(par_h, poles + m) for m in chosen]

            def sweep(i, carry, inside=True):
                state, adjoint, resid, skip = carry
                back = extended - 1 - i
                x = vec(mixed_h, i)
                g = vec(gout_h, back)
                keep_fwd = keep[i + 1]
                keep_bwd = keep[back + 2]
                state = [decay[m] * (state[m] * keep_fwd) + x for m in range(per_pass)]
                adjoint = [decay[m] * (adjoint[m] * keep_bwd) + g for m in range(per_pass)]
                forward = total_of(coeff[m] * state[m] for m in range(per_pass))
                backward = total_of(coeff[m] * adjoint[m] for m in range(per_pass))
                if inside:
                    own = vec(mixed_h, back)
                    resid = [resid[m] + own * adjoint[m] for m in range(per_pass)]
                if part == 0:
                    put(conv_h, i, forward + gain * x)
                    put(adj_h, back, backward + gain * g)
                    if inside:
                        skip = skip + own * g
                else:
                    put(conv_h, i, forward + vec(conv_h, i))
                    put(adj_h, back, backward + vec(adj_h, back))
                return state, adjoint, resid, skip

            carry = (zeros, zeros, zeros, zero)
            for i in range(HALO):
                carry = sweep(i, carry, inside=False)
            _, _, resid, skip = lax.fori_loop(HALO, extended, sweep, carry, unroll=32)
            for i, m in enumerate(chosen):
                put(partial.at[half], m, resid[i])
            if part == 0:
                put(partial.at[half], poles, skip)
        start_all(outgoing)

    each_group(groups, group)
    each_group(groups, lambda half: wait_all(group_copies(near_out, far_out, out_sems, half)))


def posted_rows(keep, conv, adj, up, key, val):
    def posted(p):
        keep_one = keep[p + 1]
        keep_two = keep_one * keep[p]
        conv_out = rounded(vec(conv, p))
        grad_mixed = rounded(vec(adj, p))
        now = [vec(up, p) * conv_out, grad_mixed * vec(val, p), grad_mixed * vec(key, p)]
        return now, [keep_one * g for g in now], [keep_two * g for g in now]

    return posted


def sums_kernel(
    rows, groups, far_lengths, arrived, par_in, partial_in, conv_in, adj_in, up_in, key_in, val_in,
    feat_in, conv_out, adj_out, payload,
    lengths, par, partial, conv, adj, up, key, val, feat, before, after, sums, zero_scr, keep,
    length_sem, in_sems, out_sems,
):
    me = lax.axis_index("ctx")
    base = me * rows
    count = arrived.shape[0]
    poles = (par.shape[1] // SUB - 1) // 2
    extended = rows + HALO
    padded = rows + 2 * HALO
    get_lengths = pltpu.make_async_copy(far_lengths, lengths, length_sem)
    get_lengths.start()
    far = [par_in, partial_in, conv_in, adj_in, up_in, key_in, val_in, feat_in]
    near = [par, partial, conv, adj, up, key, val, feat]
    each_group(groups, lambda half: start_all(group_copies(far, near, in_sems, half)))
    zero_scr[...] = jnp.zeros((SUB, LANES), F32)
    zero = zero_scr[...]
    get_lengths.wait()
    starts = segment_starts(lengths)
    fill_keep(keep, starts, base, rows)
    until, since = jnp.int32(extended), jnp.int32(0)
    first, last, newest = jnp.int32(0), jnp.int32(2**30), jnp.int32(0)
    for start in starts:
        at = start - base
        until = jnp.where(at >= 0, jnp.minimum(until, at), until)
        since = jnp.where(at <= extended, jnp.maximum(since, at), since)
        first = jnp.where(at <= 0, jnp.maximum(first, start), first)
        last = jnp.where(at > extended, jnp.minimum(last, start), last)
        newest = jnp.where(at <= extended, jnp.maximum(newest, start), newest)
    steps = jnp.maximum(until, extended - since)
    through = flag(newest < base + rows)
    chunk = unroll_of(extended)

    def group(half):
        incoming = group_copies(far, near, in_sems, half)
        outgoing = group_copies([conv, adj], [conv_out, adj_out], out_sems, half)
        par_h, partial_h, conv_h, adj_h = par.at[half], partial.at[half], conv.at[half], adj.at[half]
        feat_h = feat.at[half]
        wait_all(incoming[:2])
        per_pass = poles // 2
        zeros = [zero] * per_pass
        for part in range(2):
            chosen = list(range(part * per_pass, (part + 1) * per_pass))
            rate = [jnp.exp(vec(par_h, m)) for m in chosen]
            block = [jnp.exp(-rows * r) for r in rate]

            def arrived_states(d):
                got = []
                for m in range(chosen[0], chosen[-1] + 1, 2):
                    pair = arrived[d, half, m * SUB : (m + 2) * SUB, :].astype(F32)
                    got += [pair[:SUB], pair[SUB:]]
                return got

            def from_before(d, carry):
                joined = flag((d + 1) * rows - 1 >= first)
                got = arrived_states(d)
                return [block[i] * carry[i] + joined * got[i] for i in range(per_pass)]

            def from_after(i, carry):
                d = count - 1 - i
                joined = flag(d * rows + HALO < last)
                got = arrived_states(d)
                return [block[i] * carry[i] + joined * got[i] for i in range(per_pass)]

            state = lax.fori_loop(0, me, from_before, zeros)
            adjoint = lax.fori_loop(0, count - 1 - me, from_after, zeros)
            own = arrived_states(me)
            for i, m in enumerate(chosen):
                scale = vec(par_h, poles + m) * jnp.exp(-rate[i])
                put(before, m, scale * state[i])
                put(after, m, scale * adjoint[i])
                cross = jnp.exp(-(HALO + 1) * rate[i]) * (adjoint[i] * through)
                put(sums, (9 + m) * groups + half, vec(partial_h, m) + cross * own[i])
        put(sums, (9 + poles) * groups + half, vec(partial_h, poles))
        decay = [jnp.exp(-jnp.exp(vec(par_h, m))) for m in range(poles)]
        enter = [vec(before, m) for m in range(poles)]
        leave = [vec(after, m) for m in range(poles)]
        wait_all(incoming[2:4])

        def carried(i, carry):
            enter, leave = carry
            for step in range(chunk):
                p = chunk * i + step
                back = extended - 1 - p
                put(conv_h, p, vec(conv_h, p) + flag(p < until) * total_of(enter))
                put(adj_h, back, vec(adj_h, back) + flag(back >= since) * total_of(leave))
                enter = [decay[m] * enter[m] for m in range(poles)]
                leave = [decay[m] * leave[m] for m in range(poles)]
            return enter, leave

        lax.fori_loop(0, (steps + chunk - 1) // chunk, carried, (enter, leave))
        start_all(outgoing)
        wait_all(incoming[4:])
        posted = posted_rows(keep, conv_h, adj_h, up.at[half], key.at[half], val.at[half])

        def tap_terms(i, carry):
            tap_sums, feat_now, feat_one = carry
            p = rows - 1 - i
            now, masked_one, masked_two = posted(p)
            feat_two = [vec(feat_h, third * padded + p) for third in range(3)]
            new_sums = []
            for third in range(3):
                new_sums += [
                    tap_sums[3 * third] + now[third] * feat_now[third],
                    tap_sums[3 * third + 1] + masked_one[third] * feat_one[third],
                    tap_sums[3 * third + 2] + masked_two[third] * feat_two[third],
                ]
            return new_sums, feat_one, feat_two

        feat_last = [vec(feat_h, third * padded + rows + 1) for third in range(3)]
        feat_before = [vec(feat_h, third * padded + rows) for third in range(3)]
        tap_sums, _, _ = lax.fori_loop(
            0, rows, tap_terms, ([zero] * 9, feat_last, feat_before), unroll=4
        )
        for third in range(3):
            for j in range(3):
                put(sums, (3 * j + third) * groups + half, tap_sums[3 * third + j])

    each_group(groups, group)
    width = groups * SUB
    same = 9 * width
    tap_sums = sums[0:same, :].astype(BF16)
    columns = (payload.shape[1] - same) // 16
    for e in range(count):
        payload[e, 0:same, :] = tap_sums
        first_row = same + (e * width) // count
        for j in range(columns):
            value = sums[pl.ds(first_row + j, 16, stride=width), :]
            payload[e, same + 16 * j : same + 16 * (j + 1), :] = value.astype(BF16)
        last_row = first_row + poles * width
        payload[e, same + 16 * columns :, :] = sums[last_row : last_row + SUB, :].astype(BF16)
    each_group(
        groups,
        lambda half: wait_all(group_copies([conv, adj], [conv_out, adj_out], out_sems, half)),
    )


def grads_kernel(
    rows, groups, far_lengths, tap_in, conv_in, adj_in, up_in, key_in, val_in, grads,
    lengths, tap, conv, adj, up, key, val, post, ready, keep, length_sem, in_sems, out_sems,
):
    extended = rows + HALO
    get_lengths = pltpu.make_async_copy(far_lengths, lengths, length_sem)
    get_lengths.start()
    far = [tap_in, conv_in, adj_in, up_in, key_in, val_in]
    near = [tap, conv, adj, up, key, val]
    each_group(groups, lambda half: start_all(group_copies(far, near, in_sems, half)))

    def leaving(half):
        return [
            pltpu.make_async_copy(
                ready.at[half, third],
                grads.at[
                    0, :, pl.ds(pl.multiple_of((third * groups + half) * GROUP, GROUP), GROUP)
                ],
                out_sems.at[half, third],
            )
            for third in range(3)
        ]

    get_lengths.wait()
    fill_keep(keep, segment_starts(lengths), lax.axis_index("ctx") * rows, rows)

    def group(half):
        wait_all(group_copies(far, near, in_sems, half))
        taps_h = [[vec(tap.at[half], third * 3 + j) for j in range(3)] for third in range(3)]
        posted = posted_rows(
            keep, conv.at[half], adj.at[half], up.at[half], key.at[half], val.at[half]
        )
        _, _, far_two = posted(extended - 1)
        _, near_one, near_two = posted(extended - 2)

        def transposed(i, carry):
            one, two, three = carry
            p = rows - 1 - i
            now, masked_one, masked_two = posted(p)
            for third in range(3):
                back = (
                    taps_h[third][0] * now[third]
                    + taps_h[third][1] * one[third]
                    + taps_h[third][2] * three[third]
                )
                put(post, third * rows + p, back)
            return masked_one, masked_two, two

        lax.fori_loop(0, rows, transposed, (near_one, near_two, far_two), unroll=4)

        def write(i, carry):
            for third in range(3):
                for j in range(SUB):
                    value = post[pl.ds((third * rows + i * 16) * SUB + j, 16, stride=SUB), :]
                    lanes = slice(j * LANES, (j + 1) * LANES)
                    ready[half, third, pl.ds(pl.multiple_of(i * 16, 16), 16), lanes] = value.astype(
                        BF16
                    )
            return carry

        lax.fori_loop(0, rows // 16, write, 0, unroll=2)
        start_all(leaving(half))

    each_group(groups, group)
    each_group(groups, lambda half: wait_all(leaving(half)))


def share_kernel(parts, out):
    mine = parts[0].astype(F32)
    for k in range(1, parts.shape[0]):
        mine = mine + parts[k].astype(F32)
    out[...] = mine.astype(BF16)


def emit_kernel(groups, scale, shares, grad_taps, resid, skip, whole):
    me = lax.axis_index("ctx")
    width = groups * SUB
    poles, per_shard = resid.shape
    mine = shares[0].astype(F32)
    for k in range(1, shares.shape[0]):
        mine = mine + shares[k].astype(F32)
    whole[...] = mine * scale
    for k in range(3 * width):
        grad_taps[:, k * LANES : (k + 1) * LANES] = whole[pl.ds(k, 3, stride=3 * width), :]
    first = 9 * width
    columns = (whole.shape[0] - first) // 16
    last = first + 16 * columns
    if per_shard >= LANES:
        for j in range(columns):
            lanes = slice(j * LANES, (j + 1) * LANES)
            resid[:, lanes] = whole[first + 16 * j : first + 16 * (j + 1), :]
            skip[:, lanes] = whole[last + j : last + j + 1, :]
    else:
        per = LANES // per_shard
        rows = whole[first : first + 16, :]
        final = whole[last : last + 1, :]
        place = lax.rem(me, per)
        chosen, chosen_last = rows[:, :per_shard], final[:, :per_shard]
        for i in range(1, per):
            lanes = slice(i * per_shard, (i + 1) * per_shard)
            chosen = jnp.where(place == i, rows[:, lanes], chosen)
            chosen_last = jnp.where(place == i, final[:, lanes], chosen_last)
        resid[...] = chosen
        skip[...] = chosen_last


def swap(block, axes):
    return lax.all_to_all(block, axes, split_axis=0, concat_axis=0, tiled=True)


def per_device(features, upstream, lengths, conv_taps, residues, log_rate, skip_gain):
    rows = features.shape[1]
    channels = upstream.shape[2]
    poles = residues.shape[0]
    ctx_count = lax.axis_size("ctx")
    total = ctx_count * lax.axis_size("dp")
    per_shard = channels // ctx_count
    groups = channels // GROUP
    grad_scale = 1.0 / math.sqrt(rows * total)
    extended = rows + HALO
    padded = rows + 2 * HALO
    state_rows = poles * SUB
    limits = pltpu.CompilerParams(vmem_limit_bytes=40 * 1024 * 1024)
    hbm = pl.BlockSpec(memory_space=pltpu.HBM)
    vmem = pl.BlockSpec(memory_space=pltpu.VMEM)

    def tall(height):
        return jax.ShapeDtypeStruct((groups, height * SUB, LANES), F32)

    def near(*heights):
        return [pltpu.VMEM((groups, height * SUB, LANES), F32) for height in heights]

    def scratch(height):
        return pltpu.VMEM((height * SUB, LANES), F32)

    def sems(*shape):
        return pltpu.SemaphoreType.DMA(shape)

    keep = pltpu.SMEM((rows + 8,), F32)
    small = pltpu.SMEM(lengths.shape, jnp.int32)

    def call(kernel, name, ins, in_specs, outs, out_specs, scratch_shapes=(), cost=None):
        ins = [
            pltpu.with_memory_space_constraint(x, pltpu.HBM) if spec is hbm else x
            for x, spec in zip(ins, in_specs)
        ]
        if isinstance(outs, list):
            outs = [
                pltpu.HBM(out.shape, out.dtype) if spec is hbm else out
                for out, spec in zip(outs, out_specs)
            ]
        return pl.pallas_call(
            kernel,
            out_shape=outs,
            in_specs=in_specs,
            out_specs=out_specs,
            scratch_shapes=list(scratch_shapes),
            compiler_params=limits,
            cost_estimate=cost,
            name=name,
        )(*ins)

    block_rows = (3 * poles + 2) * tiles_of(per_shard)
    block = (-(-block_rows // SUB) * SUB, min(per_shard, LANES))
    span = features.shape[2]
    params, edge, head = call(
        start_kernel,
        "start",
        [log_rate, residues, skip_gain[None], features, upstream],
        [hbm] * 5,
        [
            jax.ShapeDtypeStruct((ctx_count,) + block, BF16),
            jax.ShapeDtypeStruct((HALO, span), BF16),
            jax.ShapeDtypeStruct((HALO, span + channels), BF16),
        ],
        [vmem] * 3,
        [
            pltpu.VMEM((poles, per_shard), F32),
            pltpu.VMEM((poles, per_shard), F32),
            pltpu.VMEM((1, per_shard), F32),
            pltpu.VMEM((16, span), BF16),
            pltpu.VMEM((16, span), BF16),
            pltpu.VMEM((16, channels), BF16),
            pltpu.VMEM(block, F32),
            sems(6),
        ],
    )
    params = swap(params, "ctx")
    left = shifted(edge, "ctx", 1)
    right = shifted(head, "ctx", -1)

    near_mixed, near_gout, feat, up, mixed, gout, tap, key, val = call(
        functools.partial(features_kernel, rows, groups),
        "features",
        [lengths, features, upstream, left, right, conv_taps],
        [hbm] * 3 + [vmem] * 3,
        [tall(extended)] * 2
        + [tall(3 * padded)]
        + [tall(extended)] * 3
        + [tall(9)]
        + [tall(extended)] * 2,
        [vmem] * 2 + [hbm] * 7,
        [
            small,
            pltpu.VMEM((groups, 3, rows, GROUP), BF16),
            pltpu.VMEM((groups, rows, GROUP), BF16),
        ]
        + near(3 * padded, extended, extended, extended, 9, extended, extended)
        + [keep, sems(), sems(groups, 4), sems(groups, 7)],
        pl.CostEstimate(flops=5 * 10**9, bytes_accessed=4 * 10**7, transcendentals=0),
    )
    state_rows = poles * SUB
    payload, par = call(
        functools.partial(ends_kernel, rows, groups),
        "ends",
        [params, near_mixed, near_gout],
        [vmem] * 3,
        [
            jax.ShapeDtypeStruct((ctx_count, groups, state_rows, LANES), BF16),
            tall(2 * poles + 1),
        ],
        [vmem, hbm],
        near(2 * poles + 1)
        + [pltpu.VMEM((2, state_rows, LANES), BF16)]
        + [pltpu.VMEM((block[0], LANES), F32), scratch(1)]
        + [sems(groups, 1)],
    )
    arrived = swap(payload, "ctx")
    conv, adj, partial = call(
        functools.partial(local_kernel, rows, groups),
        "local",
        [lengths, mixed, gout, par],
        [hbm] * 4,
        [tall(extended)] * 2 + [tall(poles + 1)],
        [hbm] * 3,
        [small]
        + near(extended, extended, 2 * poles + 1, extended, extended, poles + 1)
        + [scratch(1), keep, sems(), sems(groups, 3), sems(groups, 3)],
    )
    used = (10 + poles) * groups * SUB
    sum_rows = 9 * groups * SUB + 16 * tiles_of(per_shard) + SUB
    conv, adj, sums = call(
        functools.partial(sums_kernel, rows, groups),
        "sums",
        [lengths, arrived, par, partial, conv, adj, up, key, val, feat],
        [hbm, vmem] + [hbm] * 8,
        [tall(extended)] * 2 + [jax.ShapeDtypeStruct((ctx_count, sum_rows, LANES), BF16)],
        [hbm, hbm, vmem],
        [small]
        + near(2 * poles + 1, poles + 1, extended, extended, extended, extended, extended)
        + near(3 * padded)
        + [scratch(poles), scratch(poles)]
        + [pltpu.VMEM((used + 16, LANES), F32), scratch(1), keep]
        + [sems(), sems(groups, 8), sems(groups, 2)],
    )
    parts = swap(sums, "ctx")
    (grads,) = call(
        functools.partial(grads_kernel, rows, groups),
        "grads",
        [lengths, tap, conv, adj, up, key, val],
        [hbm] * 7,
        [jax.ShapeDtypeStruct(features.shape, BF16)],
        [hbm],
        [small]
        + near(9, extended, extended, extended, extended, extended)
        + [scratch(3 * rows), pltpu.VMEM((groups, 3, rows, GROUP), BF16), keep]
        + [sems(), sems(groups, 6), sems(groups, 3)],
    )
    mine = call(
        share_kernel,
        "share",
        [parts],
        [vmem],
        jax.ShapeDtypeStruct((sum_rows, LANES), BF16),
        vmem,
    )
    grad_taps, resid, skip = call(
        functools.partial(emit_kernel, groups, grad_scale),
        "emit",
        [lax.all_gather(mine, "dp")],
        [vmem],
        [
            jax.ShapeDtypeStruct((3, 3 * channels), F32),
            jax.ShapeDtypeStruct((poles, per_shard), F32),
            jax.ShapeDtypeStruct((1, per_shard), F32),
        ],
        [vmem] * 3,
        [pltpu.VMEM((sum_rows, LANES), F32)],
    )
    return grads, grad_taps, resid, skip.reshape(per_shard)


def solution(mesh):
    return jax.shard_map(
        per_device,
        mesh=mesh,
        in_specs=(
            P("dp", "ctx", None),
            P("dp", "ctx", None),
            P("dp", None),
            P(),
            P(None, "ctx"),
            P(None, "ctx"),
            P("ctx"),
        ),
        out_specs=(P("dp", "ctx", None), P(), P(None, "ctx"), P("ctx")),
        check_vma=False,
    )
```
